32 devices in a mesh: rep: 2 (over y), fsdp: 16 (over z, x, core).
Axes of the slice: x: 2, y: 2, z: 4, core: 2. Of those that a mesh axis runs over, the one named last changes fastest.
Arguments:
- tokens: bfloat16 [37632, 768], P(('rep', 'fsdp')), may hold values from -6 to 6
- mask_flags: int32 [192, 196], P(('rep', 'fsdp')), may hold values 0 or 1
- mask_token: bfloat16 [768], P('fsdp'), may hold values from -4 to 4
- norm1_gain: bfloat16 [768], P('fsdp'), may hold values from 0.099609375 to 1.8984375
- norm1_bias: bfloat16 [768], P('fsdp'), may hold values from -1.5 to 1.5
- qkv_weight: bfloat16 [768, 2304], P('fsdp'), may hold values from -0.21875 to 0.21875
- query_bias: bfloat16 [768], P('fsdp'), may hold values from -1.5 to 1.5
- value_bias: bfloat16 [768], P('fsdp'), may hold values from -1.5 to 1.5
- proj_weight: bfloat16 [768, 768], P('fsdp'), may hold values from -1.75 to 1.75
- proj_bias: bfloat16 [768], P('fsdp'), may hold values from -1.5 to 1.5
- norm2_gain: bfloat16 [768], P('fsdp'), may hold values from 0.099609375 to 1.8984375
- norm2_bias: bfloat16 [768], P('fsdp'), may hold values from -1.5 to 1.5
- fc1_weight: bfloat16 [768, 3072], P('fsdp'), may hold values from -0.21875 to 0.21875
- fc1_bias: bfloat16 [3072], P('fsdp'), may hold values from -1.5 to 1.5
- fc2_weight: bfloat16 [3072, 768], P('fsdp'), may hold values from -0.109375 to 0.109375
- fc2_bias: bfloat16 [768], P('fsdp'), may hold values from -1.5 to 1.5
- out_grad: bfloat16 [37632, 768], P(('rep', 'fsdp')), may hold values from -6 to 6
Outputs:
- block_out: bfloat16 [37632, 768], P(('rep', 'fsdp'))
- input_grad: float32 [37632, 768], P(('rep', 'fsdp'))
- grad_mask_token: float32 [768], P('fsdp')
- grad_norm1_gain: float32 [768], P('fsdp')
- grad_norm1_bias: float32 [768], P('fsdp')
- grad_qkv_weight: float32 [768, 2304], P('fsdp')
- grad_query_bias: float32 [768], P('fsdp')
- grad_value_bias: float32 [768], P('fsdp')
- grad_proj_weight: float32 [768, 768], P('fsdp')
- grad_proj_bias: float32 [768], P('fsdp')
- grad_norm2_gain: float32 [768], P('fsdp')
- grad_norm2_bias: float32 [768], P('fsdp')
- grad_fc1_weight: float32 [768, 3072], P('fsdp')
- grad_fc1_bias: float32 [3072], P('fsdp')
- grad_fc2_weight: float32 [3072, 768], P('fsdp')
- grad_fc2_bias: float32 [768], P('fsdp')
The draws below stay inside these ranges and needn't reach their ends.
Inputs may be any that keep to these rules, and one draw needn't show every extreme that they name: `mask_flags`: 1 marks a patch replaced by the mask token.
All inputs are finite; a program needn't handle non-finite values. No bound on the sum of `mask_flags` on one device may be relied on, other than what follows from the above.
Results may differ from the reference program's by a relative error of at most 0.012.
Values may be sent and summed in bfloat16 or wider, within the bound.
No kernel may reach another device: no remote copies, remote signals or barrier semaphores. Data moves between devices by JAX's collectives and lax.ppermute only.
A program may use at most 256 MiB of HBM per device.

```python
import math
import jax
import jax.numpy as jnp
from jax import lax

D = 768
HEADS = 12
FF = 3072
SEQ = 196
IMAGES = 192
TOKENS = 37632


def with_ends(drawn, rng, least, high):
    longest = drawn.shape.index(max(drawn.shape))
    spots = []
    for shift in (0, 1):
        where = [jax.random.randint(jax.random.fold_in(rng, axis), (), 0, length) for axis, length in enumerate(drawn.shape)]
        where[longest] = (where[longest] + shift) % drawn.shape[longest]
        spots.append(tuple(where))
    return drawn.at[spots[0]].set(least).at[spots[1]].set(high)


def raised(drawn, key, source, target, blocks, factor):
    owner, partner = [(jnp.arange(drawn.shape[axis_at]) // (drawn.shape[axis_at] // blocks)).reshape([-1 if axis == axis_at else 1 for axis in range(drawn.ndim)]) for axis_at in (source, target)]
    chosen = jax.random.permutation(key, blocks)[partner]
    strong = (owner == chosen) | (owner == (partner + blocks // 2) % blocks)
    return jnp.where(strong, factor * drawn, drawn)


def block_levels(own_key, dims, cuts, low, top_value):
    loudness = 1.0
    for axis_at, blocks in cuts:
        draws = jax.random.uniform(jax.random.fold_in(jax.random.fold_in(own_key, 6), axis_at), (blocks,), jnp.float32, low / len(cuts), top_value / len(cuts))
        loudness = loudness * jnp.repeat(jnp.exp(draws), dims[axis_at] // blocks).reshape((-1,) + (1,) * (len(dims) - 1 - axis_at))
    return loudness


def normal_values(own_key, shape, deviation, reach, shards=(), held_as=jnp.bfloat16):
    values = deviation * jax.random.normal(own_key, shape, jnp.float32)
    if shards:
        values = values * block_levels(own_key, shape, shards, -0.22, 0.18)
    return jnp.clip(values, -reach, reach).astype(held_as)


def gaussian_with(rng, shape, deviation, reach, cuts, heavy, dtype=jnp.bfloat16):
    result = deviation * jax.random.normal(rng, shape, jnp.float32)
    if cuts:
        result = result * block_levels(rng, shape, cuts, -0.22, 0.18)
    return jnp.clip(raised(result, jax.random.fold_in(rng, 3), *heavy), -reach, reach).astype(dtype)


def setup_inputs(seed: int = 0) -> dict:
    key_list = jax.random.split(jax.random.key(seed), 18)
    return {
        "tokens": gaussian_with(key_list[0], (TOKENS, D), 1.0, 6.0, ((0, 32),), (0, 1, 32, 2.75)),
        "mask_flags": with_ends((jax.random.randint(key_list[1], (IMAGES, SEQ), 0, 5) < 2).astype(jnp.int32), jax.random.fold_in(key_list[1], 1), 0, 1),
        "mask_token": normal_values(key_list[2], (D,), 1.0, 4.0, ((0, 16),)),
        "norm1_gain": jnp.clip(1.0 + 0.18 * jax.random.normal(key_list[3], (D,), jnp.float32), 0.099609375, 1.8984375).astype(jnp.bfloat16),
        "norm1_bias": normal_values(key_list[4], (D,), 0.3, 1.5, ((0, 16),)),
        "qkv_weight": normal_values(key_list[5], (D, 3 * D), D ** -0.5, 0.21875, ((0, 16),)),
        "query_bias": normal_values(key_list[6], (D,), 0.3, 1.5, ((0, 16),)),
        "value_bias": normal_values(key_list[7], (D,), 0.3, 1.5, ((0, 16),)),
        "proj_weight": normal_values(key_list[8], (D, D), (max(3 * D // SEQ, 1)) ** -0.5, 1.75, ((0, 16),)),
        "proj_bias": normal_values(key_list[9], (D,), 0.3, 1.5, ((0, 16),)),
        "norm2_gain": jnp.clip(1.0 + 0.18 * jax.random.normal(key_list[10], (D,), jnp.float32), 0.099609375, 1.8984375).astype(jnp.bfloat16),
        "norm2_bias": normal_values(key_list[11], (D,), 0.3, 1.5, ((0, 16),)),
        "fc1_weight": normal_values(key_list[12], (D, FF), D ** -0.5, 0.21875, ((0, 16),)),
        "fc1_bias": normal_values(key_list[13], (FF,), 0.3, 1.5, ((0, 16),)),
        "fc2_weight": normal_values(key_list[14], (FF, D), FF ** -0.5, 0.109375, ((0, 16),)),
        "fc2_bias": normal_values(key_list[15], (D,), 0.3, 1.5, ((0, 16),)),
        "out_grad": gaussian_with(key_list[16], (TOKENS, D), 1.0, 6.0, ((0, 32),), (0, 1, 32, 2.75)),
    }


@jax.custom_vjp
def low(v):
    return lax.optimization_barrier(v.astype(jnp.bfloat16)).astype(jnp.float32)

@jax.custom_vjp
def low_back(v):
    return v

def low_keep(v):
    return (low(v), None)

def low_pass(kept, grad):
    return (grad,)

def back_keep(v):
    return (v, None)

def back_low(kept, grad):
    return (low(grad),)
low.defvjp(low_keep, low_pass)
low_back.defvjp(back_keep, back_low)
highest = lax.Precision.HIGHEST
group_images = 16

def layer_norm(values, gain, shift):
    mean_row = lax.optimization_barrier(jnp.mean(values, axis=-1, keepdims=True))
    centred = values - mean_row
    spread = lax.optimization_barrier(jnp.mean(centred * centred, axis=-1, keepdims=True))
    return centred * lax.rsqrt(spread + 1e-06) * gain + shift

def exact_gelu(values):
    return jax.nn.gelu(values, approximate=False)

def group_block(inputs, params):
    rows_in, flags = inputs
    token_row, gain_one, shift_one, w_qkv, bias_query, bias_value, w_proj, bias_proj, gain_two, shift_two, w_up, bias_up, w_down, bias_down = params
    images, patches = flags.shape
    row_count, model_width = rows_in.shape
    head_dim = model_width // HEADS
    chosen = flags.reshape(row_count, 1) == 1
    block_in = jnp.where(chosen, token_row[None, :], rows_in)
    norm_one = low(layer_norm(block_in, gain_one, shift_one))
    qkv_bias = jnp.concatenate([bias_query, jnp.zeros_like(bias_query), bias_value])
    qkv_rows = low_back(low(jnp.dot(norm_one, w_qkv, precision=highest) + qkv_bias))
    shaped = qkv_rows.reshape(images, patches, 3, HEADS, head_dim)
    queries = shaped[:, :, 0]
    key_rows = shaped[:, :, 1]
    value_rows = shaped[:, :, 2]
    scores = low_back(jnp.einsum('bqhd,bkhd->bhqk', queries, key_rows, precision=highest) * (1.0 / math.sqrt(head_dim)))
    attn_probs = low(jax.nn.softmax(scores, axis=-1))
    attended = jnp.einsum('bhqk,bkhd->bqhd', attn_probs, value_rows, precision=highest).reshape(row_count, model_width)
    attended = low_back(low(attended))
    residual = block_in + low_back(jnp.dot(attended, w_proj, precision=highest)) + bias_proj
    norm_two = low(layer_norm(residual, gain_two, shift_two))
    hidden_pre = low_back(jnp.dot(norm_two, w_up, precision=highest) + bias_up)
    hidden_act = low(exact_gelu(hidden_pre))
    return residual + low_back(jnp.dot(hidden_act, w_down, precision=highest)) + bias_down

def reference(tokens, mask_flags, mask_token, norm1_gain, norm1_bias, qkv_weight, query_bias, value_bias, proj_weight, proj_bias, norm2_gain, norm2_bias, fc1_weight, fc1_bias, fc2_weight, fc2_bias, out_grad):
    params = tuple((member.astype(jnp.float32) for member in (mask_token, norm1_gain, norm1_bias, qkv_weight, query_bias, value_bias, proj_weight, proj_bias, norm2_gain, norm2_bias, fc1_weight, fc1_bias, fc2_weight, fc2_bias)))
    group_count = mask_flags.shape[0] // group_images
    flags_grouped = mask_flags.reshape(group_count, group_images, SEQ)
    stepper = jax.checkpoint(group_block)

    def forward(rows_all, weights_all):
        grouped = rows_all.reshape(group_count, group_images * SEQ, D)
        outputs = lax.map(lambda inputs: stepper(inputs, weights_all), (grouped, flags_grouped))
        return outputs.reshape(group_count * group_images * SEQ, D)
    block_out, backward = jax.vjp(forward, tokens.astype(jnp.float32), params)
    grad_rows, grad_params = backward(out_grad.astype(jnp.float32))
    return (block_out.astype(jnp.bfloat16), grad_rows) + tuple(grad_params)
```

```python
import functools
import math

import jax
import jax.numpy as jnp
from jax import lax
from jax.experimental import pallas as pl
from jax.experimental.pallas import tpu as pltpu
from jax.sharding import PartitionSpec as P

F32 = jnp.float32
BF16 = jnp.bfloat16
HEAD = 64
GROUP = 256
NEG = -1e30
VMEM = 56 * 2**20


def dot(a, b):
    return lax.dot_general(a, b, (((1,), (0,)), ((), ())), preferred_element_type=F32)


def dot_rows(a, b):
    return lax.dot_general(a, b, (((0,), (0,)), ((), ())), preferred_element_type=F32)


def dot_cols(a, b):
    return lax.dot_general(a, b, (((1,), (1,)), ((), ())), preferred_element_type=F32)


class Place:
    def __init__(self, count):
        self.count = count
        self.far = count // 4

    def own(self):
        index = lax.axis_index("fsdp")
        return index // 4, (index // 2) % 2, index % 2

    def other_core(self):
        return [(i, i ^ 1) for i in range(self.count)]

    def other_x(self):
        return [(i, i ^ 2) for i in range(self.count)]

    def along_z(self, step):
        return [(i, (i + 4 * step) % self.count) for i in range(self.count)]

    def row_of(self, own, dc, dx, dz):
        z, x, c = own
        zz = lax.rem(z + (dz % self.far), self.far)
        xx = x if dx == 0 else 1 - x
        cc = c if dc == 0 else 1 - c
        return (zz * 2 + xx) * 2 + cc


def gather_pieces(place, stack):
    came = [stack]
    for step in range(1, place.far):
        came.append(lax.ppermute(stack, "fsdp", place.along_z(step)))
    mine = jnp.stack(came)
    beside = lax.ppermute(mine, "fsdp", place.other_x())
    mine_core = lax.ppermute(mine, "fsdp", place.other_core())
    beside_core = lax.ppermute(beside, "fsdp", place.other_core())
    return [mine, beside, mine_core, beside_core]


def add_low(*terms):
    total = terms[0].astype(F32)
    for term in terms[1:]:
        total = total + term.astype(F32)
    return total


def scatter_pieces(place, keep, send):
    kind = keep.dtype
    came = lax.ppermute(send, "fsdp", place.other_core())
    across = add_low(keep[1], came[1]).astype(kind)
    from_x = lax.ppermute(across, "fsdp", place.other_x())
    parts = [add_low(keep[0, d], came[0, d], from_x[d]).astype(kind) for d in range(place.far)]
    terms = [parts[0]]
    for step in range(1, place.far):
        terms.append(lax.ppermute(parts[step], "fsdp", place.along_z(step)))
    summed = add_low(*terms).astype(kind)
    twin = lax.ppermute(summed, "rep", [(0, 1), (1, 0)])
    return add_low(summed, twin)


def load_weight(place, refs, spot, lead=0):
    own = place.own()
    rows = refs[0].shape[2]
    for which, ref in enumerate(refs):
        for d in range(place.far):
            at = place.row_of(own, which // 2, which % 2, -d) * rows
            spot[pl.ds(pl.multiple_of(at, 16), rows), :] = ref[d, lead]


def store_grad(place, spot, keep, send, lead=0):
    own = place.own()
    rows = keep.shape[3]
    for dc, ref in enumerate((keep, send)):
        for dx in range(2):
            for d in range(place.far):
                at = place.row_of(own, dc, dx, d) * rows
                ref[dx, d, lead] = spot[pl.ds(pl.multiple_of(at, 16), rows), :]


def norm_stats(v):
    mean = jnp.mean(v, axis=-1, keepdims=True)
    centred = v - mean
    spread = jnp.mean(centred * centred, axis=-1, keepdims=True)
    scale = lax.rsqrt(spread + 1e-06)
    return centred * scale, scale


def norm_back(up, xhat, scale, gain):
    e = up * gain
    return (e - jnp.mean(e, axis=-1, keepdims=True) - xhat * jnp.mean(e * xhat, axis=-1, keepdims=True)) * scale


ERF_P = 0.3275911 / math.sqrt(2.0)
ERF_A = (0.254829592, -0.284496736, 1.421413741, -1.453152027, 1.061405429)


def gelu_and_slope(z):
    t = 1.0 / (1.0 + ERF_P * jnp.abs(z))
    e = jnp.exp(-0.5 * (z * z))
    poly = 0.5 * ERF_A[4]
    for a in ERF_A[3::-1]:
        poly = poly * t + 0.5 * a
    q = poly * t * e
    phi = jnp.where(z > 0, 1.0 - q, q)
    return z * phi, phi + z * (e * (1.0 / math.sqrt(2.0 * math.pi)))


class Rows:
    def __init__(self, images, patches):
        self.images = images
        self.patches = patches
        self.pad = -(-patches // 16) * 16
        self.all = images * self.pad
        self.raw = images * patches


def flag_column(rows, flags):
    wide = flags[...].astype(F32)
    wide = jnp.concatenate([wide, jnp.zeros((8 - rows.images, rows.patches), F32)], axis=0)
    gap = -rows.patches % 128
    return jnp.concatenate([wide, jnp.zeros((8, gap), F32)], axis=1).T


def norm_one_kernel(rows, tokens, flags, grads, vec, base_o, norm_o, grad_o):
    cols = flag_column(rows, flags)
    token = vec[0:1, :]
    gain, shift = vec[1:2, :], vec[2:3, :]
    gap = jnp.zeros((rows.pad - rows.patches, tokens.shape[1]), F32)
    for i in range(rows.images):
        lo = rows.patches * i
        at = pl.ds(rows.pad * i, rows.pad)
        first = lo // 16 * 16
        last = min(-(-(lo + rows.patches) // 16) * 16, rows.raw)
        part = tokens[first:last, :].astype(F32)[lo - first : lo - first + rows.patches]
        base = jnp.where(cols[: rows.patches, i : i + 1] > 0.5, token, part)
        base = jnp.concatenate([base, gap], axis=0)
        base_o[at, :] = base.astype(BF16)
        xhat, _ = norm_stats(base)
        norm_o[at, :] = (xhat * gain + shift).astype(BF16)
        part = grads[first:last, :].astype(F32)[lo - first : lo - first + rows.patches]
        grad_o[at, :] = jnp.concatenate([part, gap], axis=0).astype(BF16)


def whole(shape):
    return pl.BlockSpec(shape, lambda *j: (0,) * len(shape))


def params():
    return pltpu.CompilerParams(vmem_limit_bytes=VMEM)


def cost(flops, count):
    return pl.CostEstimate(flops=int(flops), bytes_accessed=int(count), transcendentals=0)


def norm_one_call(rows, tokens, flags, grads, vec):
    width = tokens.shape[1]
    out = jax.ShapeDtypeStruct((rows.all, width), BF16)
    return pl.pallas_call(
        functools.partial(norm_one_kernel, rows),
        out_shape=[out, out, out],
        compiler_params=params(),
        cost_estimate=cost(4e9, 9e6),
        name="norm_one",
    )(tokens, flags, grads, vec)


def halves(x, first):
    zero = jnp.zeros_like(x)
    return jnp.concatenate([jnp.where(first, x, zero), jnp.where(first, zero, x)], axis=0)


def attend_kernel(place, rows, base_group, norm, vec, *refs):
    nw = 4 if place else 1
    w_in, (q_o, k_o, v_o, att_o, p_o), rest = refs[:nw], refs[nw : nw + 5], refs[nw + 5 :]
    j = pl.program_id(0)
    if place:
        w = rest[0].at[0]
        load_weight(place, w_in, w)
    else:
        w = w_in[0].at[0]
    x = norm[...]
    lanes = pl.ds(pl.multiple_of((base_group + j) * GROUP, GROUP), GROUP)
    q_o[0] = ((dot(x, w[:, 0:GROUP]) + vec[3:4, lanes]).astype(BF16) * 0.125).astype(BF16)
    k_o[0] = dot(x, w[:, GROUP : 2 * GROUP]).astype(BF16)
    v_o[0] = (dot(x, w[:, 2 * GROUP :]) + vec[4:5, lanes]).astype(BF16)
    s = rows.pad
    first = lax.broadcasted_iota(jnp.int32, (s, 128), 1) < HEAD
    live = lax.broadcasted_iota(jnp.int32, (s, 2 * s), 0) < rows.patches

    def image(i):
        at = pl.ds(pl.multiple_of(i * s, 16), s)
        for p in range(2):
            cols = pl.ds(128 * p, 128)
            q, k, v = q_o[0, at, cols], k_o[0, at, cols], v_o[0, at, cols]
            score = jnp.where(live, dot_cols(k, halves(q, first)), NEG)
            peak = jnp.max(score, axis=0, keepdims=True)
            e = jnp.exp(score - peak)
            probs = (e * (1.0 / jnp.sum(e, axis=0, keepdims=True))).astype(BF16)
            p_o[0, p, i] = probs
            o = dot_rows(probs, v)
            att_o[0, at, cols] = jnp.where(first, o[:s], o[s:]).astype(BF16)

    def step(i, carry):
        for u in range(3):
            image(i * 3 + u)
        return carry

    lax.fori_loop(0, rows.images // 3, step, 0)


def piece_specs(place, weight, blocks=1):
    if place is None:
        return [pl.BlockSpec((blocks, *weight[0].shape[1:]), lambda j: (j, 0, 0))]
    z, _, r, w = weight[0].shape
    return [pl.BlockSpec((z, blocks, r, w), lambda j: (0, j, 0, 0))] * 4


def attend_call(place, rows, base_group, groups, norm, vec, weight):
    s = rows.pad
    width = norm.shape[1]
    row = pl.BlockSpec((1, rows.all, GROUP), lambda j: (j, 0, 0))
    out = jax.ShapeDtypeStruct((groups, rows.all, GROUP), BF16)
    outs = [out] * 4 + [jax.ShapeDtypeStruct((groups, 2, rows.images, s, 2 * s), BF16)]
    specs = [row] * 4 + [pl.BlockSpec((1, 2, rows.images, s, 2 * s), lambda j: (j, 0, 0, 0, 0))]
    if place:
        outs.append(jax.ShapeDtypeStruct((groups, width, 3 * GROUP), BF16))
        specs.append(pl.BlockSpec((1, width, 3 * GROUP), lambda j: (j, 0, 0)))
    res = pl.pallas_call(
        functools.partial(attend_kernel, place, rows, base_group),
        grid=(groups,),
        in_specs=[whole(norm.shape), whole(vec.shape)] + piece_specs(place, weight),
        out_specs=specs,
        out_shape=outs,
        compiler_params=params(),
        cost_estimate=cost(groups * 6e9, groups * 8e6),
        name="attend",
    )(norm, vec, *weight)
    return list(res) if place else list(res) + [weight[0]]


def project_kernel(place, groups, vec, base, *refs):
    nw = 4 if place else 1
    na = len(groups)
    atts, w_in, rest = refs[:na], refs[na : na + nw], refs[na + nw :]
    resid_o, norm_o = rest[:2]
    if place:
        w = rest[2]
        load_weight(place, w_in, w)
    else:
        w = w_in[0].at[0]
    total = base[...].astype(F32) + vec[5:6, :]
    g = 0
    for a, count in zip(atts, groups):
        for b in range(count):
            total = total + dot(a[b], w[pl.ds(g * GROUP, GROUP), :])
            g += 1
    resid_o[...] = total
    xhat, _ = norm_stats(total)
    norm_o[...] = (xhat * vec[6:7, :] + vec[7:8, :]).astype(BF16)


def project_call(place, rows, vec, base, atts, weight):
    width = base.shape[1]
    outs = [jax.ShapeDtypeStruct((rows.all, width), F32), jax.ShapeDtypeStruct((rows.all, width), BF16)]
    if place:
        outs.append(jax.ShapeDtypeStruct((width, width), BF16))
    res = pl.pallas_call(
        functools.partial(project_kernel, place, [a.shape[0] for a in atts]),
        out_shape=outs,
        compiler_params=params(),
        cost_estimate=cost(3e9, 12e6),
        name="project",
    )(vec, base, *atts, *weight)
    return list(res) if place else list(res) + [weight[0][0]]


def feed_kernel(place, rows, first_block, carried, norm, grad, vec, *refs):
    nw = 4 if place else 1
    w_in, rest = refs[:nw], refs[nw:]
    if carried:
        (acc_in, gn_in), rest = rest[:2], rest[2:]
    acc_o, gn_o, bias_o = rest[:3]
    j = pl.program_id(0)
    if place:
        keep, send, w_up, w_down, act_s, gp_s, g_s = rest[3:]
        load_weight(place, w_in, w_up, 0)
        load_weight(place, w_in, w_down, 1)
    else:
        grads_o, act_s, gp_s = rest[3:]
        w_up, w_down = w_in[0].at[0], w_in[0].at[1]

    @pl.when(j == 0)
    def _():
        if carried:
            acc_o[...] = acc_in[...]
            gn_o[...] = gn_in[...]
        else:
            acc_o[...] = jnp.zeros_like(acc_o)
            gn_o[...] = jnp.zeros_like(gn_o)

    bias = vec[pl.ds(9 + first_block + j, 1), :]
    step = rows.pad
    for b in range(rows.images):
        at = pl.ds(b * step, step)
        z = dot(norm[at, :], w_up[...]) + bias
        up = dot_cols(grad[at, :], w_down[...])
        act, slope = gelu_and_slope(z)
        act = act.astype(BF16)
        gp = (up * slope).astype(BF16)
        act_s[at, :] = act
        gp_s[at, :] = gp
        acc_o[at, :] += dot(act, w_down[...])
        gn_o[at, :] += dot_cols(gp, w_up[...])
    bias_o[0] = jnp.sum(gp_s[...].astype(F32), axis=0, keepdims=True)
    g_up = dot_rows(norm[...], gp_s[...]).astype(BF16)
    if place:
        g_s[...] = g_up
        store_grad(place, g_s, keep, send, 0)
    else:
        grads_o[0] = g_up
    g_down = dot_rows(act_s[...], grad[...]).astype(BF16)
    if place:
        g_s[...] = g_down
        store_grad(place, g_s, keep, send, 1)
    else:
        grads_o[1] = g_down


def grad_out(place, blocks, width, r, per_step):
    if place is None:
        return (
            [jax.ShapeDtypeStruct((blocks, width, width), BF16)],
            [pl.BlockSpec((per_step, width, width), lambda j: (j, 0, 0))],
        )
    shape = (2, place.far, blocks, r, width)
    block = (2, place.far, per_step, r, width)
    return (
        [jax.ShapeDtypeStruct(shape, BF16)] * 2,
        [pl.BlockSpec(block, lambda j: (0, 0, j, 0, 0))] * 2,
    )


def feed_call(place, rows, first_block, blocks, norm, grad, vec, weight, carried=None):
    width = norm.shape[1]
    r = weight[0].shape[2] if place else None
    acc = jax.ShapeDtypeStruct((rows.all, width), F32)
    outs, specs = grad_out(place, 2 * blocks, width, r, 2)
    scratch = [pltpu.VMEM((rows.all, width), BF16)] * 2
    if place:
        scratch = [pltpu.VMEM((width, width), BF16)] * 2 + scratch + [pltpu.VMEM((width, width), BF16)]
    args = [norm, grad, vec, *weight]
    in_specs = [whole(norm.shape), whole(grad.shape), whole(vec.shape)] + piece_specs(place, weight, 2)
    if carried:
        args += list(carried)
        in_specs += [whole(acc.shape)] * 2
    return pl.pallas_call(
        functools.partial(feed_kernel, place, rows, first_block, bool(carried)),
        grid=(blocks,),
        in_specs=in_specs,
        out_specs=[whole(acc.shape)] * 2 + [pl.BlockSpec((1, 1, width), lambda j: (j, 0, 0))] + specs,
        out_shape=[acc, acc, jax.ShapeDtypeStruct((blocks, 1, width), F32)] + outs,
        scratch_shapes=scratch,
        compiler_params=params(),
        cost_estimate=cost(blocks * 1.2e10, blocks * 20e6),
        name="feed",
    )(*args)


def middle_kernel(rows, resid, acc, gn, grad, vec, w, out_o, gres_o, low_o, da_o, sums_o):
    xhat, scale = norm_stats(resid[...])
    gain = vec[6:7, :]
    up = gn[...]
    g = grad[...].astype(F32)
    total = g + norm_back(up, xhat, scale, gain)
    gres_o[...] = total
    low = total.astype(BF16)
    low_o[...] = low
    da_o[...] = dot_cols(low, w[...]).astype(BF16)
    sums_o[...] = jnp.concatenate(
        [
            jnp.sum(total, axis=0, keepdims=True),
            jnp.sum(up * xhat, axis=0, keepdims=True),
            jnp.sum(up, axis=0, keepdims=True),
            jnp.sum(g, axis=0, keepdims=True),
        ],
        axis=0,
    )
    final = resid[...] + acc[...] + vec[8:9, :]
    parts = [final[rows.pad * i : rows.pad * i + rows.patches] for i in range(rows.images)]
    out_o[...] = jnp.concatenate(parts, axis=0).astype(BF16)


def middle_call(rows, resid, acc, gn, grad, vec, w):
    width = resid.shape[1]
    return pl.pallas_call(
        functools.partial(middle_kernel, rows),
        out_shape=[
            jax.ShapeDtypeStruct((rows.raw, width), BF16),
            jax.ShapeDtypeStruct((rows.all, width), F32),
            jax.ShapeDtypeStruct((rows.all, width), BF16),
            jax.ShapeDtypeStruct((rows.all, width), BF16),
            jax.ShapeDtypeStruct((4, width), F32),
        ],
        compiler_params=params(),
        cost_estimate=cost(4e9, 20e6),
        name="middle",
    )(resid, acc, gn, grad, vec, w)


def attend_back_kernel(place, rows, base_group, projects, carried, norm, q_i, k_i, v_i, p_i, da, w, *refs):
    j = pl.program_id(0)
    lead = 1 if projects else 0
    if projects:
        (low, *atts), refs = refs[: 1 + projects], refs[1 + projects :]
    if carried:
        gn_in, refs = refs[0], refs[1:]
    gn_o, bias_o = refs[:2]
    if place:
        keep, send, d_s, g_s = refs[2:]
    else:
        grads_o, d_s = refs[2:]
    s = rows.pad
    first = lax.broadcasted_iota(jnp.int32, (s, 128), 1) < HEAD

    def emit(value):
        if place:
            g_s[...] = value.astype(BF16)
            store_grad(place, g_s, keep, send)
        else:
            grads_o[0] = value.astype(BF16)

    if projects:

        @pl.when(j == 0)
        def _():
            both = jnp.concatenate([a[b] for a in atts for b in range(a.shape[0])], axis=1)
            emit(dot_rows(both, low[...]))

    @pl.when(j == lead)
    def _():
        gn_o[...] = gn_in[...] if carried else jnp.zeros_like(gn_o)

    def image(i):
        at = pl.ds(pl.multiple_of(i * s, 16), s)
        for p in range(2):
            cols = pl.ds(128 * p, 128)
            q, k, v = q_i[0, at, cols], k_i[0, at, cols], v_i[0, at, cols]
            q2, da2 = halves(q, first), halves(da[at, cols], first)
            low_probs = p_i[0, p, i]
            d_s[at, pl.ds(2 * GROUP + 128 * p, 128)] = dot(low_probs, da2).astype(BF16)
            up = dot_cols(v, da2)
            probs = low_probs.astype(F32)
            inner = jnp.sum(probs * up, axis=0, keepdims=True)
            ds = (probs * (up - inner)).astype(BF16)
            d_s[at, pl.ds(GROUP + 128 * p, 128)] = dot(ds, q2).astype(BF16)
            dq = dot_rows(ds, k)
            d_s[at, cols] = (jnp.where(first, dq[:s], dq[s:]) * 0.125).astype(BF16)

    def group():
        def step(i, carry):
            for u in range(3):
                image(i * 3 + u)
            return carry

        lax.fori_loop(0, rows.images // 3, step, 0)
        bias_o[0] = jnp.sum(d_s[...].astype(F32), axis=0, keepdims=True)
        emit(dot_rows(norm[...], d_s[...]))
        gn_o[...] += dot_cols(d_s[...], w[0])

    if projects:
        pl.when(j >= 1)(group)
    else:
        group()


def attend_back_call(place, rows, base_group, norm, q, k, v, probs, da, w, r, project=None, carried=None):
    groups = q.shape[0]
    width = norm.shape[1]
    s = rows.pad
    lead = 1 if project else 0
    steps = groups + lead

    def at(j):
        return jnp.maximum(j - lead, 0) if lead else j

    row = pl.BlockSpec((1, rows.all, GROUP), lambda j: (at(j), 0, 0))
    in_specs = [whole(norm.shape), row, row, row]
    in_specs += [pl.BlockSpec((1, 2, rows.images, s, 2 * s), lambda j: (at(j), 0, 0, 0, 0))]
    in_specs += [pl.BlockSpec((rows.all, GROUP), lambda j: (0, base_group + at(j)))]
    in_specs += [pl.BlockSpec((1, width, 3 * GROUP), lambda j: (at(j), 0, 0))]
    args = [norm, q, k, v, probs, da, w]
    if project:
        args += list(project)
        in_specs += [whole(a.shape) for a in project]
    if carried is not None:
        args.append(carried)
        in_specs.append(whole(carried.shape))
    outs, specs = grad_out(place, steps, width, r, 1)
    scratch = [pltpu.VMEM((rows.all, 3 * GROUP), BF16)]
    if place:
        scratch.append(pltpu.VMEM((width, 3 * GROUP), BF16))
    return pl.pallas_call(
        functools.partial(
            attend_back_kernel, place, rows, base_group, len(project) - 1 if project else 0, carried is not None
        ),
        grid=(steps,),
        in_specs=in_specs,
        out_specs=[whole((rows.all, width)), pl.BlockSpec((1, 1, 3 * GROUP), lambda j: (at(j), 0, 0))] + specs,
        out_shape=[
            jax.ShapeDtypeStruct((rows.all, width), F32),
            jax.ShapeDtypeStruct((groups, 1, 3 * GROUP), F32),
        ]
        + outs,
        scratch_shapes=scratch,
        compiler_params=params(),
        cost_estimate=cost(steps * 8e9, steps * 12e6),
        name="attend_back",
    )(*args)


def last_kernel(rows, base, gn, gres, flags, vec, out_o, sums_o):
    cols = flag_column(rows, flags)
    gain = vec[1:2, :]
    token = jnp.zeros((1, base.shape[1]), F32)
    gain_sum, shift_sum = token, token
    for i in range(rows.images):
        at = pl.ds(rows.pad * i, rows.pad)
        xhat, scale = norm_stats(base[at, :].astype(F32))
        up = gn[at, :]
        total = gres[at, :] + norm_back(up, xhat, scale, gain)
        chosen = cols[: rows.pad, i : i + 1] > 0.5
        token = token + jnp.sum(jnp.where(chosen, total, 0.0), axis=0, keepdims=True)
        gain_sum = gain_sum + jnp.sum(up * xhat, axis=0, keepdims=True)
        shift_sum = shift_sum + jnp.sum(up, axis=0, keepdims=True)
        out_o[pl.ds(rows.patches * i, rows.patches), :] = jnp.where(chosen, 0.0, total)[: rows.patches]
    sums_o[...] = jnp.concatenate([token, gain_sum, shift_sum], axis=0)


def last_call(rows, base, gn, gres, flags, vec):
    width = base.shape[1]
    return pl.pallas_call(
        functools.partial(last_kernel, rows),
        out_shape=[jax.ShapeDtypeStruct((rows.raw, width), F32), jax.ShapeDtypeStruct((3, width), F32)],
        compiler_params=params(),
        cost_estimate=cost(4e9, 14e6),
        name="last",
    )(base, gn, gres, flags, vec)


def local(
    count,
    tokens,
    mask_flags,
    mask_token,
    norm1_gain,
    norm1_bias,
    qkv_weight,
    query_bias,
    value_bias,
    proj_weight,
    proj_bias,
    norm2_gain,
    norm2_bias,
    fc1_weight,
    fc1_bias,
    fc2_weight,
    fc2_bias,
    out_grad,
):
    images, patches = mask_flags.shape
    rows = Rows(images, patches)
    r, width = proj_weight.shape
    place = Place(count) if r % 16 == 0 else None
    quarter = fc1_weight.shape[1] // width

    qkv_blocks = qkv_weight.reshape(r, 3, 3, GROUP).transpose(2, 0, 1, 3).reshape(3, r, 3 * GROUP)
    up_blocks = fc1_weight.reshape(r, count, quarter, r).transpose(2, 0, 1, 3).reshape(quarter, r, width)
    down_blocks = fc2_weight.reshape(quarter, r, width)
    small = jnp.concatenate(
        [
            mask_token,
            norm1_gain,
            norm1_bias,
            query_bias,
            value_bias,
            proj_bias,
            norm2_gain,
            norm2_bias,
            fc2_bias,
            fc1_bias,
        ]
    )
    kinds = small.shape[0] // r

    if place:
        z, x, c = place.own()
        padded = jnp.pad(small, (0, -small.shape[0] % 1024)).reshape(1, -1, 128)
        came = jnp.stack(gather_pieces(place, padded))
        came = came.reshape(2, 2, place.far, -1)[..., : small.shape[0]]
        came = jnp.where(c == 0, came, came[::-1])
        came = jnp.where(x == 0, came, came[:, ::-1])
        came = jnp.roll(came[:, :, ::-1], z + 1, axis=2)
        came = came.transpose(2, 1, 0, 3).reshape(count, kinds, r)

        def gather(stack):
            return gather_pieces(place, stack)

        def scatter(pieces):
            return scatter_pieces(place, *pieces)

    else:
        came = lax.all_gather(small, "fsdp", axis=0, tiled=True).reshape(count, kinds, r)

        def gather(stack):
            return [lax.all_gather(stack, "fsdp", axis=1, tiled=True)]

        def scatter(pieces):
            share = lax.psum_scatter(pieces[0].astype(F32), "fsdp", scatter_dimension=1, tiled=True)
            return lax.psum(share, "rep")

    vec = came.transpose(1, 0, 2).reshape(kinds, width).astype(F32)
    vec = jnp.pad(vec, ((0, 16 - kinds), (0, 0)))

    w_a = gather(qkv_blocks[:1])
    w_b = gather(qkv_blocks[1:])
    w_p = gather(proj_weight[None])
    ff = jnp.stack([up_blocks, down_blocks], axis=1).reshape(2 * quarter, r, width)
    w_f = [gather(ff[:quarter]), gather(ff[quarter:])]

    base, norm, grad = norm_one_call(rows, tokens, mask_flags, out_grad, vec)
    q_a, k_a, v_a, att_a, p_a, wq_a = attend_call(place, rows, 0, 1, norm, vec, w_a)
    q_b, k_b, v_b, att_b, p_b, wq_b = attend_call(place, rows, 1, 2, norm, vec, w_b)
    resid, norm_two, w_proj = project_call(place, rows, vec, base, [att_a, att_b], w_p)

    half = quarter // 2
    acc, gn, gb_a, *gf_a = feed_call(place, rows, 0, half, norm_two, grad, vec, w_f[0])
    acc, gn, gb_b, *gf_b = feed_call(place, rows, half, half, norm_two, grad, vec, w_f[1], (acc, gn))
    sum_fa = scatter(gf_a)

    block_out, gres, low, da, sums_two = middle_call(rows, resid, acc, gn, grad, vec, w_proj)
    sum_fb = scatter(gf_b)
    gn1, qb_b, *gq_b = attend_back_call(
        place, rows, 1, norm, q_b, k_b, v_b, p_b, da, wq_b, r, project=[low, att_a, att_b]
    )
    sum_qb = scatter(gq_b)
    gn1, qb_a, *gq_a = attend_back_call(place, rows, 0, norm, q_a, k_a, v_a, p_a, da, wq_a, r, carried=gn1)
    sum_qa = scatter(gq_a)
    input_grad, sums_one = last_call(rows, base, gn1, gres, mask_flags, vec)

    qkv_sums = jnp.concatenate([qb_a, qb_b], axis=0)[:, 0]
    late = jnp.concatenate(
        [
            sums_one,
            qkv_sums[:, :GROUP].reshape(1, width),
            qkv_sums[:, 2 * GROUP :].reshape(1, width),
            sums_two,
            gb_a[:, 0],
            gb_b[:, 0],
        ],
        axis=0,
    )
    late = late.reshape(kinds, count, r).transpose(1, 0, 2).reshape(count, kinds * r)
    if place:
        late = jnp.pad(late, ((0, 0), (0, -late.shape[1] % 1024))).reshape(place.far, 2, 2, -1, 128)
        late = jnp.roll(late, -z, axis=0)
        late = jnp.where(x == 0, late, late[:, ::-1]).transpose(1, 2, 0, 3, 4)
        late = jnp.where(c == 0, late, late[:, ::-1])
        shares = scatter_pieces(place, late[:, 0], late[:, 1]).reshape(-1)[: kinds * r]
    else:
        shares = lax.psum(lax.psum_scatter(late, "fsdp", scatter_dimension=0, tiled=True), "rep").reshape(-1)
    shares = shares.reshape(kinds, r)
    token_s, gain1_s, shift1_s, qb_s, vb_s, pb_s, gain2_s, shift2_s, db_s = [shares[i] for i in range(9)]
    ub_s = shares[9:].reshape(-1)

    g_qkv = jnp.concatenate([sum_qa, sum_qb[1:]], axis=0).reshape(3, r, 3, GROUP)
    g_qkv = g_qkv.transpose(1, 2, 0, 3).reshape(r, 3 * width)
    g_ff = jnp.concatenate([sum_fa, sum_fb], axis=0).reshape(quarter, 2, r, width)
    g_up = g_ff[:, 0].reshape(quarter, r, count, r).transpose(1, 2, 0, 3).reshape(r, quarter * width)
    g_down = g_ff[:, 1].reshape(quarter * r, width)
    return (
        block_out,
        input_grad,
        token_s,
        gain1_s,
        shift1_s,
        g_qkv,
        qb_s,
        vb_s,
        sum_qb[0],
        pb_s,
        gain2_s,
        shift2_s,
        g_up,
        ub_s,
        g_down,
        db_s,
    )


def solution(mesh):
    both, one = P(("rep", "fsdp"), None), P("fsdp")
    flat = P("fsdp", None)
    in_specs = (both, both, one, one, one, flat, one, one, flat, one, one, one, flat, one, flat, one, both)
    out_specs = (both, both, one, one, one, flat, one, one, flat, one, one, one, flat, one, flat, one)
    return jax.shard_map(
        functools.partial(local, mesh.shape["fsdp"]),
        mesh=mesh,
        in_specs=in_specs,
        out_specs=out_specs,
        check_vma=False,
    )
```

```python
import functools
import math

import jax
import jax.numpy as jnp
from jax import lax
from jax.experimental import pallas as pl
from jax.experimental.pallas import tpu as pltpu
from jax.sharding import PartitionSpec as P

F32 = jnp.float32
BF16 = jnp.bfloat16
HEAD = 64
GROUP = 256
NEG = -1e30
VMEM = 56 * 2**20


def dot(a, b):
    return lax.dot_general(a, b, (((1,), (0,)), ((), ())), preferred_element_type=F32)


def dot_rows(a, b):
    return lax.dot_general(a, b, (((0,), (0,)), ((), ())), preferred_element_type=F32)


def dot_cols(a, b):
    return lax.dot_general(a, b, (((1,), (1,)), ((), ())), preferred_element_type=F32)


FAR = 4


class Place:
    def __init__(self, count):
        self.count = count

    def own(self):
        index = lax.axis_index("fsdp")
        return index // 4, (index // 2) % 2, index % 2

    def swap(self, bits):
        return [(i, i ^ bits) for i in range(self.count)]

    def core(self, v):
        return lax.ppermute(v, "fsdp", self.swap(1))

    def along_x(self, v):
        return lax.ppermute(v, "fsdp", self.swap(2))

    def along_z(self, d):
        return lambda v: lax.ppermute(v, "fsdp", self.swap(4 * d))

    def along_y(self, v):
        return lax.ppermute(v, "rep", [(0, 1), (1, 0)])

    def along_xy(self, v):
        n = self.count
        return lax.ppermute(
            v, ("rep", "fsdp"), [(y * n + i, (1 - y) * n + (i ^ 2)) for y in range(2) for i in range(n)]
        )


def shard_at(own, dc, dx, dz):
    z, x, c = own
    return (lax.bitwise_xor(z, dz) * 2 + lax.bitwise_xor(x, dx)) * 2 + lax.bitwise_xor(c, dc)


def add_low(*terms):
    total = terms[0].astype(F32)
    for term in terms[1:]:
        total = total + term.astype(F32)
    return total


def low(v):
    return v.astype(BF16)


def by_side(side, first, second, axis):
    return jnp.where(side == 0, jnp.concatenate([first, second], axis), jnp.concatenate([second, first], axis))


class Weight:
    def __init__(self, kind, arrays):
        self.kind = kind
        self.arrays = arrays


def gather_fast(place, stack):
    came = yield [(place.along_z(d), stack) for d in range(1, FAR)]
    own = jnp.stack([stack] + came)
    beside, own_core = yield [(place.along_x, own), (place.core, own)]
    (beside_core,) = yield [(place.core, beside)]
    return Weight("rows", [own, beside, own_core, beside_core])


def half_columns(stack):
    half = stack.shape[2] // 2
    return lax.dynamic_slice_in_dim(stack, lax.axis_index("rep") * half, half, axis=2)


def gather_wide(place, stack):
    mine = half_columns(stack)
    came = yield [(place.along_z(d), mine) for d in range(1, FAR)]
    own = jnp.stack([mine] + came)
    came = yield [(place.along_x, own), (place.along_y, own), (place.along_xy, own)]
    here = jnp.stack([own] + came)
    (across,) = yield [(place.core, here)]
    return Weight("halves", [here, across])


def gather_even(place, stack):
    mine = half_columns(stack)
    came = yield [(place.along_z(d), mine) for d in range(1, FAR)]
    own = jnp.stack([mine] + came)
    beside, twin = yield [(place.along_x, own), (place.along_y, own)]
    corner = yield [(place.along_y, beside[:2]), (place.along_x, twin[2:])]
    here = jnp.stack([own, beside, twin, jnp.concatenate(corner)])
    (across,) = yield [(place.core, here)]
    return Weight("halves", [here, across])


def gather_late_y(place, stack):
    mine = half_columns(stack)
    came = yield [(place.along_z(d), mine) for d in range(1, FAR)]
    own = jnp.stack([mine] + came)
    (beside,) = yield [(place.along_x, own)]
    side = jnp.stack([own, beside])
    (twin,) = yield [(place.along_y, side)]
    here = jnp.concatenate([side, twin])
    (across,) = yield [(place.core, here)]
    return Weight("halves", [here, across])


def scatter_early_y(place, keep, send):
    (came,) = yield [(place.core, send)]
    (came_y,) = yield [(place.along_y, low(add_low(keep[1], came[1])))]
    (came_x,) = yield [(place.along_x, low(add_low(keep[0, 1], came[0, 1], came_y[1])))]
    total = low(add_low(keep[0, 0], came[0, 0], came_y[0], came_x))
    came = yield [(place.along_z(d), total[d]) for d in range(1, FAR)]
    return low(add_low(total[0], *came))


def scatter_wide(place, keep, send):
    (came,) = yield [(place.core, send)]

    def pair(dy, dx):
        return low(add_low(keep[dy, dx], came[dy, dx]))

    came_xy = yield [(place.along_x, pair(0, 1)), (place.along_y, pair(1, 0)), (place.along_xy, pair(1, 1))]
    total = low(add_low(keep[0, 0], came[0, 0], *came_xy))
    came = yield [(place.along_z(d), total[d]) for d in range(1, FAR)]
    return low(add_low(total[0], *came))


def send_twin(place, *mine):
    twins = yield [(place.along_y, v) for v in mine]
    return list(mine), twins


class Flow:
    def __init__(self):
        self.live = {}
        self.done = {}

    def begin(self, name, steps):
        self.live[name] = (steps, next(steps), None)

    def send(self, *arrays):
        waiting = [name for name, (_, pairs, sent) in self.live.items() if sent is None]
        flat = [v for name in waiting for _, v in self.live[name][1]]
        flat = list(lax.optimization_barrier(tuple(flat) + tuple(arrays)))
        for name in waiting:
            steps, pairs, _ = self.live[name]
            sent = [move(v) for (move, _), v in zip(pairs, flat)]
            flat = flat[len(pairs) :]
            self.live[name] = (steps, pairs, sent)
        return flat

    def meet(self, names, *arrays):
        names = [name for name in names if name in self.live]
        flat = [v for name in names for v in self.live[name][2]]
        flat = list(lax.optimization_barrier(tuple(flat) + tuple(arrays)))
        for name in names:
            steps, pairs, _ = self.live[name]
            mine, flat = flat[: len(pairs)], flat[len(pairs) :]
            try:
                self.live[name] = (steps, steps.send(mine), None)
            except StopIteration as stop:
                del self.live[name]
                self.done[name] = stop.value
        return flat

    def turn(self, names, *arrays):
        return self.send(*self.meet(names, *arrays))


def half_at(dy, width):
    at = lax.bitwise_xor(lax.axis_index("rep"), dy) * width
    return pl.ds(pl.multiple_of(at, 128), width)


def load_weight(place, kind, rows, refs, spot, lead=0):
    own = place.own()
    for dc in range(2):
        for dx in range(2):
            for d in range(FAR):
                at = pl.ds(pl.multiple_of(shard_at(own, dc, dx, d) * rows, 16), rows)
                if kind == "rows":
                    spot[at, :] = refs[2 * dc + dx][d, lead, :rows]
                else:
                    for dy in range(2):
                        spot[at, half_at(dy, refs[0].shape[-1])] = refs[dc][2 * dy + dx, d, lead]


def store_grad(place, spot, keep, send, lead=0):
    own = place.own()
    rows, width = keep.shape[-2:]
    for dc, ref in enumerate((keep, send)):
        for dx in range(2):
            for d in range(FAR):
                at = pl.ds(pl.multiple_of(shard_at(own, dc, dx, d) * rows, 16), rows)
                if len(keep.shape) == 5:
                    ref[dx, d, lead] = spot[at, :]
                else:
                    for dy in range(2):
                        ref[dy, dx, d, lead] = spot[at, half_at(dy, width)]


def norm_stats(v):
    mean = jnp.mean(v, axis=-1, keepdims=True)
    centred = v - mean
    spread = jnp.mean(centred * centred, axis=-1, keepdims=True)
    scale = lax.rsqrt(spread + 1e-06)
    return centred * scale, scale


def norm_back(up, xhat, scale, gain):
    e = up * gain
    return (e - jnp.mean(e, axis=-1, keepdims=True) - xhat * jnp.mean(e * xhat, axis=-1, keepdims=True)) * scale


ERF_P = 0.3275911 / math.sqrt(2.0)
ERF_A = (0.254829592, -0.284496736, 1.421413741, -1.453152027, 1.061405429)


def gelu_and_slope(z):
    t = 1.0 / (1.0 + ERF_P * jnp.abs(z))
    e = jnp.exp(-0.5 * (z * z))
    poly = 0.5 * ERF_A[4]
    for a in ERF_A[3::-1]:
        poly = poly * t + 0.5 * a
    q = poly * t * e
    phi = jnp.where(z > 0, 1.0 - q, q)
    return z * phi, phi + z * (e * (1.0 / math.sqrt(2.0 * math.pi)))


class Rows:
    def __init__(self, images, patches):
        self.images = images
        self.patches = patches
        self.pad = -(-patches // 16) * 16
        self.all = images * self.pad
        self.raw = images * patches

    def block(self, width, count=1):
        return pl.BlockSpec((self.pad * count, width), lambda j: (j, 0))


def flag_column(rows, flags):
    wide = flags[...].astype(F32)
    wide = jnp.concatenate([wide, jnp.zeros((8 - rows.images, rows.patches), F32)], axis=0)
    gap = -rows.patches % 128
    return jnp.concatenate([wide, jnp.zeros((8, gap), F32)], axis=1).T


def padded_image(rows, ref, i):
    lo = rows.patches * i
    first = lo // 16 * 16
    last = min(-(-(lo + rows.patches) // 16) * 16, rows.raw)
    part = ref[first:last, :].astype(F32)[lo - first : lo - first + rows.patches]
    return jnp.concatenate([part, jnp.zeros((rows.pad - rows.patches, ref.shape[1]), F32)], axis=0)


def pad_kernel(rows, tokens, grads, base_o, grad_o):
    j = pl.program_id(0)

    def image(i):
        base_o[...] = padded_image(rows, tokens, i).astype(BF16)
        grad_o[...] = padded_image(rows, grads, i).astype(BF16)

    for i in range(rows.images):
        pl.when(j == i)(functools.partial(image, i))


def norm_one_kernel(rows, tokens, flags, vec, base_o, norm_o):
    cols = flag_column(rows, flags)
    row = lax.broadcasted_iota(jnp.int32, (rows.pad, 1), 0)
    for i in range(rows.images):
        at = pl.ds(i * rows.pad, rows.pad)
        masked = jnp.logical_and(cols[: rows.pad, i : i + 1] > 0.5, row < rows.patches)
        base = jnp.where(masked, vec[0:1, :], tokens[at, :].astype(F32))
        base_o[at, :] = base.astype(BF16)
        xhat, _ = norm_stats(base)
        norm_o[at, :] = (xhat * vec[1:2, :] + vec[2:3, :]).astype(BF16)


def whole(shape):
    return pl.BlockSpec(shape, lambda *j: (0,) * len(shape))


def params():
    return pltpu.CompilerParams(vmem_limit_bytes=VMEM)


def cost(flops, count):
    return pl.CostEstimate(flops=int(flops) // 100, bytes_accessed=int(count) // 100, transcendentals=0)


def pad_call(rows, tokens, grads):
    width = tokens.shape[1]
    out = jax.ShapeDtypeStruct((rows.all, width), BF16)
    return pl.pallas_call(
        functools.partial(pad_kernel, rows),
        grid=(rows.images,),
        in_specs=[whole(tokens.shape), whole(grads.shape)],
        out_specs=[rows.block(width)] * 2,
        out_shape=[out, out],
        compiler_params=params(),
        cost_estimate=cost(4e9, 9e6),
        name="pad_rows",
    )(tokens, grads)


def norm_one_call(rows, tokens, flags, vec):
    out = jax.ShapeDtypeStruct(tokens.shape, BF16)
    return pl.pallas_call(
        functools.partial(norm_one_kernel, rows),
        out_shape=[out, out],
        compiler_params=params(),
        cost_estimate=cost(4e9, 9e6),
        name="norm_one",
    )(tokens, flags, vec)


def pack_kernel(count, quarter, *refs):
    *vectors, wide, qkv, proj, up, down = refs[: -2 - quarter // 2]
    first_o, second_o, *ff_o = refs[-2 - quarter // 2 :]
    r, width = proj.shape

    def group(g):
        return [qkv[:, i * width + g * GROUP : i * width + (g + 1) * GROUP] for i in range(3)]

    for i, part in enumerate(group(0)):
        first_o[0, :r, i * GROUP : (i + 1) * GROUP] = part
    small = [v[...].astype(F32) for v in vectors]
    small += [wide[:, r * i : r * (i + 1)].astype(F32) for i in range(quarter)]
    small = jnp.concatenate(small + [jnp.zeros((16 - len(small), r), F32)], axis=0)
    first_o[0, r:, :] = jnp.concatenate([small, jnp.zeros((16, width - r), F32)], axis=1).astype(BF16)
    for g in (1, 2):
        for i, part in enumerate(group(g)):
            second_o[g - 1, :, i * GROUP : (i + 1) * GROUP] = part
    second_o[2] = proj[...]
    for t in range(quarter):
        out = ff_o[t // 2]
        cols = [up[:, (k * quarter + t) * r : (k * quarter + t + 1) * r] for k in range(count)]
        out[t % 2 * 2] = jnp.concatenate(cols, axis=1)
        out[t % 2 * 2 + 1] = down[t * r : (t + 1) * r, :]


def pack_call(count, vectors, wide, qkv, proj, up, down):
    r, width = proj.shape
    quarter = up.shape[1] // width
    shapes = [(1, r + 16, width), (3, r, width)] + [(4, r, width)] * (quarter // 2)
    return pl.pallas_call(
        functools.partial(pack_kernel, count, quarter),
        out_shape=[jax.ShapeDtypeStruct(shape, BF16) for shape in shapes],
        compiler_params=params(),
        cost_estimate=cost(1e6, 1e5),
        name="pack",
    )(*[v[None] for v in vectors], wide[None], qkv, proj, up, down)


def unpack_kernel(count, quarter, first_mine, first_twin, *refs):
    later, (qkv_o, proj_o, up_o, down_o) = refs[:6], refs[6:]
    r, half = later[0].shape[1:]
    width = 2 * half

    def joined(k):
        mine, twin = later[2 * k], later[2 * k + 1]
        out = []
        for b in range(mine.shape[0]):
            a, t = mine[b].astype(F32), twin[b].astype(F32)
            here = jnp.concatenate([a, t], axis=1)
            there = jnp.concatenate([t, a], axis=1)
            out.append(jnp.where(lax.axis_index("rep") == 0, here, there))
        return out

    ff = [first_mine[b].astype(F32) + first_twin[b].astype(F32) for b in range(4)] + joined(0)
    heads = joined(1) + joined(2)
    proj_o[...] = heads[0]
    for g in range(3):
        for i in range(3):
            qkv_o[:, i * width + g * GROUP : i * width + (g + 1) * GROUP] = heads[1 + g][:, i * GROUP : (i + 1) * GROUP]
    ups = [ff[2 * t] for t in range(quarter)]
    up_o[...] = jnp.concatenate([ups[t][:, k * r : (k + 1) * r] for k in range(count) for t in range(quarter)], axis=1)
    for t in range(quarter):
        down_o[t * r : (t + 1) * r, :] = ff[2 * t + 1]


def unpack_call(count, quarter, first, later):
    r, width = first[0].shape[1:]
    shapes = [(r, 3 * width), (r, width), (r, quarter * width), (quarter * r, width)]
    return pl.pallas_call(
        functools.partial(unpack_kernel, count, quarter),
        out_shape=[jax.ShapeDtypeStruct(shape, F32) for shape in shapes],
        compiler_params=params(),
        cost_estimate=cost(1e6, 1e5),
        name="unpack",
    )(*first, *later)


def halves(x, first):
    zero = jnp.zeros_like(x)
    return jnp.concatenate([jnp.where(first, x, zero), jnp.where(first, zero, x)], axis=0)


def attend_kernel(place, kind, nw, before, rows, base_group, norm, vec, *refs):
    w_in, (q_o, k_o, v_o, att_o, p_o, w_o) = refs[:nw], refs[nw + before :]
    j = pl.program_id(0)
    w = w_o.at[0]
    if kind == "whole":
        w[...] = w_in[0][0]
    else:
        load_weight(place, kind, norm.shape[1] // place.count, w_in, w)
    x = norm[...]
    lanes = pl.ds(pl.multiple_of((base_group + j) * GROUP, GROUP), GROUP)
    q_o[0] = ((dot(x, w[:, 0:GROUP]) + vec[3:4, lanes]).astype(BF16) * 0.125).astype(BF16)
    k_o[0] = dot(x, w[:, GROUP : 2 * GROUP]).astype(BF16)
    v_o[0] = (dot(x, w[:, 2 * GROUP :]) + vec[4:5, lanes]).astype(BF16)
    s = rows.pad
    first = lax.broadcasted_iota(jnp.int32, (s, 128), 1) < HEAD
    live = lax.broadcasted_iota(jnp.int32, (s, 2 * s), 0) < rows.patches

    def image(i):
        at = pl.ds(pl.multiple_of(i * s, 16), s)
        for p in range(2):
            cols = pl.ds(128 * p, 128)
            q, k, v = q_o[0, at, cols], k_o[0, at, cols], v_o[0, at, cols]
            score = jnp.where(live, dot_cols(k, halves(q, first)), NEG)
            peak = jnp.max(score, axis=0, keepdims=True)
            e = jnp.exp(score - peak)
            probs = (e * (1.0 / jnp.sum(e, axis=0, keepdims=True))).astype(BF16)
            p_o[0, p, i] = probs
            o = dot_rows(probs, v)
            att_o[0, at, cols] = jnp.where(first, o[:s], o[s:]).astype(BF16)

    def step(i, carry):
        for u in range(3):
            image(i * 3 + u)
        return carry

    lax.fori_loop(0, rows.images // 3, step, 0)


def piece_specs(weight, blocks=1, first=0):
    if weight.kind == "whole":
        return [pl.BlockSpec((blocks, *weight.arrays[0].shape[1:]), lambda j: (first + j, 0, 0))]
    if weight.kind == "rows":
        z, _, r, w = weight.arrays[0].shape
        return [pl.BlockSpec((z, blocks, r, w), lambda j: (0, first + j, 0, 0))] * 4
    k, z, _, r, w = weight.arrays[0].shape
    return [pl.BlockSpec((k, z, blocks, r, w), lambda j: (0, 0, first + j, 0, 0))] * 2


def attend_call(place, rows, group, groups, norm, vec, weight, before=()):
    s = rows.pad
    width = norm.shape[1]
    row = pl.BlockSpec((1, rows.all, GROUP), lambda j: (group + j, 0, 0))
    out = jax.ShapeDtypeStruct((3, rows.all, GROUP), BF16)
    outs = [out] * 4 + [jax.ShapeDtypeStruct((3, 2, rows.images, s, 2 * s), BF16)]
    specs = [row] * 4 + [pl.BlockSpec((1, 2, rows.images, s, 2 * s), lambda j: (group + j, 0, 0, 0, 0))]
    outs.append(jax.ShapeDtypeStruct((3, width, 3 * GROUP), BF16))
    specs.append(pl.BlockSpec((1, width, 3 * GROUP), lambda j: (group + j, 0, 0)))
    args = [norm, vec, *weight.arrays, *before]
    first = len(args) - len(before)
    return pl.pallas_call(
        functools.partial(attend_kernel, place, weight.kind, len(weight.arrays), len(before), rows, group),
        grid=(groups,),
        in_specs=[whole(norm.shape), whole(vec.shape)]
        + piece_specs(weight)
        + [pl.BlockSpec(memory_space=pl.ANY)] * len(before),
        out_specs=specs,
        out_shape=outs,
        input_output_aliases={first + i: i for i in range(len(before))},
        compiler_params=params(),
        cost_estimate=cost(groups * 6e9, groups * 8e6),
        name="attend",
    )(*args)


def project_kernel(place, kind, nw, spot, vec, base, att, *refs):
    w_in, (resid_o, norm_o, w_o) = refs[:nw], refs[nw:]

    @pl.when(pl.program_id(0) == 0)
    def _():
        if kind == "whole":
            w_o[0] = w_in[0][0]
        else:
            load_weight(place, kind, base.shape[1] // place.count, w_in, w_o.at[0])

    both = jnp.concatenate([att[g] for g in range(att.shape[0])], axis=1)
    total = dot(both, w_o[0]) + base[...].astype(F32) + vec[5:6, :]
    resid_o[...] = total
    xhat, _ = norm_stats(total)
    norm_o[...] = (xhat * vec[6:7, :] + vec[7:8, :]).astype(BF16)


def project_call(place, rows, vec, base, att, weight, spot):
    width = base.shape[1]
    outs = [
        jax.ShapeDtypeStruct((rows.all, width), F32),
        jax.ShapeDtypeStruct((rows.all, width), BF16),
        jax.ShapeDtypeStruct((1, width, width), BF16),
    ]
    some = rows.images // 3
    pieces = [
        pl.BlockSpec(block.block_shape, lambda j, at=block.index_map(0): at)
        for block in piece_specs(weight, 1, spot)
    ]
    return pl.pallas_call(
        functools.partial(project_kernel, place, weight.kind, len(weight.arrays), spot),
        grid=(3,),
        in_specs=[whole(vec.shape), rows.block(width, some)]
        + [pl.BlockSpec((3, rows.pad * some, GROUP), lambda j: (0, j, 0))]
        + pieces,
        out_specs=[rows.block(width, some)] * 2 + [whole(outs[2].shape)],
        out_shape=outs,
        compiler_params=params(),
        cost_estimate=cost(3e9, 12e6),
        name="project",
    )(vec, base, att, *weight.arrays)


def feed_kernel(place, kind, form, nw, rows, block, carried, norm, grad, vec, *refs):
    w_in, rest = refs[:nw], refs[nw:]
    if carried:
        (acc_in, gn_in), rest = rest[:2], rest[2:]
    acc_o, gn_o, bias_o = rest[:3]
    j = pl.program_id(0)
    grads_o, rest = rest[3 : 3 + (1 if form == "whole" else 2)], rest[3 + (1 if form == "whole" else 2) :]
    act_s, gp_s, g_s = rest[:3]
    if kind == "whole":
        w_up, w_down = w_in[0].at[0], w_in[0].at[1]
    else:
        w_up, w_down = rest[3:]
        r = norm.shape[1] // place.count
        load_weight(place, kind, r, w_in, w_up, 0)
        load_weight(place, kind, r, w_in, w_down, 1)

    @pl.when(j == 0)
    def _():
        if carried:
            acc_o[...] = acc_in[...]
            gn_o[...] = gn_in[...]
        else:
            acc_o[...] = jnp.zeros_like(acc_o)
            gn_o[...] = jnp.zeros_like(gn_o)

    bias = vec[pl.ds(9 + block + j, 1), :]
    step = rows.pad
    for b in range(rows.images):
        at = pl.ds(b * step, step)
        z = dot(norm[at, :], w_up[...]) + bias
        up = dot_cols(grad[at, :], w_down[...])
        act, slope = gelu_and_slope(z)
        act = act.astype(BF16)
        gp = (up * slope).astype(BF16)
        act_s[at, :] = act
        gp_s[at, :] = gp
        acc_o[at, :] += dot(act, w_down[...])
        gn_o[at, :] += dot_cols(gp, w_up[...])
    bias_o[0] = jnp.sum(gp_s[...].astype(F32), axis=0, keepdims=True)
    for i, (left, right) in enumerate(((norm, gp_s), (act_s, grad))):
        value = dot_rows(left[...], right[...]).astype(BF16)
        if form == "whole":
            grads_o[0][i] = value
        else:
            g_s[...] = value
            store_grad(place, g_s, *grads_o, i)


def grad_out(kind, blocks, width, r, per_step):
    if kind == "whole":
        return (
            [jax.ShapeDtypeStruct((blocks, width, width), BF16)],
            [pl.BlockSpec((per_step, width, width), lambda j: (j, 0, 0))],
        )
    if kind == "few":
        lead, w = (2, FAR), width
    else:
        lead, w = (2, 2, FAR), width // 2
    zero = (0,) * len(lead)
    return (
        [jax.ShapeDtypeStruct((*lead, blocks, r, w), BF16)] * 2,
        [pl.BlockSpec((*lead, per_step, r, w), lambda j: (*zero, j, 0, 0))] * 2,
    )


def feed_call(place, rows, block, blocks, norm, grad, vec, weight, form, r, carried):
    width = norm.shape[1]
    acc = jax.ShapeDtypeStruct((rows.all, width), F32)
    outs, specs = grad_out(form, 2 * blocks, width, r, 2)
    scratch = [pltpu.VMEM((rows.all, width), BF16)] * 2 + [pltpu.VMEM((width, width), BF16)]
    if weight.kind != "whole":
        scratch = scratch + [pltpu.VMEM((width, width), BF16)] * 2
    args = [norm, grad, vec, *weight.arrays, *carried]
    in_specs = [whole(norm.shape), whole(grad.shape), whole(vec.shape)] + piece_specs(weight, 2)
    in_specs += [whole(acc.shape)] * len(carried)
    return pl.pallas_call(
        functools.partial(feed_kernel, place, weight.kind, form, len(weight.arrays), rows, block, bool(carried)),
        grid=(blocks,),
        in_specs=in_specs,
        out_specs=[whole(acc.shape)] * 2 + [pl.BlockSpec((1, 1, width), lambda j: (j, 0, 0))] + specs,
        out_shape=[acc, acc, jax.ShapeDtypeStruct((blocks, 1, width), F32)] + outs,
        scratch_shapes=scratch,
        compiler_params=params(),
        cost_estimate=cost(blocks * 1.2e10, blocks * 20e6),
        name="feed",
    )(*args)


def middle_kernel(rows, resid, acc, gn, grad, vec, w, out_o, low_o, da_o, sums_o):
    xhat, scale = norm_stats(resid[...])
    gain = vec[6:7, :]
    up = gn[...]
    g = grad[...].astype(F32)
    total = g + norm_back(up, xhat, scale, gain)
    lowered = total.astype(BF16)
    low_o[...] = lowered
    da_o[...] = dot_cols(lowered, w[0]).astype(BF16)
    sums = jnp.concatenate(
        [
            jnp.sum(total, axis=0, keepdims=True),
            jnp.sum(up * xhat, axis=0, keepdims=True),
            jnp.sum(up, axis=0, keepdims=True),
            jnp.sum(g, axis=0, keepdims=True),
        ],
        axis=0,
    )
    final = resid[...] + acc[...] + vec[8:9, :]
    j = pl.program_id(0)
    for i in range(rows.images):

        @pl.when(j == i)
        def _():
            sums_o[...] = sums if i == 0 else sums_o[...] + sums
            out_o[rows.patches * i : rows.patches * (i + 1), :] = final[: rows.patches]


def middle_call(rows, resid, acc, gn, grad, vec, weight):
    width = resid.shape[1]
    block = rows.block(width)
    outs = [
        jax.ShapeDtypeStruct((rows.raw, width), BF16),
        jax.ShapeDtypeStruct((rows.all, width), BF16),
        jax.ShapeDtypeStruct((rows.all, width), BF16),
        jax.ShapeDtypeStruct((4, width), F32),
    ]

    def kernel(resid, acc, gn, grad, vec, w, out_o, low_o, da_o, sums_o, out_s):
        middle_kernel(rows, resid, acc, gn, grad, vec, w, out_s, low_o, da_o, sums_o)

        @pl.when(pl.program_id(0) == rows.images - 1)
        def _():
            out_o[...] = out_s[...].astype(BF16)

    return pl.pallas_call(
        kernel,
        grid=(rows.images,),
        in_specs=[block] * 4 + [whole(vec.shape), whole(weight.shape)],
        out_specs=[whole(outs[0].shape), block, block, whole(outs[3].shape)],
        out_shape=outs,
        scratch_shapes=[pltpu.VMEM((rows.raw, width), F32)],
        compiler_params=params(),
        cost_estimate=cost(4e9, 20e6),
        name="middle",
    )(resid, acc, gn, grad, vec, weight)


STEP = 3


def attend_back_kernel(place, kind, rows, projects, norm, da, *refs):
    g, j = pl.program_id(0), pl.program_id(1)
    q_i, k_i, v_i, p_i, refs = *refs[:4], refs[4:]
    if projects:
        (lowered, *atts), refs = refs[: 1 + projects], refs[1 + projects :]
    d_o, bias_o = refs[:2]
    if kind == "whole":
        (grads_o,) = refs[2:]
    else:
        keep, send, g_s = refs[2:]
    s = rows.pad
    some = rows.images // STEP
    first = lax.broadcasted_iota(jnp.int32, (s, 128), 1) < HEAD

    def emit(value, spot):
        if kind == "whole":
            grads_o[spot] = value.astype(BF16)
        else:
            g_s[...] = value.astype(BF16)
            store_grad(place, g_s, keep, send, spot)

    for i in range(some):
        at = pl.ds(i * s, s)
        to = pl.ds(pl.multiple_of((j * some + i) * s, 16), s)
        for p in range(2):
            cols = pl.ds(128 * p, 128)
            q, k, v = q_i[0, at, cols], k_i[0, at, cols], v_i[0, at, cols]
            q2, da2 = halves(q, first), halves(da[at, cols], first)
            low_probs = p_i[0, p, i]
            d_o[0, to, pl.ds(2 * GROUP + 128 * p, 128)] = dot(low_probs, da2).astype(BF16)
            up = dot_cols(v, da2)
            probs = low_probs.astype(F32)
            inner = jnp.sum(probs * up, axis=0, keepdims=True)
            ds = (probs * (up - inner)).astype(BF16)
            d_o[0, to, pl.ds(GROUP + 128 * p, 128)] = dot(ds, q2).astype(BF16)
            dq = dot_rows(ds, k)
            d_o[0, to, cols] = (jnp.where(first, dq[:s], dq[s:]) * 0.125).astype(BF16)

    @pl.when(j == STEP - 1)
    def _():
        if projects:

            @pl.when(g == 0)
            def _():
                both = jnp.concatenate([a[b] for a in atts for b in range(a.shape[0])], axis=1)
                emit(dot_rows(both, lowered[...]), 0)

        bias_o[0] = jnp.sum(d_o[0].astype(F32), axis=0, keepdims=True)
        emit(dot_rows(norm[...], d_o[0]), g + (1 if projects else 0))


def attend_back_call(place, rows, group, groups, norm, q, k, v, probs, da, r, shape="few", project=()):
    width = norm.shape[1]
    s = rows.pad
    some = rows.images // STEP
    row = pl.BlockSpec((1, s * some, GROUP), lambda g, j: (group + g, j, 0))
    in_specs = [whole(norm.shape), pl.BlockSpec((s * some, GROUP), lambda g, j: (j, group + g)), row, row, row]
    in_specs += [pl.BlockSpec((1, 2, some, s, 2 * s), lambda g, j: (group + g, 0, j, 0, 0))]
    in_specs += [whole(a.shape) for a in project]
    kind = shape if place else "whole"
    outs, specs = grad_out(kind, groups + (1 if project else 0), width, r, 1)
    specs = [whole(out.shape) for out in outs]
    return pl.pallas_call(
        functools.partial(attend_back_kernel, place, kind, rows, max(len(project) - 1, 0)),
        grid=(groups, STEP),
        in_specs=in_specs,
        out_specs=[
            pl.BlockSpec((1, rows.all, width), lambda g, j: (g, 0, 0)),
            pl.BlockSpec((1, 1, width), lambda g, j: (g, 0, 0)),
        ]
        + specs,
        out_shape=[
            jax.ShapeDtypeStruct((groups, rows.all, width), BF16),
            jax.ShapeDtypeStruct((groups, 1, width), F32),
        ]
        + outs,
        scratch_shapes=[pltpu.VMEM((width, width), BF16)] if place else [],
        compiler_params=params(),
        cost_estimate=cost(8e9 * groups, 12e6 * groups),
        name="attend_back",
    )(norm, da, q, k, v, probs, *project)


def last_kernel(rows, counts, base, low, flags, vec, w, *refs):
    dqkv, (out_o, sums_o) = refs[: len(counts)], refs[len(counts) :]
    cols = flag_column(rows, flags)
    gain = vec[1:2, :]
    parts = [d[b] for d, count in zip(dqkv, counts) for b in range(count)]
    up = dot_cols(parts[0], w[0])
    for g in range(1, len(parts)):
        up = up + dot_cols(parts[g], w[g])
    xhat, scale = norm_stats(base[...].astype(F32))
    total = low[...].astype(F32) + norm_back(up, xhat, scale, gain)
    row = lax.broadcasted_iota(jnp.int32, (rows.pad, 1), 0)
    j = pl.program_id(0)
    for i in range(rows.images):

        @pl.when(j == i)
        def _():
            chosen = jnp.logical_and(cols[: rows.pad, i : i + 1] > 0.5, row < rows.patches)
            sums = jnp.concatenate(
                [
                    jnp.sum(jnp.where(chosen, total, 0.0), axis=0, keepdims=True),
                    jnp.sum(up * xhat, axis=0, keepdims=True),
                    jnp.sum(up, axis=0, keepdims=True),
                ],
                axis=0,
            )
            sums_o[...] = sums if i == 0 else sums_o[...] + sums
            out_o[rows.patches * i : rows.patches * (i + 1), :] = jnp.where(chosen, 0.0, total)[: rows.patches]


def last_call(rows, base, low, flags, vec, w, dqkv):
    width = base.shape[1]
    block = rows.block(width)
    outs = [jax.ShapeDtypeStruct((rows.raw, width), F32), jax.ShapeDtypeStruct((3, width), F32)]
    return pl.pallas_call(
        functools.partial(last_kernel, rows, [d.shape[0] for d in dqkv]),
        grid=(rows.images,),
        in_specs=[block, block, whole(flags.shape), whole(vec.shape), whole(w.shape)]
        + [pl.BlockSpec((d.shape[0], rows.pad, width), lambda j: (0, j, 0)) for d in dqkv],
        out_specs=[whole(out.shape) for out in outs],
        out_shape=outs,
        compiler_params=params(),
        cost_estimate=cost(4e9, 14e6),
        name="last",
    )(base, low, flags, vec, w, *dqkv)


def local(
    count,
    tokens,
    mask_flags,
    mask_token,
    norm1_gain,
    norm1_bias,
    qkv_weight,
    query_bias,
    value_bias,
    proj_weight,
    proj_bias,
    norm2_gain,
    norm2_bias,
    fc1_weight,
    fc1_bias,
    fc2_weight,
    fc2_bias,
    out_grad,
):
    images, patches = mask_flags.shape
    rows = Rows(images, patches)
    r, width = proj_weight.shape
    place = Place(count) if r % 16 == 0 and count == 4 * FAR else None
    quarter = fc1_weight.shape[1] // width

    half = quarter // 2
    vectors = (mask_token, norm1_gain, norm1_bias, query_bias, value_bias, proj_bias, norm2_gain, norm2_bias, fc2_bias)
    kinds = len(vectors) + quarter

    def whole_gather(stack):
        return Weight("whole", [lax.all_gather(stack, "fsdp", axis=1, tiled=True)])

    def whole_scatter(sums):
        share = lax.psum_scatter(sums if place else sums.astype(F32), "fsdp", scatter_dimension=1, tiled=True)
        return share if place else lax.psum(share, "rep")

    flow = Flow()
    pad_in = (tokens, out_grad)
    if place:
        z, x, c = place.own()
        first, second, ff_0, ff_1 = pack_call(count, vectors, fc1_bias, qkv_weight, proj_weight, fc1_weight, fc2_weight)
        flow.begin("wa", gather_fast(place, first))
        pad_in = flow.send(*pad_in)
    else:
        qkv_blocks = qkv_weight.reshape(r, 3, 3, GROUP).transpose(2, 0, 1, 3).reshape(3, r, 3 * GROUP)
        up_blocks = fc1_weight.reshape(r, count, quarter, r).transpose(2, 0, 1, 3).reshape(quarter, r, width)
        down_blocks = fc2_weight.reshape(quarter, r, width)
        ff = jnp.stack([up_blocks, down_blocks], axis=1).reshape(2 * quarter, r, width)
        w_a, w_b = whole_gather(qkv_blocks[:1]), whole_gather(jnp.concatenate([qkv_blocks[1:], proj_weight[None]]))
        w_f0, w_f1 = whole_gather(ff[: 2 * half]), whole_gather(ff[2 * half :])
        small = jnp.concatenate([v[None] for v in vectors] + [fc1_bias.reshape(quarter, r)])
        came = lax.all_gather(small, "fsdp", axis=1, tiled=True)
        came = jnp.pad(came, ((0, 16 - kinds), (0, 0)))
    base, grad = pad_call(rows, *pad_in)
    if place:
        (base,) = flow.meet(["wa"], base)
        flow.begin("wb", gather_wide(place, second))
        (base,) = flow.send(base)
        (base,) = flow.meet(["wa"], base)
        (base,) = flow.send(base)
        (base,) = flow.meet(["wa"], base)
        w_a = flow.done["wa"]
        came = jnp.stack([part[:, 0, r:, :r] for part in w_a.arrays]).reshape(2, 2, FAR, -1, r)
        came = jnp.where(c == 0, came, came[::-1])
        came = jnp.where(x == 0, came, came[:, ::-1])
        came = jnp.where(z % 2 == 0, came, came.reshape(2, 2, 2, 2, -1, r)[:, :, :, ::-1].reshape(came.shape))
        came = jnp.where(z < 2, came, came.reshape(2, 2, 2, 2, -1, r)[:, :, ::-1].reshape(came.shape))
        came = came.transpose(3, 2, 1, 0, 4)
    vec = came.reshape(16, width).astype(F32)

    base, norm = norm_one_call(rows, base, mask_flags, vec)
    if place:
        (norm,) = flow.meet(["wb"], norm)
        flow.begin("wf0", gather_even(place, ff_0))
        (norm,) = flow.send(norm)
    attends = attend_call(place, rows, 0, 1, norm, vec, w_a)
    if place:
        norm, *attends = flow.turn(["wb", "wf0"], norm, *attends)
        norm, ff_1, *attends = flow.meet(["wb"], norm, ff_1, *attends)
        w_b = flow.done["wb"]
        w_f1 = whole_gather(ff_1)
    q, k, v, att, probs, wqkv = attend_call(place, rows, 1, 2, norm, vec, w_b, attends)
    if place:
        (att,) = flow.turn(["wf0"], att)
    resid, norm_two, w_proj = project_call(place, rows, vec, base, att, w_b, 2)
    if place:
        (norm_two,) = flow.turn(["wf0"], norm_two)
        (norm_two,) = flow.meet(["wf0"], norm_two)
        w_f0 = flow.done["wf0"]

    acc, gn, gb_0, *f0 = feed_call(place, rows, 0, half, norm_two, grad, vec, w_f0, "whole", r, ())
    f0 = whole_scatter(f0[0])
    form = "wide" if place else "whole"
    acc, gn, gb_1, *f1 = feed_call(place, rows, half, half, norm_two, grad, vec, w_f1, form, r, (acc, gn))
    if place:
        flow.begin("f1", scatter_early_y(place, *f1))
        acc, gn = flow.send(acc, gn)
    else:
        f1 = whole_scatter(f1[0])

    block_out, lowered, da, sums_two = middle_call(rows, resid, acc, gn, grad, vec, w_proj)
    if place:
        (da,) = flow.turn(["f1"], da)
    dq_0, qs_0, *sums_c = attend_back_call(
        place, rows, 0, 2, norm, q, k, v, probs, da, r, form, project=[lowered, att]
    )
    if place:
        flow.begin("c", scatter_wide(place, *sums_c))
        dq_0, norm, f0 = flow.meet(["f1"], dq_0, norm, f0)
        flow.begin("f0", send_twin(place, f0))
        dq_0, norm = flow.send(dq_0, norm)
    dq_1, qs_1, *sums_d = attend_back_call(place, rows, 2, 1, norm, q, k, v, probs, da, r, form)
    if place:
        flow.begin("d", scatter_wide(place, *sums_d))
        (dq_1,) = flow.turn(["c", "f1", "f0"], dq_1)
    input_grad, sums_one = last_call(rows, base, lowered, mask_flags, vec, wqkv, [dq_0, dq_1])

    qkv_sums = jnp.concatenate([qs_0, qs_1], axis=0)[:, 0]
    late = jnp.concatenate(
        [
            sums_one,
            qkv_sums[:, :GROUP].reshape(1, width),
            qkv_sums[:, 2 * GROUP :].reshape(1, width),
            sums_two,
            gb_0[:, 0],
            gb_1[:, 0],
        ],
        axis=0,
    )
    late = late.reshape(kinds, count, r).transpose(1, 0, 2)
    if place:
        late = jnp.pad(late, ((0, 0), (0, -kinds % 8), (0, 0)))
        late, input_grad = flow.turn(["d"], late, input_grad)
        late = lax.all_to_all(jnp.concatenate([late, late]), ("rep", "fsdp"), 0, 0, tiled=True)
        (late,) = flow.meet(["c", "f1"], late)
        flow.begin("f1y", send_twin(place, flow.done["f1"]))
        (late,) = flow.send(late)
        (late,) = flow.turn(["d"], late)
        (late,) = flow.meet(["c"], late)
        flow.begin("cy", send_twin(place, flow.done["c"]))
        (late,) = flow.send(late)
        (late,) = flow.meet(["d", "f1y"], late)
        flow.begin("dy", send_twin(place, flow.done["d"]))
        (late,) = flow.send(late)
        (late,) = flow.meet(["cy", "dy"], late)
        shares = late.sum(axis=0)
        f0, f1, sums_c, sums_d = [flow.done[name] for name in ("f0", "f1y", "cy", "dy")]
        later = [side[0] for pair in (f1, sums_c, sums_d) for side in pair]
        g_qkv, g_proj, g_up, g_down = unpack_call(count, quarter, [side[0] for side in f0], later)
    else:
        shares = lax.psum(lax.psum_scatter(late, "fsdp", scatter_dimension=0, tiled=True), "rep")[0]
        sums_c = jnp.concatenate([whole_scatter(sums_c[0]), whole_scatter(sums_d[0])])
        g_proj = sums_c[0]
        g_qkv = sums_c[1:].reshape(3, r, 3, GROUP).transpose(1, 2, 0, 3).reshape(r, 3 * width)
        g_ff = jnp.concatenate([f0, f1], axis=0).reshape(quarter, 2, r, width)
        g_up = g_ff[:, 0].reshape(quarter, r, count, r).transpose(1, 2, 0, 3).reshape(r, quarter * width)
        g_down = g_ff[:, 1].reshape(quarter * r, width)
    token_s, gain1_s, shift1_s, qb_s, vb_s, pb_s, gain2_s, shift2_s, db_s = [shares[i] for i in range(9)]
    ub_s = shares[9:kinds].reshape(-1)
    return (
        block_out,
        input_grad,
        token_s,
        gain1_s,
        shift1_s,
        g_qkv,
        qb_s,
        vb_s,
        g_proj,
        pb_s,
        gain2_s,
        shift2_s,
        g_up,
        ub_s,
        g_down,
        db_s,
    )


def solution(mesh):
    both, one = P(("rep", "fsdp"), None), P("fsdp")
    flat = P("fsdp", None)
    in_specs = (both, both, one, one, one, flat, one, one, flat, one, one, one, flat, one, flat, one, both)
    out_specs = (both, both, one, one, one, flat, one, one, flat, one, one, one, flat, one, flat, one)
    return jax.shard_map(
        functools.partial(local, mesh.shape["fsdp"]),
        mesh=mesh,
        in_specs=in_specs,
        out_specs=out_specs,
        check_vma=False,
    )
```

```python
import functools
import math

import jax
import jax.numpy as jnp
from jax import lax
from jax.experimental import pallas as pl
from jax.experimental.pallas import tpu as pltpu
from jax.sharding import PartitionSpec as P

F32 = jnp.float32
BF16 = jnp.bfloat16
HEAD = 64
GROUP = 256
NEG = -1e30
VMEM = 56 * 2**20


def dot(a, b):
    return lax.dot_general(a, b, (((1,), (0,)), ((), ())), preferred_element_type=F32)


def dot_rows(a, b):
    return lax.dot_general(a, b, (((0,), (0,)), ((), ())), preferred_element_type=F32)


def dot_cols(a, b):
    return lax.dot_general(a, b, (((1,), (1,)), ((), ())), preferred_element_type=F32)


FAR = 4


class Place:
    def __init__(self, count):
        self.count = count

    def own(self):
        index = lax.axis_index("fsdp")
        return index // 4, (index // 2) % 2, index % 2

    def swap(self, bits):
        return [(i, i ^ bits) for i in range(self.count)]

    def core(self, v):
        return lax.ppermute(v, "fsdp", self.swap(1))

    def along_x(self, v):
        return lax.ppermute(v, "fsdp", self.swap(2))

    def along_z(self, d):
        return lambda v: lax.ppermute(v, "fsdp", self.swap(4 * d))

    def along_y(self, v):
        return lax.ppermute(v, "rep", [(0, 1), (1, 0)])

    def along_xy(self, v):
        n = self.count
        return lax.ppermute(
            v, ("rep", "fsdp"), [(y * n + i, (1 - y) * n + (i ^ 2)) for y in range(2) for i in range(n)]
        )


def shard_at(own, dc, dx, dz):
    z, x, c = own
    return (lax.bitwise_xor(z, dz) * 2 + lax.bitwise_xor(x, dx)) * 2 + lax.bitwise_xor(c, dc)


def add_low(*terms):
    total = terms[0].astype(F32)
    for term in terms[1:]:
        total = total + term.astype(F32)
    return total


def low(v):
    return v.astype(BF16)


def by_side(side, first, second, axis):
    return jnp.where(side == 0, jnp.concatenate([first, second], axis), jnp.concatenate([second, first], axis))


class Weight:
    def __init__(self, kind, arrays):
        self.kind = kind
        self.arrays = arrays


def gather_fast(place, stack):
    came = yield [(place.along_z(d), stack) for d in range(1, FAR)]
    own = jnp.stack([stack] + came)
    beside, own_core = yield [(place.along_x, own), (place.core, own)]
    (beside_core,) = yield [(place.core, beside)]
    return Weight("rows", [own, beside, own_core, beside_core])


def half_columns(stack):
    half = stack.shape[2] // 2
    return lax.dynamic_slice_in_dim(stack, lax.axis_index("rep") * half, half, axis=2)


def gather_wide(place, stack):
    mine = half_columns(stack)
    came = yield [(place.along_z(d), mine) for d in range(1, FAR)]
    own = jnp.stack([mine] + came)
    came = yield [(place.along_x, own), (place.along_y, own), (place.along_xy, own)]
    here = jnp.stack([own] + came)
    (across,) = yield [(place.core, here)]
    return Weight("halves", [here, across])


def gather_even(place, stack):
    mine = half_columns(stack)
    came = yield [(place.along_z(d), mine) for d in range(1, FAR)]
    own = jnp.stack([mine] + came)
    beside, twin = yield [(place.along_x, own), (place.along_y, own)]
    corner = yield [(place.along_y, beside[:2]), (place.along_x, twin[2:])]
    here = jnp.stack([own, beside, twin, jnp.concatenate(corner)])
    (across,) = yield [(place.core, here)]
    return Weight("halves", [here, across])


def gather_late_y(place, stack):
    mine = half_columns(stack)
    came = yield [(place.along_z(d), mine) for d in range(1, FAR)]
    own = jnp.stack([mine] + came)
    (beside,) = yield [(place.along_x, own)]
    side = jnp.stack([own, beside])
    (twin,) = yield [(place.along_y, side)]
    here = jnp.concatenate([side, twin])
    (across,) = yield [(place.core, here)]
    return Weight("halves", [here, across])


def scatter_early_y(place, keep, send):
    (came,) = yield [(place.core, send)]
    (came_y,) = yield [(place.along_y, low(add_low(keep[1], came[1])))]
    (came_x,) = yield [(place.along_x, low(add_low(keep[0, 1], came[0, 1], came_y[1])))]
    total = low(add_low(keep[0, 0], came[0, 0], came_y[0], came_x))
    came = yield [(place.along_z(d), total[d]) for d in range(1, FAR)]
    return low(add_low(total[0], *came))


def scatter_wide(place, keep, send):
    (came,) = yield [(place.core, send)]

    def pair(dy, dx):
        return low(add_low(keep[dy, dx], came[dy, dx]))

    came_xy = yield [(place.along_x, pair(0, 1)), (place.along_y, pair(1, 0)), (place.along_xy, pair(1, 1))]
    total = low(add_low(keep[0, 0], came[0, 0], *came_xy))
    came = yield [(place.along_z(d), total[d]) for d in range(1, FAR)]
    return low(add_low(total[0], *came))


def send_twin(place, *mine):
    twins = yield [(place.along_y, v) for v in mine]
    return list(mine), twins


class Flow:
    def __init__(self):
        self.live = {}
        self.done = {}

    def begin(self, name, steps):
        self.live[name] = (steps, next(steps), None)

    def send(self, *arrays):
        waiting = [name for name, (_, pairs, sent) in self.live.items() if sent is None]
        flat = [v for name in waiting for _, v in self.live[name][1]]
        flat = list(lax.optimization_barrier(tuple(flat) + tuple(arrays)))
        for name in waiting:
            steps, pairs, _ = self.live[name]
            sent = [move(v) for (move, _), v in zip(pairs, flat)]
            flat = flat[len(pairs) :]
            self.live[name] = (steps, pairs, sent)
        return flat

    def meet(self, names, *arrays):
        names = [name for name in names if name in self.live]
        flat = [v for name in names for v in self.live[name][2]]
        flat = list(lax.optimization_barrier(tuple(flat) + tuple(arrays)))
        for name in names:
            steps, pairs, _ = self.live[name]
            mine, flat = flat[: len(pairs)], flat[len(pairs) :]
            try:
                self.live[name] = (steps, steps.send(mine), None)
            except StopIteration as stop:
                del self.live[name]
                self.done[name] = stop.value
        return flat

    def turn(self, names, *arrays):
        return self.send(*self.meet(names, *arrays))


def half_at(dy, width):
    at = lax.bitwise_xor(lax.axis_index("rep"), dy) * width
    return pl.ds(pl.multiple_of(at, 128), width)


def load_weight(place, kind, rows, refs, spot, lead=0):
    own = place.own()
    for dc in range(2):
        for dx in range(2):
            for d in range(FAR):
                at = pl.ds(pl.multiple_of(shard_at(own, dc, dx, d) * rows, 16), rows)
                if kind == "rows":
                    spot[at, :] = refs[2 * dc + dx][d, lead, :rows]
                else:
                    for dy in range(2):
                        spot[at, half_at(dy, refs[0].shape[-1])] = refs[dc][2 * dy + dx, d, lead]


def store_grad(place, spot, keep, send, lead=0):
    own = place.own()
    rows, width = keep.shape[-2:]
    for dc, ref in enumerate((keep, send)):
        for dx in range(2):
            for d in range(FAR):
                at = pl.ds(pl.multiple_of(shard_at(own, dc, dx, d) * rows, 16), rows)
                if len(keep.shape) == 5:
                    ref[dx, d, lead] = spot[at, :]
                else:
                    for dy in range(2):
                        ref[dy, dx, d, lead] = spot[at, half_at(dy, width)]


def norm_stats(v):
    mean = jnp.mean(v, axis=-1, keepdims=True)
    centred = v - mean
    spread = jnp.mean(centred * centred, axis=-1, keepdims=True)
    scale = lax.rsqrt(spread + 1e-06)
    return centred * scale, scale


def norm_back(up, xhat, scale, gain):
    e = up * gain
    return (e - jnp.mean(e, axis=-1, keepdims=True) - xhat * jnp.mean(e * xhat, axis=-1, keepdims=True)) * scale


ERF_P = 0.3275911 / math.sqrt(2.0)
ERF_A = (0.254829592, -0.284496736, 1.421413741, -1.453152027, 1.061405429)


def gelu_and_slope(z):
    t = 1.0 / (1.0 + ERF_P * jnp.abs(z))
    e = jnp.exp(-0.5 * (z * z))
    poly = 0.5 * ERF_A[4]
    for a in ERF_A[3::-1]:
        poly = poly * t + 0.5 * a
    q = poly * t * e
    phi = jnp.where(z > 0, 1.0 - q, q)
    return z * phi, phi + z * (e * (1.0 / math.sqrt(2.0 * math.pi)))


class Rows:
    def __init__(self, images, patches):
        self.images = images
        self.patches = patches
        self.pad = -(-patches // 16) * 16
        self.all = images * self.pad
        self.raw = images * patches

    def block(self, width, count=1):
        return pl.BlockSpec((self.pad * count, width), lambda j: (j, 0))


def flag_column(rows, flags):
    wide = flags[...].astype(F32)
    wide = jnp.concatenate([wide, jnp.zeros((8 - rows.images, rows.patches), F32)], axis=0)
    gap = -rows.patches % 128
    return jnp.concatenate([wide, jnp.zeros((8, gap), F32)], axis=1).T


def padded_image(rows, ref, i):
    lo = rows.patches * i
    first = lo // 16 * 16
    last = min(-(-(lo + rows.patches) // 16) * 16, rows.raw)
    part = ref[first:last, :].astype(F32)[lo - first : lo - first + rows.patches]
    return jnp.concatenate([part, jnp.zeros((rows.pad - rows.patches, ref.shape[1]), F32)], axis=0)


def pad_kernel(rows, tokens, grads, base_o, grad_o):
    j = pl.program_id(0)

    def image(i):
        base_o[...] = padded_image(rows, tokens, i).astype(BF16)
        grad_o[...] = padded_image(rows, grads, i).astype(BF16)

    for i in range(rows.images):
        pl.when(j == i)(functools.partial(image, i))


def norm_one_kernel(rows, tokens, flags, vec, base_o, norm_o):
    cols = flag_column(rows, flags)
    row = lax.broadcasted_iota(jnp.int32, (rows.pad, 1), 0)
    for i in range(rows.images):
        at = pl.ds(i * rows.pad, rows.pad)
        masked = jnp.logical_and(cols[: rows.pad, i : i + 1] > 0.5, row < rows.patches)
        base = jnp.where(masked, vec[0:1, :], tokens[at, :].astype(F32))
        base_o[at, :] = base.astype(BF16)
        xhat, _ = norm_stats(base)
        norm_o[at, :] = (xhat * vec[1:2, :] + vec[2:3, :]).astype(BF16)


def whole(shape):
    return pl.BlockSpec(shape, lambda *j: (0,) * len(shape))


def params():
    return pltpu.CompilerParams(vmem_limit_bytes=VMEM)


SCALE = 0.01


def cost(micros):
    return pl.CostEstimate(flops=int(micros * SCALE * 1.15e9), bytes_accessed=int(micros * SCALE * 3e6), transcendentals=0)


def pad_call(rows, tokens, grads):
    width = tokens.shape[1]
    out = jax.ShapeDtypeStruct((rows.all, width), BF16)
    return pl.pallas_call(
        functools.partial(pad_kernel, rows),
        grid=(rows.images,),
        in_specs=[whole(tokens.shape), whole(grads.shape)],
        out_specs=[rows.block(width)] * 2,
        out_shape=[out, out],
        compiler_params=params(),
        cost_estimate=cost(5),
        name="pad_rows",
    )(tokens, grads)


def norm_one_call(rows, tokens, flags, vec):
    out = jax.ShapeDtypeStruct(tokens.shape, BF16)
    return pl.pallas_call(
        functools.partial(norm_one_kernel, rows),
        out_shape=[out, out],
        compiler_params=params(),
        cost_estimate=cost(5),
        name="norm_one",
    )(tokens, flags, vec)


def pack_kernel(count, quarter, *refs):
    *vectors, wide, qkv, proj, up, down = refs[: -2 - quarter // 2]
    first_o, second_o, *ff_o = refs[-2 - quarter // 2 :]
    r, width = proj.shape

    def group(g):
        return [qkv[:, i * width + g * GROUP : i * width + (g + 1) * GROUP] for i in range(3)]

    for i, part in enumerate(group(0)):
        first_o[0, :r, i * GROUP : (i + 1) * GROUP] = part
    small = [v[...].astype(F32) for v in vectors]
    small += [wide[:, r * i : r * (i + 1)].astype(F32) for i in range(quarter)]
    small = jnp.concatenate(small + [jnp.zeros((16 - len(small), r), F32)], axis=0)
    first_o[0, r:, :] = jnp.concatenate([small, jnp.zeros((16, width - r), F32)], axis=1).astype(BF16)
    for g in (1, 2):
        for i, part in enumerate(group(g)):
            second_o[g - 1, :, i * GROUP : (i + 1) * GROUP] = part
    second_o[2] = proj[...]
    for t in range(quarter):
        out = ff_o[t // 2]
        cols = [up[:, (k * quarter + t) * r : (k * quarter + t + 1) * r] for k in range(count)]
        out[t % 2 * 2] = jnp.concatenate(cols, axis=1)
        out[t % 2 * 2 + 1] = down[t * r : (t + 1) * r, :]


def pack_call(count, vectors, wide, qkv, proj, up, down):
    r, width = proj.shape
    quarter = up.shape[1] // width
    shapes = [(1, r + 16, width), (3, r, width)] + [(4, r, width)] * (quarter // 2)
    return pl.pallas_call(
        functools.partial(pack_kernel, count, quarter),
        out_shape=[jax.ShapeDtypeStruct(shape, BF16) for shape in shapes],
        compiler_params=params(),
        cost_estimate=cost(2.5),
        name="pack",
    )(*[v[None] for v in vectors], wide[None], qkv, proj, up, down)


def unpack_kernel(count, quarter, *refs):
    sums, (qkv_o, proj_o, up_o, down_o) = refs[:6], refs[6:]
    r = proj_o.shape[0]
    width = proj_o.shape[1]

    def added(k):
        return [sums[2 * k][b].astype(F32) + sums[2 * k + 1][b].astype(F32) for b in range(sums[2 * k].shape[0])]

    def joined(k):
        out = []
        for b in range(sums[2 * k].shape[0]):
            mine, twin = sums[2 * k][b].astype(F32), sums[2 * k + 1][b].astype(F32)
            here = jnp.concatenate([mine, twin], axis=1)
            there = jnp.concatenate([twin, mine], axis=1)
            out.append(jnp.where(lax.axis_index("rep") == 0, here, there))
        return out

    ff = added(0) + joined(1)
    heads = joined(2)
    proj_o[...] = heads[0]
    for g in range(3):
        for i in range(3):
            qkv_o[:, i * width + g * GROUP : i * width + (g + 1) * GROUP] = heads[1 + g][:, i * GROUP : (i + 1) * GROUP]
    ups = [ff[2 * t] for t in range(quarter)]
    up_o[...] = jnp.concatenate([ups[t][:, k * r : (k + 1) * r] for k in range(count) for t in range(quarter)], axis=1)
    for t in range(quarter):
        down_o[t * r : (t + 1) * r, :] = ff[2 * t + 1]


def unpack_call(count, quarter, sums):
    r, width = sums[0].shape[1:]
    shapes = [(r, 3 * width), (r, width), (r, quarter * width), (quarter * r, width)]
    return pl.pallas_call(
        functools.partial(unpack_kernel, count, quarter),
        out_shape=[jax.ShapeDtypeStruct(shape, F32) for shape in shapes],
        compiler_params=params(),
        cost_estimate=cost(3),
        name="unpack",
    )(*sums)


def halves(x, first):
    zero = jnp.zeros_like(x)
    return jnp.concatenate([jnp.where(first, x, zero), jnp.where(first, zero, x)], axis=0)


def attend_kernel(place, kind, nw, before, rows, base_group, norm, vec, *refs):
    w_in, (q_o, k_o, v_o, att_o, p_o, w_o) = refs[:nw], refs[nw + before :]
    j = pl.program_id(0)
    w = w_o.at[0]
    if kind == "whole":
        w[...] = w_in[0][0]
    else:
        load_weight(place, kind, norm.shape[1] // place.count, w_in, w)
    x = norm[...]
    lanes = pl.ds(pl.multiple_of((base_group + j) * GROUP, GROUP), GROUP)
    q_o[0] = ((dot(x, w[:, 0:GROUP]) + vec[3:4, lanes]).astype(BF16) * 0.125).astype(BF16)
    k_o[0] = dot(x, w[:, GROUP : 2 * GROUP]).astype(BF16)
    v_o[0] = (dot(x, w[:, 2 * GROUP :]) + vec[4:5, lanes]).astype(BF16)
    s = rows.pad
    first = lax.broadcasted_iota(jnp.int32, (s, 128), 1) < HEAD
    live = lax.broadcasted_iota(jnp.int32, (s, 2 * s), 0) < rows.patches

    def image(i):
        at = pl.ds(pl.multiple_of(i * s, 16), s)
        for p in range(2):
            cols = pl.ds(128 * p, 128)
            q, k, v = q_o[0, at, cols], k_o[0, at, cols], v_o[0, at, cols]
            score = jnp.where(live, dot_cols(k, halves(q, first)), NEG)
            peak = jnp.max(score, axis=0, keepdims=True)
            e = jnp.exp(score - peak)
            probs = (e * (1.0 / jnp.sum(e, axis=0, keepdims=True))).astype(BF16)
            p_o[0, p, i] = probs
            o = dot_rows(probs, v)
            att_o[0, at, cols] = jnp.where(first, o[:s], o[s:]).astype(BF16)

    def step(i, carry):
        for u in range(3):
            image(i * 3 + u)
        return carry

    lax.fori_loop(0, rows.images // 3, step, 0)


def piece_specs(weight, blocks=1, first=0):
    if weight.kind == "whole":
        return [pl.BlockSpec((blocks, *weight.arrays[0].shape[1:]), lambda j: (first + j, 0, 0))]
    if weight.kind == "rows":
        z, _, r, w = weight.arrays[0].shape
        return [pl.BlockSpec((z, blocks, r, w), lambda j: (0, first + j, 0, 0))] * 4
    k, z, _, r, w = weight.arrays[0].shape
    return [pl.BlockSpec((k, z, blocks, r, w), lambda j: (0, 0, first + j, 0, 0))] * 2


def attend_call(place, rows, group, groups, norm, vec, weight, before=()):
    s = rows.pad
    width = norm.shape[1]
    row = pl.BlockSpec((1, rows.all, GROUP), lambda j: (group + j, 0, 0))
    out = jax.ShapeDtypeStruct((3, rows.all, GROUP), BF16)
    outs = [out] * 4 + [jax.ShapeDtypeStruct((3, 2, rows.images, s, 2 * s), BF16)]
    specs = [row] * 4 + [pl.BlockSpec((1, 2, rows.images, s, 2 * s), lambda j: (group + j, 0, 0, 0, 0))]
    outs.append(jax.ShapeDtypeStruct((3, width, 3 * GROUP), BF16))
    specs.append(pl.BlockSpec((1, width, 3 * GROUP), lambda j: (group + j, 0, 0)))
    args = [norm, vec, *weight.arrays, *before]
    first = len(args) - len(before)
    return pl.pallas_call(
        functools.partial(attend_kernel, place, weight.kind, len(weight.arrays), len(before), rows, group),
        grid=(groups,),
        in_specs=[whole(norm.shape), whole(vec.shape)]
        + piece_specs(weight)
        + [pl.BlockSpec(memory_space=pl.ANY)] * len(before),
        out_specs=specs,
        out_shape=outs,
        input_output_aliases={first + i: i for i in range(len(before))},
        compiler_params=params(),
        cost_estimate=cost(2 + 6 * groups),
        name="attend",
    )(*args)


def project_kernel(place, kind, nw, spot, vec, base, att, *refs):
    w_in, (resid_o, norm_o, w_o) = refs[:nw], refs[nw:]

    @pl.when(pl.program_id(0) == 0)
    def _():
        if kind == "whole":
            w_o[0] = w_in[0][0]
        else:
            load_weight(place, kind, base.shape[1] // place.count, w_in, w_o.at[0])

    both = jnp.concatenate([att[g] for g in range(att.shape[0])], axis=1)
    total = dot(both, w_o[0]) + base[...].astype(F32) + vec[5:6, :]
    resid_o[...] = total
    xhat, _ = norm_stats(total)
    norm_o[...] = (xhat * vec[6:7, :] + vec[7:8, :]).astype(BF16)


def project_call(place, rows, vec, base, att, weight, spot):
    width = base.shape[1]
    outs = [
        jax.ShapeDtypeStruct((rows.all, width), F32),
        jax.ShapeDtypeStruct((rows.all, width), BF16),
        jax.ShapeDtypeStruct((1, width, width), BF16),
    ]
    some = rows.images // 3
    pieces = [
        pl.BlockSpec(block.block_shape, lambda j, at=block.index_map(0): at)
        for block in piece_specs(weight, 1, spot)
    ]
    return pl.pallas_call(
        functools.partial(project_kernel, place, weight.kind, len(weight.arrays), spot),
        grid=(3,),
        in_specs=[whole(vec.shape), rows.block(width, some)]
        + [pl.BlockSpec((3, rows.pad * some, GROUP), lambda j: (0, j, 0))]
        + pieces,
        out_specs=[rows.block(width, some)] * 2 + [whole(outs[2].shape)],
        out_shape=outs,
        compiler_params=params(),
        cost_estimate=cost(7),
        name="project",
    )(vec, base, att, *weight.arrays)


def feed_kernel(place, kind, form, nw, rows, block, carried, norm, grad, vec, *refs):
    w_in, rest = refs[:nw], refs[nw:]
    if carried:
        (acc_in, gn_in), rest = rest[:2], rest[carried:]
    acc_o, gn_o, bias_o = rest[:3]
    j = pl.program_id(0)
    n = 1 if form == "whole" else 2
    grads_o, act_s, gp_s, rest = rest[3 : 3 + n], rest[3 + n], rest[4 + n], rest[5 + n :]
    if kind == "whole":
        w_up, w_down = w_in[0].at[0], w_in[0].at[1]
    else:
        w_up, w_down, rest = *rest[:2], rest[2:]
        r = norm.shape[1] // place.count
        load_weight(place, kind, r, w_in, w_up, 0)
        load_weight(place, kind, r, w_in, w_down, 1)

    @pl.when(j == 0)
    def _():
        if carried:
            acc_o[...] = acc_in[...]
            gn_o[...] = gn_in[...]
        else:
            acc_o[...] = jnp.zeros_like(acc_o)
            gn_o[...] = jnp.zeros_like(gn_o)

    bias = vec[pl.ds(9 + block + j, 1), :]
    step = rows.pad
    for b in range(rows.images):
        at = pl.ds(b * step, step)
        z = dot(norm[at, :], w_up[...]) + bias
        up = dot_cols(grad[at, :], w_down[...])
        act, slope = gelu_and_slope(z)
        act = act.astype(BF16)
        gp = (up * slope).astype(BF16)
        act_s[at, :] = act
        gp_s[at, :] = gp
        acc_o[at, :] += dot(act, w_down[...])
        gn_o[at, :] += dot_cols(gp, w_up[...])
    bias_o[0] = jnp.sum(gp_s[...].astype(F32), axis=0, keepdims=True)
    for i, (left, right) in enumerate(((norm, gp_s), (act_s, grad))):
        value = dot_rows(left[...], right[...]).astype(BF16)
        if form == "whole":
            grads_o[0][i] = value
        else:
            rest[0][...] = value
            store_grad(place, rest[0], *grads_o, i)


def grad_out(kind, blocks, width, r, per_step):
    if kind == "whole":
        return (
            [jax.ShapeDtypeStruct((blocks, width, width), BF16)],
            [pl.BlockSpec((per_step, width, width), lambda j: (j, 0, 0))],
        )
    if kind == "few":
        lead, w = (2, FAR), width
    else:
        lead, w = (2, 2, FAR), width // 2
    zero = (0,) * len(lead)
    return (
        [jax.ShapeDtypeStruct((*lead, blocks, r, w), BF16)] * 2,
        [pl.BlockSpec((*lead, per_step, r, w), lambda j: (*zero, j, 0, 0))] * 2,
    )


def feed_call(place, rows, block, blocks, spot, norm, grad, vec, weight, form, r, carried):
    width = norm.shape[1]
    acc = jax.ShapeDtypeStruct((rows.all, width), F32)
    outs, specs = grad_out(form, 2 * blocks, width, r, 2)
    scratch = [pltpu.VMEM((rows.all, width), BF16)] * 2
    scratch += [pltpu.VMEM((width, width), BF16)] * ((2 if weight.kind != "whole" else 0) + (form != "whole"))
    args = [norm, grad, vec, *weight.arrays, *carried]
    in_specs = [whole(norm.shape), whole(grad.shape), whole(vec.shape)] + piece_specs(weight, 2, spot)
    in_specs += [whole(acc.shape)] * len(carried)
    return pl.pallas_call(
        functools.partial(feed_kernel, place, weight.kind, form, len(weight.arrays), rows, block, len(carried)),
        grid=(blocks,),
        in_specs=in_specs,
        out_specs=[whole(acc.shape)] * 2 + [pl.BlockSpec((1, 1, width), lambda j: (j, 0, 0))] + specs,
        out_shape=[acc, acc, jax.ShapeDtypeStruct((blocks, 1, width), F32)] + outs,
        scratch_shapes=scratch,
        compiler_params=params(),
        cost_estimate=cost(15 * blocks),
        name="feed",
    )(*args)


def middle_kernel(rows, resid, acc, gn, grad, vec, w, out_o, low_o, da_o, sums_o):
    xhat, scale = norm_stats(resid[...])
    gain = vec[6:7, :]
    up = gn[...]
    g = grad[...].astype(F32)
    total = g + norm_back(up, xhat, scale, gain)
    lowered = total.astype(BF16)
    low_o[...] = lowered
    da_o[...] = dot_cols(lowered, w[0]).astype(BF16)
    sums = jnp.concatenate(
        [
            jnp.sum(total, axis=0, keepdims=True),
            jnp.sum(up * xhat, axis=0, keepdims=True),
            jnp.sum(up, axis=0, keepdims=True),
            jnp.sum(g, axis=0, keepdims=True),
        ],
        axis=0,
    )
    final = resid[...] + acc[...] + vec[8:9, :]
    j = pl.program_id(0)
    for i in range(rows.images):

        @pl.when(j == i)
        def _():
            sums_o[...] = sums if i == 0 else sums_o[...] + sums
            out_o[rows.patches * i : rows.patches * (i + 1), :] = final[: rows.patches]


def middle_call(rows, resid, acc, gn, grad, vec, weight):
    width = resid.shape[1]
    block = rows.block(width)
    outs = [
        jax.ShapeDtypeStruct((rows.raw, width), BF16),
        jax.ShapeDtypeStruct((rows.all, width), BF16),
        jax.ShapeDtypeStruct((rows.all, width), BF16),
        jax.ShapeDtypeStruct((4, width), F32),
    ]

    def kernel(resid, acc, gn, grad, vec, w, out_o, low_o, da_o, sums_o, out_s):
        middle_kernel(rows, resid, acc, gn, grad, vec, w, out_s, low_o, da_o, sums_o)

        @pl.when(pl.program_id(0) == rows.images - 1)
        def _():
            out_o[...] = out_s[...].astype(BF16)

    return pl.pallas_call(
        kernel,
        grid=(rows.images,),
        in_specs=[block] * 4 + [whole(vec.shape), whole(weight.shape)],
        out_specs=[whole(outs[0].shape), block, block, whole(outs[3].shape)],
        out_shape=outs,
        scratch_shapes=[pltpu.VMEM((rows.raw, width), F32)],
        compiler_params=params(),
        cost_estimate=cost(12),
        name="middle",
    )(resid, acc, gn, grad, vec, weight)


STEP = 3


def attend_back_kernel(place, kind, rows, projects, norm, da, *refs):
    g, j = pl.program_id(0), pl.program_id(1)
    q_i, k_i, v_i, p_i, refs = *refs[:4], refs[4:]
    if projects:
        (lowered, *atts), refs = refs[: 1 + projects], refs[1 + projects :]
    d_o, bias_o = refs[:2]
    if kind == "whole":
        (grads_o,) = refs[2:]
    else:
        keep, send, g_s = refs[2:]
    s = rows.pad
    some = rows.images // STEP
    first = lax.broadcasted_iota(jnp.int32, (s, 128), 1) < HEAD

    def emit(value, spot):
        if kind == "whole":
            grads_o[spot] = value.astype(BF16)
        else:
            g_s[...] = value.astype(BF16)
            store_grad(place, g_s, keep, send, spot)

    for i in range(some):
        at = pl.ds(i * s, s)
        to = pl.ds(pl.multiple_of((j * some + i) * s, 16), s)
        for p in range(2):
            cols = pl.ds(128 * p, 128)
            q, k, v = q_i[0, at, cols], k_i[0, at, cols], v_i[0, at, cols]
            q2, da2 = halves(q, first), halves(da[at, cols], first)
            low_probs = p_i[0, p, i]
            d_o[0, to, pl.ds(2 * GROUP + 128 * p, 128)] = dot(low_probs, da2).astype(BF16)
            up = dot_cols(v, da2)
            probs = low_probs.astype(F32)
            inner = jnp.sum(probs * up, axis=0, keepdims=True)
            ds = (probs * (up - inner)).astype(BF16)
            d_o[0, to, pl.ds(GROUP + 128 * p, 128)] = dot(ds, q2).astype(BF16)
            dq = dot_rows(ds, k)
            d_o[0, to, cols] = (jnp.where(first, dq[:s], dq[s:]) * 0.125).astype(BF16)

    @pl.when(j == STEP - 1)
    def _():
        if projects:

            @pl.when(g == 0)
            def _():
                both = jnp.concatenate([a[b] for a in atts for b in range(a.shape[0])], axis=1)
                emit(dot_rows(both, lowered[...]), 0)

        bias_o[0] = jnp.sum(d_o[0].astype(F32), axis=0, keepdims=True)
        emit(dot_rows(norm[...], d_o[0]), g + (1 if projects else 0))


def attend_back_call(place, rows, group, groups, norm, q, k, v, probs, da, r, shape="few", project=()):
    width = norm.shape[1]
    s = rows.pad
    some = rows.images // STEP
    row = pl.BlockSpec((1, s * some, GROUP), lambda g, j: (group + g, j, 0))
    in_specs = [whole(norm.shape), pl.BlockSpec((s * some, GROUP), lambda g, j: (j, group + g)), row, row, row]
    in_specs += [pl.BlockSpec((1, 2, some, s, 2 * s), lambda g, j: (group + g, 0, j, 0, 0))]
    in_specs += [whole(a.shape) for a in project]
    kind = shape
    outs, specs = grad_out(kind, groups + (1 if project else 0), width, r, 1)
    specs = [whole(out.shape) for out in outs]
    return pl.pallas_call(
        functools.partial(attend_back_kernel, place, kind, rows, max(len(project) - 1, 0)),
        grid=(groups, STEP),
        in_specs=in_specs,
        out_specs=[
            pl.BlockSpec((1, rows.all, width), lambda g, j: (g, 0, 0)),
            pl.BlockSpec((1, 1, width), lambda g, j: (g, 0, 0)),
        ]
        + specs,
        out_shape=[
            jax.ShapeDtypeStruct((groups, rows.all, width), BF16),
            jax.ShapeDtypeStruct((groups, 1, width), F32),
        ]
        + outs,
        scratch_shapes=[] if kind == "whole" else [pltpu.VMEM((width, width), BF16)],
        compiler_params=params(),
        cost_estimate=cost(11 * groups),
        name="attend_back",
    )(norm, da, q, k, v, probs, *project)


def last_kernel(rows, counts, quarter, count, base, low, flags, vec, w, *refs):
    n = len(counts)
    dqkv, biases, two, feeds, (out_o, late_o, sums_o) = refs[:n], refs[n : 2 * n], refs[2 * n], refs[2 * n + 1 : -3], refs[-3:]
    cols = flag_column(rows, flags)
    gain = vec[1:2, :]
    parts = [d[b] for d, count in zip(dqkv, counts) for b in range(count)]
    up = dot_cols(parts[0], w[0])
    for g in range(1, len(parts)):
        up = up + dot_cols(parts[g], w[g])
    xhat, scale = norm_stats(base[...].astype(F32))
    total = low[...].astype(F32) + norm_back(up, xhat, scale, gain)
    row = lax.broadcasted_iota(jnp.int32, (rows.pad, 1), 0)
    j = pl.program_id(0)
    for i in range(rows.images):

        @pl.when(j == i)
        def _():
            chosen = jnp.logical_and(cols[: rows.pad, i : i + 1] > 0.5, row < rows.patches)
            sums = jnp.concatenate(
                [
                    jnp.sum(jnp.where(chosen, total, 0.0), axis=0, keepdims=True),
                    jnp.sum(up * xhat, axis=0, keepdims=True),
                    jnp.sum(up, axis=0, keepdims=True),
                ],
                axis=0,
            )
            sums_o[...] = sums if i == 0 else sums_o[...] + sums
            out_o[rows.patches * i : rows.patches * (i + 1), :] = jnp.where(chosen, 0.0, total)[: rows.patches]

    @pl.when(j == rows.images - 1)
    def _():
        groups = [b[g] for b, group_count in zip(biases, counts) for g in range(group_count)]
        query = jnp.concatenate([g[:, :GROUP] for g in groups], axis=1)
        value = jnp.concatenate([g[:, 2 * GROUP :] for g in groups], axis=1)
        hidden = [f[b] for f in feeds for b in range(f.shape[0])]
        width = base.shape[1]
        every = jnp.concatenate(
            [sums_o[...], query, value, two[...], *hidden, jnp.zeros((9 - quarter - 2, width), F32)], axis=0
        )
        r = width // count
        for k in range(late_o.shape[0]):
            at = k % count
            late_o[k] = every[:, at * r : (at + 1) * r]


def last_call(rows, count, copies, base, low, flags, vec, w, dqkv, biases, two, feeds):
    width = base.shape[1]
    block = rows.block(width)
    outs = [
        jax.ShapeDtypeStruct((rows.raw, width), F32),
        jax.ShapeDtypeStruct((copies * count, 16, width // count), F32),
    ]
    quarter = sum(f.shape[0] for f in feeds)
    small = [*biases, two, *feeds]
    return pl.pallas_call(
        functools.partial(last_kernel, rows, [d.shape[0] for d in dqkv], quarter, count),
        grid=(rows.images,),
        in_specs=[block, block, whole(flags.shape), whole(vec.shape), whole(w.shape)]
        + [pl.BlockSpec((d.shape[0], rows.pad, width), lambda j: (0, j, 0)) for d in dqkv]
        + [whole(v.shape) for v in small],
        out_specs=[whole(out.shape) for out in outs],
        out_shape=outs,
        scratch_shapes=[pltpu.VMEM((3, width), F32)],
        compiler_params=params(),
        cost_estimate=cost(1500),
        name="last",
    )(base, low, flags, vec, w, *dqkv, *small)


def local(
    count,
    tokens,
    mask_flags,
    mask_token,
    norm1_gain,
    norm1_bias,
    qkv_weight,
    query_bias,
    value_bias,
    proj_weight,
    proj_bias,
    norm2_gain,
    norm2_bias,
    fc1_weight,
    fc1_bias,
    fc2_weight,
    fc2_bias,
    out_grad,
):
    images, patches = mask_flags.shape
    rows = Rows(images, patches)
    r, width = proj_weight.shape
    place = Place(count) if r % 16 == 0 and count == 4 * FAR else None
    quarter = fc1_weight.shape[1] // width

    half = quarter // 2
    vectors = (mask_token, norm1_gain, norm1_bias, query_bias, value_bias, proj_bias, norm2_gain, norm2_bias, fc2_bias)
    kinds = len(vectors) + quarter

    def whole_gather(stack):
        return Weight("whole", [lax.all_gather(stack, "fsdp", axis=1, tiled=True)])

    def whole_scatter(sums):
        share = lax.psum_scatter(sums if place else sums.astype(F32), "fsdp", scatter_dimension=1, tiled=True)
        return share if place else lax.psum(share, "rep")

    flow = Flow()
    pad_in = (tokens, out_grad)
    if place:
        z, x, c = place.own()
        first, second, ff_0, ff_1 = pack_call(count, vectors, fc1_bias, qkv_weight, proj_weight, fc1_weight, fc2_weight)
        flow.begin("wa", gather_fast(place, first))
        pad_in = flow.send(*pad_in)
    else:
        qkv_blocks = qkv_weight.reshape(r, 3, 3, GROUP).transpose(2, 0, 1, 3).reshape(3, r, 3 * GROUP)
        up_blocks = fc1_weight.reshape(r, count, quarter, r).transpose(2, 0, 1, 3).reshape(quarter, r, width)
        down_blocks = fc2_weight.reshape(quarter, r, width)
        ff = jnp.stack([up_blocks, down_blocks], axis=1).reshape(2 * quarter, r, width)
        w_a, w_b = whole_gather(qkv_blocks[:1]), whole_gather(jnp.concatenate([qkv_blocks[1:], proj_weight[None]]))
        w_f0, w_f1 = whole_gather(ff[: 2 * half]), whole_gather(ff[2 * half :])
        small = jnp.concatenate([v[None] for v in vectors] + [fc1_bias.reshape(quarter, r)])
        came = lax.all_gather(small, "fsdp", axis=1, tiled=True)
        came = jnp.pad(came, ((0, 16 - kinds), (0, 0)))
    base, grad = pad_call(rows, *pad_in)
    if place:
        (base,) = flow.meet(["wa"], base)
        flow.begin("wb", gather_wide(place, second))
        flow.begin("wf0", gather_even(place, ff_0))
        (base,) = flow.send(base)
        (base,) = flow.turn(["wa"], base)
        (base,) = flow.meet(["wa"], base)
        w_a = flow.done["wa"]
        came = jnp.stack([part[:, 0, r:, :r] for part in w_a.arrays]).reshape(2, 2, FAR, -1, r)
        came = jnp.where(c == 0, came, came[::-1])
        came = jnp.where(x == 0, came, came[:, ::-1])
        came = jnp.where(z % 2 == 0, came, came.reshape(2, 2, 2, 2, -1, r)[:, :, :, ::-1].reshape(came.shape))
        came = jnp.where(z < 2, came, came.reshape(2, 2, 2, 2, -1, r)[:, :, ::-1].reshape(came.shape))
        came = came.transpose(3, 2, 1, 0, 4)
    vec = came.reshape(16, width).astype(F32)

    base, norm = norm_one_call(rows, base, mask_flags, vec)
    if place:
        (norm,) = flow.turn(["wb"], norm)
    attends = attend_call(place, rows, 0, 1, norm, vec, w_a)
    if place:
        norm, *attends = flow.turn(["wb", "wf0"], norm, *attends)
        norm, ff_1, *attends = flow.meet(["wb"], norm, ff_1, *attends)
        w_b = flow.done["wb"]
        w_f1 = whole_gather(ff_1)
    q, k, v, att, probs, wqkv = attend_call(place, rows, 1, 2, norm, vec, w_b, attends)
    if place:
        (att,) = flow.turn(["wf0"], att)
    resid, norm_two, w_proj = project_call(place, rows, vec, base, att, w_b, 2)
    if place:
        (norm_two,) = flow.turn(["wf0"], norm_two)
        (norm_two,) = flow.meet(["wf0"], norm_two)
        w_f0 = flow.done["wf0"]

    form = "wide" if place else "whole"
    acc, gn, gb_0, f0 = feed_call(place, rows, 0, half, 0, norm_two, grad, vec, w_f0, "whole", r, ())
    f0 = whole_scatter(f0)
    acc, gn, gb_1, *f1 = feed_call(place, rows, half, half, 0, norm_two, grad, vec, w_f1, form, r, (acc, gn))
    if place:
        flow.begin("f1", scatter_wide(place, *f1))
        acc, gn = flow.send(acc, gn)

    block_out, lowered, da, sums_two = middle_call(rows, resid, acc, gn, grad, vec, w_proj)
    if place:
        (da,) = flow.turn(["f1"], da)
    dqkv, qs, *sums_c = attend_back_call(
        place, rows, 0, 3, norm, q, k, v, probs, da, r, form, project=[lowered, att]
    )
    if place:
        flow.begin("c", scatter_wide(place, *sums_c))
        dqkv, f0 = flow.meet(["f1"], dqkv, f0)
        flow.begin("f0", send_twin(place, f0))
        (dqkv,) = flow.send(dqkv)
    input_grad, late = last_call(
        rows,
        count,
        2 if place else 1,
        base,
        lowered,
        mask_flags,
        vec,
        wqkv,
        [dqkv],
        [qs],
        sums_two,
        [gb_0, gb_1],
    )
    if place:
        late, input_grad = flow.turn(["c", "f1", "f0"], late, input_grad)
        late = lax.all_to_all(late, ("rep", "fsdp"), 0, 0, tiled=True)
        (late,) = flow.meet(["c"], late)
        flow.begin("fy", send_twin(place, flow.done["f1"]))
        (late,) = flow.send(late)
        (late,) = flow.meet(["c", "fy"], late)
        flow.begin("cy", send_twin(place, flow.done["c"]))
        (late,) = flow.send(late)
        (late,) = flow.meet(["cy"], late)
        shares = late.sum(axis=0)
        sums = [side for name in ("f0", "fy", "cy") for pair in zip(*flow.done[name]) for side in pair]
        g_qkv, g_proj, g_up, g_down = unpack_call(count, quarter, sums)
    else:
        shares = lax.psum(lax.psum_scatter(late, "fsdp", scatter_dimension=0, tiled=True), "rep")[0]
        sums_c = whole_scatter(sums_c[0])
        g_proj = sums_c[0]
        g_qkv = sums_c[1:].reshape(3, r, 3, GROUP).transpose(1, 2, 0, 3).reshape(r, 3 * width)
        g_ff = jnp.concatenate([f0, whole_scatter(f1[0])]).reshape(quarter, 2, r, width)
        g_up = g_ff[:, 0].reshape(quarter, r, count, r).transpose(1, 2, 0, 3).reshape(r, quarter * width)
        g_down = g_ff[:, 1].reshape(quarter * r, width)
    token_s, gain1_s, shift1_s, qb_s, vb_s, pb_s, gain2_s, shift2_s, db_s = [shares[i] for i in range(9)]
    ub_s = shares[9:kinds].reshape(-1)
    return (
        block_out,
        input_grad,
        token_s,
        gain1_s,
        shift1_s,
        g_qkv,
        qb_s,
        vb_s,
        g_proj,
        pb_s,
        gain2_s,
        shift2_s,
        g_up,
        ub_s,
        g_down,
        db_s,
    )


def solution(mesh):
    both, one = P(("rep", "fsdp"), None), P("fsdp")
    flat = P("fsdp", None)
    in_specs = (both, both, one, one, one, flat, one, one, flat, one, one, one, flat, one, flat, one, both)
    out_specs = (both, both, one, one, one, flat, one, one, flat, one, one, one, flat, one, flat, one)
    return jax.shard_map(
        functools.partial(local, mesh.shape["fsdp"]),
        mesh=mesh,
        in_specs=in_specs,
        out_specs=out_specs,
        check_vma=False,
    )
```

```python
import functools
import math

import jax
import jax.numpy as jnp
from jax import lax
from jax.experimental import pallas as pl
from jax.experimental.pallas import tpu as pltpu
from jax.sharding import PartitionSpec as P

F32 = jnp.float32
BF16 = jnp.bfloat16
HEAD = 64
GROUP = 256
NEG = -1e30
VMEM = 56 * 2**20


def dot(a, b):
    return lax.dot_general(a, b, (((1,), (0,)), ((), ())), preferred_element_type=F32)


def dot_rows(a, b):
    return lax.dot_general(a, b, (((0,), (0,)), ((), ())), preferred_element_type=F32)


def dot_cols(a, b):
    return lax.dot_general(a, b, (((1,), (1,)), ((), ())), preferred_element_type=F32)


FAR = 4


class Place:
    def __init__(self, count):
        self.count = count

    def own(self):
        index = lax.axis_index("fsdp")
        return index // 4, (index // 2) % 2, index % 2

    def swap(self, bits):
        return [(i, i ^ bits) for i in range(self.count)]

    def core(self, v):
        return lax.ppermute(v, "fsdp", self.swap(1))

    def along_x(self, v):
        return lax.ppermute(v, "fsdp", self.swap(2))

    def along_z(self, d):
        return lambda v: lax.ppermute(v, "fsdp", self.swap(4 * d))

    def along_y(self, v):
        return lax.ppermute(v, "rep", [(0, 1), (1, 0)])

    def along_xy(self, v):
        n = self.count
        return lax.ppermute(
            v, ("rep", "fsdp"), [(y * n + i, (1 - y) * n + (i ^ 2)) for y in range(2) for i in range(n)]
        )


def shard_at(own, dc, dx, dz):
    z, x, c = own
    return (lax.bitwise_xor(z, dz) * 2 + lax.bitwise_xor(x, dx)) * 2 + lax.bitwise_xor(c, dc)


def add_low(*terms):
    total = terms[0].astype(F32)
    for term in terms[1:]:
        total = total + term.astype(F32)
    return total


def low(v):
    return v.astype(BF16)


def by_side(side, first, second, axis):
    return jnp.where(side == 0, jnp.concatenate([first, second], axis), jnp.concatenate([second, first], axis))


class Weight:
    def __init__(self, kind, arrays):
        self.kind = kind
        self.arrays = arrays


def gather_fast(place, stack):
    came = yield [(place.along_z(d), stack) for d in range(1, FAR)]
    own = jnp.stack([stack] + came)
    beside, own_core = yield [(place.along_x, own), (place.core, own)]
    (beside_core,) = yield [(place.core, beside)]
    return Weight("rows", [own, beside, own_core, beside_core])


def half_columns(stack):
    half = stack.shape[2] // 2
    return lax.dynamic_slice_in_dim(stack, lax.axis_index("rep") * half, half, axis=2)


def gather_wide(place, stack):
    mine = half_columns(stack)
    came = yield [(place.along_z(d), mine) for d in range(1, FAR)]
    own = jnp.stack([mine] + came)
    came = yield [(place.along_x, own), (place.along_y, own), (place.along_xy, own)]
    here = jnp.stack([own] + came)
    (across,) = yield [(place.core, here)]
    return Weight("halves", [here, across])


def gather_even(place, stack):
    mine = half_columns(stack)
    came = yield [(place.along_z(d), mine) for d in range(1, FAR)]
    own = jnp.stack([mine] + came)
    beside, twin = yield [(place.along_x, own), (place.along_y, own)]
    corner = yield [(place.along_y, beside[:2]), (place.along_x, twin[2:])]
    here = jnp.stack([own, beside, twin, jnp.concatenate(corner)])
    (across,) = yield [(place.core, here)]
    return Weight("halves", [here, across])


def gather_late_y(place, stack):
    mine = half_columns(stack)
    came = yield [(place.along_z(d), mine) for d in range(1, FAR)]
    own = jnp.stack([mine] + came)
    (beside,) = yield [(place.along_x, own)]
    side = jnp.stack([own, beside])
    (twin,) = yield [(place.along_y, side)]
    here = jnp.concatenate([side, twin])
    (across,) = yield [(place.core, here)]
    return Weight("halves", [here, across])


def scatter_early_y(place, keep, send):
    (came,) = yield [(place.core, send)]
    (came_y,) = yield [(place.along_y, low(add_low(keep[1], came[1])))]
    (came_x,) = yield [(place.along_x, low(add_low(keep[0, 1], came[0, 1], came_y[1])))]
    total = low(add_low(keep[0, 0], came[0, 0], came_y[0], came_x))
    came = yield [(place.along_z(d), total[d]) for d in range(1, FAR)]
    return low(add_low(total[0], *came))


def scatter_wide(place, keep, send):
    (came,) = yield [(place.core, send)]

    def pair(dy, dx):
        return low(add_low(keep[dy, dx], came[dy, dx]))

    came_xy = yield [(place.along_x, pair(0, 1)), (place.along_y, pair(1, 0)), (place.along_xy, pair(1, 1))]
    total = low(add_low(keep[0, 0], came[0, 0], *came_xy))
    came = yield [(place.along_z(d), total[d]) for d in range(1, FAR)]
    return low(add_low(total[0], *came))


def send_twin(place, *mine):
    twins = yield [(place.along_y, v) for v in mine]
    return list(mine), twins


class Flow:
    def __init__(self):
        self.live = {}
        self.done = {}

    def begin(self, name, steps):
        self.live[name] = (steps, next(steps), None)

    def send(self, *arrays):
        waiting = [name for name, (_, pairs, sent) in self.live.items() if sent is None]
        flat = [v for name in waiting for _, v in self.live[name][1]]
        flat = list(lax.optimization_barrier(tuple(flat) + tuple(arrays)))
        for name in waiting:
            steps, pairs, _ = self.live[name]
            sent = [move(v) for (move, _), v in zip(pairs, flat)]
            flat = flat[len(pairs) :]
            self.live[name] = (steps, pairs, sent)
        return flat

    def meet(self, names, *arrays):
        names = [name for name in names if name in self.live]
        flat = [v for name in names for v in self.live[name][2]]
        flat = list(lax.optimization_barrier(tuple(flat) + tuple(arrays)))
        for name in names:
            steps, pairs, _ = self.live[name]
            mine, flat = flat[: len(pairs)], flat[len(pairs) :]
            try:
                self.live[name] = (steps, steps.send(mine), None)
            except StopIteration as stop:
                del self.live[name]
                self.done[name] = stop.value
        return flat

    def turn(self, names, *arrays):
        return self.send(*self.meet(names, *arrays))


def half_at(dy, width):
    at = lax.bitwise_xor(lax.axis_index("rep"), dy) * width
    return pl.ds(pl.multiple_of(at, 128), width)


def load_weight(place, kind, rows, refs, spot, lead=0):
    own = place.own()
    for dc in range(2):
        for dx in range(2):
            for d in range(FAR):
                at = pl.ds(pl.multiple_of(shard_at(own, dc, dx, d) * rows, 16), rows)
                if kind == "rows":
                    spot[at, :] = refs[2 * dc + dx][d, lead, :rows]
                else:
                    for dy in range(2):
                        spot[at, half_at(dy, refs[0].shape[-1])] = refs[dc][2 * dy + dx, d, lead]


def store_grad(place, spot, keep, send, lead=0):
    own = place.own()
    rows, width = keep.shape[-2:]
    for dc, ref in enumerate((keep, send)):
        for dx in range(2):
            for d in range(FAR):
                at = pl.ds(pl.multiple_of(shard_at(own, dc, dx, d) * rows, 16), rows)
                if len(keep.shape) == 5:
                    ref[dx, d, lead] = spot[at, :]
                else:
                    for dy in range(2):
                        ref[dy, dx, d, lead] = spot[at, half_at(dy, width)]


def norm_stats(v):
    mean = jnp.mean(v, axis=-1, keepdims=True)
    centred = v - mean
    spread = jnp.mean(centred * centred, axis=-1, keepdims=True)
    scale = lax.rsqrt(spread + 1e-06)
    return centred * scale, scale


def norm_back(up, xhat, scale, gain):
    e = up * gain
    return (e - jnp.mean(e, axis=-1, keepdims=True) - xhat * jnp.mean(e * xhat, axis=-1, keepdims=True)) * scale


ERF_P = 0.3275911 / math.sqrt(2.0)
ERF_A = (0.254829592, -0.284496736, 1.421413741, -1.453152027, 1.061405429)


def gelu_and_slope(z):
    t = 1.0 / (1.0 + ERF_P * jnp.abs(z))
    e = jnp.exp(-0.5 * (z * z))
    poly = 0.5 * ERF_A[4]
    for a in ERF_A[3::-1]:
        poly = poly * t + 0.5 * a
    q = poly * t * e
    phi = jnp.where(z > 0, 1.0 - q, q)
    return z * phi, phi + z * (e * (1.0 / math.sqrt(2.0 * math.pi)))


class Rows:
    def __init__(self, images, patches):
        self.images = images
        self.patches = patches
        self.pad = -(-patches // 16) * 16
        self.all = images * self.pad
        self.raw = images * patches

    def block(self, width, count=1):
        return pl.BlockSpec((self.pad * count, width), lambda j: (j, 0))


def flag_column(rows, flags):
    wide = flags[...].astype(F32)
    wide = jnp.concatenate([wide, jnp.zeros((8 - rows.images, rows.patches), F32)], axis=0)
    gap = -rows.patches % 128
    return jnp.concatenate([wide, jnp.zeros((8, gap), F32)], axis=1).T


def padded_image(rows, ref, i):
    lo = rows.patches * i
    first = lo // 16 * 16
    last = min(-(-(lo + rows.patches) // 16) * 16, rows.raw)
    part = ref[first:last, :].astype(F32)[lo - first : lo - first + rows.patches]
    return jnp.concatenate([part, jnp.zeros((rows.pad - rows.patches, ref.shape[1]), F32)], axis=0)


def pad_kernel(rows, tokens, grads, base_o, grad_o):
    j = pl.program_id(0)

    def image(i):
        base_o[...] = padded_image(rows, tokens, i).astype(BF16)
        grad_o[...] = padded_image(rows, grads, i).astype(BF16)

    for i in range(rows.images):
        pl.when(j == i)(functools.partial(image, i))


def norm_one_kernel(rows, tokens, flags, vec, base_o, norm_o):
    cols = flag_column(rows, flags)
    row = lax.broadcasted_iota(jnp.int32, (rows.pad, 1), 0)
    for i in range(rows.images):
        at = pl.ds(i * rows.pad, rows.pad)
        masked = jnp.logical_and(cols[: rows.pad, i : i + 1] > 0.5, row < rows.patches)
        base = jnp.where(masked, vec[0:1, :], tokens[at, :].astype(F32))
        base_o[at, :] = base.astype(BF16)
        xhat, _ = norm_stats(base)
        norm_o[at, :] = (xhat * vec[1:2, :] + vec[2:3, :]).astype(BF16)


def whole(shape):
    return pl.BlockSpec(shape, lambda *j: (0,) * len(shape))


def params():
    return pltpu.CompilerParams(vmem_limit_bytes=VMEM)


SCALE = 0.01


def cost(micros):
    return pl.CostEstimate(flops=int(micros * SCALE * 1.15e9), bytes_accessed=int(micros * SCALE * 3e6), transcendentals=0)


def pad_call(rows, tokens, grads):
    width = tokens.shape[1]
    out = jax.ShapeDtypeStruct((rows.all, width), BF16)
    return pl.pallas_call(
        functools.partial(pad_kernel, rows),
        grid=(rows.images,),
        in_specs=[whole(tokens.shape), whole(grads.shape)],
        out_specs=[rows.block(width)] * 2,
        out_shape=[out, out],
        compiler_params=params(),
        cost_estimate=cost(5),
        name="pad_rows",
    )(tokens, grads)


def norm_one_call(rows, tokens, flags, vec):
    out = jax.ShapeDtypeStruct(tokens.shape, BF16)
    return pl.pallas_call(
        functools.partial(norm_one_kernel, rows),
        out_shape=[out, out],
        compiler_params=params(),
        cost_estimate=cost(5),
        name="norm_one",
    )(tokens, flags, vec)


def pack_kernel(count, quarter, *refs):
    *vectors, wide, qkv, proj, up, down = refs[: -2 - quarter // 2]
    first_o, second_o, *ff_o = refs[-2 - quarter // 2 :]
    r, width = proj.shape

    def group(g):
        return [qkv[:, i * width + g * GROUP : i * width + (g + 1) * GROUP] for i in range(3)]

    for i, part in enumerate(group(0)):
        first_o[0, :r, i * GROUP : (i + 1) * GROUP] = part
    small = [v[...].astype(F32) for v in vectors]
    small += [wide[:, r * i : r * (i + 1)].astype(F32) for i in range(quarter)]
    small = jnp.concatenate(small + [jnp.zeros((16 - len(small), r), F32)], axis=0)
    first_o[0, r:, :] = jnp.concatenate([small, jnp.zeros((16, width - r), F32)], axis=1).astype(BF16)
    for g in (1, 2):
        for i, part in enumerate(group(g)):
            second_o[g - 1, :, i * GROUP : (i + 1) * GROUP] = part
    second_o[2] = proj[...]
    for t in range(quarter):
        out = ff_o[t // 2]
        cols = [up[:, (k * quarter + t) * r : (k * quarter + t + 1) * r] for k in range(count)]
        out[t % 2 * 2] = jnp.concatenate(cols, axis=1)
        out[t % 2 * 2 + 1] = down[t * r : (t + 1) * r, :]


def pack_call(count, vectors, wide, qkv, proj, up, down):
    r, width = proj.shape
    quarter = up.shape[1] // width
    shapes = [(1, r + 16, width), (3, r, width)] + [(4, r, width)] * (quarter // 2)
    return pl.pallas_call(
        functools.partial(pack_kernel, count, quarter),
        out_shape=[jax.ShapeDtypeStruct(shape, BF16) for shape in shapes],
        compiler_params=params(),
        cost_estimate=cost(2.5),
        name="pack",
    )(*[v[None] for v in vectors], wide[None], qkv, proj, up, down)


def unpack_kernel(count, quarter, *refs):
    sums, (qkv_o, proj_o, up_o, down_o) = refs[:6], refs[6:]
    r = proj_o.shape[0]
    width = proj_o.shape[1]

    def added(k):
        return [sums[2 * k][b].astype(F32) + sums[2 * k + 1][b].astype(F32) for b in range(sums[2 * k].shape[0])]

    def joined(k):
        out = []
        for b in range(sums[2 * k].shape[0]):
            mine, twin = sums[2 * k][b].astype(F32), sums[2 * k + 1][b].astype(F32)
            here = jnp.concatenate([mine, twin], axis=1)
            there = jnp.concatenate([twin, mine], axis=1)
            out.append(jnp.where(lax.axis_index("rep") == 0, here, there))
        return out

    ff = added(0) + joined(1)
    heads = joined(2)
    proj_o[...] = heads[0]
    for g in range(3):
        for i in range(3):
            qkv_o[:, i * width + g * GROUP : i * width + (g + 1) * GROUP] = heads[1 + g][:, i * GROUP : (i + 1) * GROUP]
    ups = [ff[2 * t] for t in range(quarter)]
    up_o[...] = jnp.concatenate([ups[t][:, k * r : (k + 1) * r] for k in range(count) for t in range(quarter)], axis=1)
    for t in range(quarter):
        down_o[t * r : (t + 1) * r, :] = ff[2 * t + 1]


def unpack_call(count, quarter, sums):
    r, width = sums[0].shape[1:]
    shapes = [(r, 3 * width), (r, width), (r, quarter * width), (quarter * r, width)]
    return pl.pallas_call(
        functools.partial(unpack_kernel, count, quarter),
        out_shape=[jax.ShapeDtypeStruct(shape, F32) for shape in shapes],
        compiler_params=params(),
        cost_estimate=cost(3),
        name="unpack",
    )(*sums)


def halves(x, first):
    zero = jnp.zeros_like(x)
    return jnp.concatenate([jnp.where(first, x, zero), jnp.where(first, zero, x)], axis=0)


def attend_kernel(place, kind, nw, before, rows, base_group, norm, vec, *refs):
    w_in, (q_o, k_o, v_o, att_o, p_o, w_o) = refs[:nw], refs[nw + before :]
    j = pl.program_id(0)
    w = w_o.at[0]
    if kind == "whole":
        w[...] = w_in[0][0]
    else:
        load_weight(place, kind, norm.shape[1] // place.count, w_in, w)
    x = norm[...]
    lanes = pl.ds(pl.multiple_of((base_group + j) * GROUP, GROUP), GROUP)
    q_o[0] = ((dot(x, w[:, 0:GROUP]) + vec[3:4, lanes]).astype(BF16) * 0.125).astype(BF16)
    k_o[0] = dot(x, w[:, GROUP : 2 * GROUP]).astype(BF16)
    v_o[0] = (dot(x, w[:, 2 * GROUP :]) + vec[4:5, lanes]).astype(BF16)
    s = rows.pad
    first = lax.broadcasted_iota(jnp.int32, (s, 128), 1) < HEAD
    live = lax.broadcasted_iota(jnp.int32, (s, 2 * s), 0) < rows.patches

    def image(i):
        at = pl.ds(pl.multiple_of(i * s, 16), s)
        for p in range(2):
            cols = pl.ds(128 * p, 128)
            q, k, v = q_o[0, at, cols], k_o[0, at, cols], v_o[0, at, cols]
            score = jnp.where(live, dot_cols(k, halves(q, first)), NEG)
            peak = jnp.max(score, axis=0, keepdims=True)
            e = jnp.exp(score - peak)
            probs = (e * (1.0 / jnp.sum(e, axis=0, keepdims=True))).astype(BF16)
            p_o[0, p, i] = probs
            o = dot_rows(probs, v)
            att_o[0, at, cols] = jnp.where(first, o[:s], o[s:]).astype(BF16)

    def step(i, carry):
        for u in range(3):
            image(i * 3 + u)
        return carry

    lax.fori_loop(0, rows.images // 3, step, 0)


def piece_specs(weight, blocks=1, first=0):
    if weight.kind == "whole":
        return [pl.BlockSpec((blocks, *weight.arrays[0].shape[1:]), lambda j: (first + j, 0, 0))]
    if weight.kind == "rows":
        z, _, r, w = weight.arrays[0].shape
        return [pl.BlockSpec((z, blocks, r, w), lambda j: (0, first + j, 0, 0))] * 4
    k, z, _, r, w = weight.arrays[0].shape
    return [pl.BlockSpec((k, z, blocks, r, w), lambda j: (0, 0, first + j, 0, 0))] * 2


def attend_call(place, rows, group, groups, norm, vec, weight, before=()):
    s = rows.pad
    width = norm.shape[1]
    row = pl.BlockSpec((1, rows.all, GROUP), lambda j: (group + j, 0, 0))
    out = jax.ShapeDtypeStruct((3, rows.all, GROUP), BF16)
    outs = [out] * 4 + [jax.ShapeDtypeStruct((3, 2, rows.images, s, 2 * s), BF16)]
    specs = [row] * 4 + [pl.BlockSpec((1, 2, rows.images, s, 2 * s), lambda j: (group + j, 0, 0, 0, 0))]
    outs.append(jax.ShapeDtypeStruct((3, width, 3 * GROUP), BF16))
    specs.append(pl.BlockSpec((1, width, 3 * GROUP), lambda j: (group + j, 0, 0)))
    args = [norm, vec, *weight.arrays, *before]
    first = len(args) - len(before)
    return pl.pallas_call(
        functools.partial(attend_kernel, place, weight.kind, len(weight.arrays), len(before), rows, group),
        grid=(groups,),
        in_specs=[whole(norm.shape), whole(vec.shape)]
        + piece_specs(weight)
        + [pl.BlockSpec(memory_space=pl.ANY)] * len(before),
        out_specs=specs,
        out_shape=outs,
        input_output_aliases={first + i: i for i in range(len(before))},
        compiler_params=params(),
        cost_estimate=cost(2 + 6 * groups),
        name="attend",
    )(*args)


def project_kernel(place, kind, nw, spot, vec, base, att, *refs):
    w_in, (resid_o, norm_o, w_o) = refs[:nw], refs[nw:]

    @pl.when(pl.program_id(0) == 0)
    def _():
        if kind == "whole":
            w_o[0] = w_in[0][0]
        else:
            load_weight(place, kind, base.shape[1] // place.count, w_in, w_o.at[0])

    both = jnp.concatenate([att[g] for g in range(att.shape[0])], axis=1)
    total = dot(both, w_o[0]) + base[...].astype(F32) + vec[5:6, :]
    resid_o[...] = total
    xhat, _ = norm_stats(total)
    norm_o[...] = (xhat * vec[6:7, :] + vec[7:8, :]).astype(BF16)


def project_call(place, rows, vec, base, att, weight, spot):
    width = base.shape[1]
    outs = [
        jax.ShapeDtypeStruct((rows.all, width), F32),
        jax.ShapeDtypeStruct((rows.all, width), BF16),
        jax.ShapeDtypeStruct((1, width, width), BF16),
    ]
    some = rows.images // 3
    pieces = [
        pl.BlockSpec(block.block_shape, lambda j, at=block.index_map(0): at)
        for block in piece_specs(weight, 1, spot)
    ]
    return pl.pallas_call(
        functools.partial(project_kernel, place, weight.kind, len(weight.arrays), spot),
        grid=(3,),
        in_specs=[whole(vec.shape), rows.block(width, some)]
        + [pl.BlockSpec((3, rows.pad * some, GROUP), lambda j: (0, j, 0))]
        + pieces,
        out_specs=[rows.block(width, some)] * 2 + [whole(outs[2].shape)],
        out_shape=outs,
        compiler_params=params(),
        cost_estimate=cost(7),
        name="project",
    )(vec, base, att, *weight.arrays)


def feed_kernel(place, kind, form, nw, rows, block, carried, norm, grad, vec, *refs):
    w_in, rest = refs[:nw], refs[nw:]
    if carried:
        (acc_in, gn_in), rest = rest[:2], rest[carried:]
    acc_o, gn_o, bias_o = rest[:3]
    j = pl.program_id(0)
    n = 1 if form == "whole" else 2
    grads_o, act_s, gp_s, rest = rest[3 : 3 + n], rest[3 + n], rest[4 + n], rest[5 + n :]
    if kind == "whole":
        w_up, w_down = w_in[0].at[0], w_in[0].at[1]
    else:
        w_up, w_down, rest = *rest[:2], rest[2:]
        r = norm.shape[1] // place.count
        load_weight(place, kind, r, w_in, w_up, 0)
        load_weight(place, kind, r, w_in, w_down, 1)

    @pl.when(j == 0)
    def _():
        if carried:
            acc_o[...] = acc_in[...]
            gn_o[...] = gn_in[...]
        else:
            acc_o[...] = jnp.zeros_like(acc_o)
            gn_o[...] = jnp.zeros_like(gn_o)

    bias = vec[pl.ds(9 + block + j, 1), :]
    step = rows.pad
    for b in range(rows.images):
        at = pl.ds(b * step, step)
        z = dot(norm[at, :], w_up[...]) + bias
        up = dot_cols(grad[at, :], w_down[...])
        act, slope = gelu_and_slope(z)
        act = act.astype(BF16)
        gp = (up * slope).astype(BF16)
        act_s[at, :] = act
        gp_s[at, :] = gp
        acc_o[at, :] += dot(act, w_down[...])
        gn_o[at, :] += dot_cols(gp, w_up[...])
    bias_o[0] = jnp.sum(gp_s[...].astype(F32), axis=0, keepdims=True)
    for i, (left, right) in enumerate(((norm, gp_s), (act_s, grad))):
        value = dot_rows(left[...], right[...]).astype(BF16)
        if form == "whole":
            grads_o[0][i] = value
        else:
            rest[0][...] = value
            store_grad(place, rest[0], *grads_o, i)


def grad_out(kind, blocks, width, r, per_step):
    if kind == "whole":
        return (
            [jax.ShapeDtypeStruct((blocks, width, width), BF16)],
            [pl.BlockSpec((per_step, width, width), lambda j: (j, 0, 0))],
        )
    if kind == "few":
        lead, w = (2, FAR), width
    else:
        lead, w = (2, 2, FAR), width // 2
    zero = (0,) * len(lead)
    return (
        [jax.ShapeDtypeStruct((*lead, blocks, r, w), BF16)] * 2,
        [pl.BlockSpec((*lead, per_step, r, w), lambda j: (*zero, j, 0, 0))] * 2,
    )


def feed_call(place, rows, block, blocks, spot, norm, grad, vec, weight, form, r, carried):
    width = norm.shape[1]
    acc = jax.ShapeDtypeStruct((rows.all, width), F32)
    outs, specs = grad_out(form, 2 * blocks, width, r, 2)
    scratch = [pltpu.VMEM((rows.all, width), BF16)] * 2
    scratch += [pltpu.VMEM((width, width), BF16)] * ((2 if weight.kind != "whole" else 0) + (form != "whole"))
    args = [norm, grad, vec, *weight.arrays, *carried]
    in_specs = [whole(norm.shape), whole(grad.shape), whole(vec.shape)] + piece_specs(weight, 2, spot)
    in_specs += [whole(acc.shape)] * len(carried)
    return pl.pallas_call(
        functools.partial(feed_kernel, place, weight.kind, form, len(weight.arrays), rows, block, len(carried)),
        grid=(blocks,),
        in_specs=in_specs,
        out_specs=[whole(acc.shape)] * 2 + [pl.BlockSpec((1, 1, width), lambda j: (j, 0, 0))] + specs,
        out_shape=[acc, acc, jax.ShapeDtypeStruct((blocks, 1, width), F32)] + outs,
        scratch_shapes=scratch,
        compiler_params=params(),
        cost_estimate=cost(15 * blocks),
        name="feed",
    )(*args)


def middle_kernel(rows, resid, acc, gn, grad, vec, w, out_o, low_o, da_o, sums_o):
    xhat, scale = norm_stats(resid[...])
    gain = vec[6:7, :]
    up = gn[...]
    g = grad[...].astype(F32)
    total = g + norm_back(up, xhat, scale, gain)
    lowered = total.astype(BF16)
    low_o[...] = lowered
    da_o[...] = dot_cols(lowered, w[0]).astype(BF16)
    sums = jnp.concatenate(
        [
            jnp.sum(total, axis=0, keepdims=True),
            jnp.sum(up * xhat, axis=0, keepdims=True),
            jnp.sum(up, axis=0, keepdims=True),
            jnp.sum(g, axis=0, keepdims=True),
        ],
        axis=0,
    )
    final = resid[...] + acc[...] + vec[8:9, :]
    j = pl.program_id(0)
    for i in range(rows.images):

        @pl.when(j == i)
        def _():
            sums_o[...] = sums if i == 0 else sums_o[...] + sums
            out_o[rows.patches * i : rows.patches * (i + 1), :] = final[: rows.patches]


def middle_call(rows, resid, acc, gn, grad, vec, weight):
    width = resid.shape[1]
    block = rows.block(width)
    outs = [
        jax.ShapeDtypeStruct((rows.raw, width), BF16),
        jax.ShapeDtypeStruct((rows.all, width), BF16),
        jax.ShapeDtypeStruct((rows.all, width), BF16),
        jax.ShapeDtypeStruct((4, width), F32),
    ]

    def kernel(resid, acc, gn, grad, vec, w, out_o, low_o, da_o, sums_o, out_s):
        middle_kernel(rows, resid, acc, gn, grad, vec, w, out_s, low_o, da_o, sums_o)

        @pl.when(pl.program_id(0) == rows.images - 1)
        def _():
            out_o[...] = out_s[...].astype(BF16)

    return pl.pallas_call(
        kernel,
        grid=(rows.images,),
        in_specs=[block] * 4 + [whole(vec.shape), whole(weight.shape)],
        out_specs=[whole(outs[0].shape), block, block, whole(outs[3].shape)],
        out_shape=outs,
        scratch_shapes=[pltpu.VMEM((rows.raw, width), F32)],
        compiler_params=params(),
        cost_estimate=cost(12),
        name="middle",
    )(resid, acc, gn, grad, vec, weight)


STEP = 2


def attend_back_kernel(place, kind, rows, projects, norm, da, *refs):
    g, j = pl.program_id(0), pl.program_id(1)
    q_i, k_i, v_i, p_i, refs = *refs[:4], refs[4:]
    if projects:
        (lowered, *atts), refs = refs[: 1 + projects], refs[1 + projects :]
    d_o, bias_o = refs[:2]
    if kind == "whole":
        (grads_o,) = refs[2:]
    else:
        keep, send, g_s = refs[2:]
    s = rows.pad
    some = rows.images // STEP
    first = lax.broadcasted_iota(jnp.int32, (s, 128), 1) < HEAD

    def emit(value, spot):
        if kind == "whole":
            grads_o[spot] = value.astype(BF16)
        else:
            g_s[...] = value.astype(BF16)
            store_grad(place, g_s, keep, send, spot)

    for i in range(some):
        at = pl.ds(i * s, s)
        to = pl.ds(pl.multiple_of((j * some + i) * s, 16), s)
        for p in range(2):
            cols = pl.ds(128 * p, 128)
            q, k, v = q_i[0, at, cols], k_i[0, at, cols], v_i[0, at, cols]
            q2, da2 = halves(q, first), halves(da[at, cols], first)
            low_probs = p_i[0, p, i]
            d_o[0, to, pl.ds(2 * GROUP + 128 * p, 128)] = dot(low_probs, da2).astype(BF16)
            up = dot_cols(v, da2)
            probs = low_probs.astype(F32)
            inner = jnp.sum(probs * up, axis=0, keepdims=True)
            ds = (probs * (up - inner)).astype(BF16)
            d_o[0, to, pl.ds(GROUP + 128 * p, 128)] = dot(ds, q2).astype(BF16)
            dq = dot_rows(ds, k)
            d_o[0, to, cols] = (jnp.where(first, dq[:s], dq[s:]) * 0.125).astype(BF16)

    @pl.when(j == STEP - 1)
    def _():
        if projects:

            @pl.when(g == 0)
            def _():
                both = jnp.concatenate([a[b] for a in atts for b in range(a.shape[0])], axis=1)
                emit(dot_rows(both, lowered[...]), 0)

        bias_o[0] = jnp.sum(d_o[0].astype(F32), axis=0, keepdims=True)
        emit(dot_rows(norm[...], d_o[0]), g + (1 if projects else 0))


def attend_back_call(place, rows, group, groups, norm, q, k, v, probs, da, r, shape="few", project=()):
    width = norm.shape[1]
    s = rows.pad
    some = rows.images // STEP
    row = pl.BlockSpec((1, s * some, GROUP), lambda g, j: (group + g, j, 0))
    in_specs = [whole(norm.shape), pl.BlockSpec((s * some, GROUP), lambda g, j: (j, group + g)), row, row, row]
    in_specs += [pl.BlockSpec((1, 2, some, s, 2 * s), lambda g, j: (group + g, 0, j, 0, 0))]
    in_specs += [whole(a.shape) for a in project]
    kind = shape
    outs, specs = grad_out(kind, groups + (1 if project else 0), width, r, 1)
    specs = [whole(out.shape) for out in outs]
    return pl.pallas_call(
        functools.partial(attend_back_kernel, place, kind, rows, max(len(project) - 1, 0)),
        grid=(groups, STEP),
        in_specs=in_specs,
        out_specs=[
            pl.BlockSpec((1, rows.all, width), lambda g, j: (g, 0, 0)),
            pl.BlockSpec((1, 1, width), lambda g, j: (g, 0, 0)),
        ]
        + specs,
        out_shape=[
            jax.ShapeDtypeStruct((groups, rows.all, width), BF16),
            jax.ShapeDtypeStruct((groups, 1, width), F32),
        ]
        + outs,
        scratch_shapes=[] if kind == "whole" else [pltpu.VMEM((width, width), BF16)],
        compiler_params=params(),
        cost_estimate=cost(11 * groups),
        name="attend_back",
    )(norm, da, q, k, v, probs, *project)


def last_kernel(rows, counts, quarter, count, base, low, flags, vec, w, *refs):
    n = len(counts)
    dqkv, biases, two, feeds, (out_o, late_o, sums_o) = refs[:n], refs[n : 2 * n], refs[2 * n], refs[2 * n + 1 : -3], refs[-3:]
    cols = flag_column(rows, flags)
    gain = vec[1:2, :]
    parts = [d[b] for d, count in zip(dqkv, counts) for b in range(count)]
    up = dot_cols(parts[0], w[0])
    for g in range(1, len(parts)):
        up = up + dot_cols(parts[g], w[g])
    xhat, scale = norm_stats(base[...].astype(F32))
    total = low[...].astype(F32) + norm_back(up, xhat, scale, gain)
    row = lax.broadcasted_iota(jnp.int32, (rows.pad, 1), 0)
    j = pl.program_id(0)
    for i in range(rows.images):

        @pl.when(j == i)
        def _():
            chosen = jnp.logical_and(cols[: rows.pad, i : i + 1] > 0.5, row < rows.patches)
            sums = jnp.concatenate(
                [
                    jnp.sum(jnp.where(chosen, total, 0.0), axis=0, keepdims=True),
                    jnp.sum(up * xhat, axis=0, keepdims=True),
                    jnp.sum(up, axis=0, keepdims=True),
                ],
                axis=0,
            )
            sums_o[...] = sums if i == 0 else sums_o[...] + sums
            out_o[rows.patches * i : rows.patches * (i + 1), :] = jnp.where(chosen, 0.0, total)[: rows.patches]

    @pl.when(j == rows.images - 1)
    def _():
        groups = [b[g] for b, group_count in zip(biases, counts) for g in range(group_count)]
        query = jnp.concatenate([g[:, :GROUP] for g in groups], axis=1)
        value = jnp.concatenate([g[:, 2 * GROUP :] for g in groups], axis=1)
        hidden = [f[b] for f in feeds for b in range(f.shape[0])]
        width = base.shape[1]
        every = jnp.concatenate(
            [sums_o[...], query, value, two[...], *hidden, jnp.zeros((9 - quarter - 2, width), F32)], axis=0
        )
        r = width // count
        for k in range(late_o.shape[0]):
            at = k % count
            late_o[k] = every[:, at * r : (at + 1) * r]


def last_call(rows, count, copies, base, low, flags, vec, w, dqkv, biases, two, feeds):
    width = base.shape[1]
    block = rows.block(width)
    outs = [
        jax.ShapeDtypeStruct((rows.raw, width), F32),
        jax.ShapeDtypeStruct((copies * count, 16, width // count), F32),
    ]
    quarter = sum(f.shape[0] for f in feeds)
    small = [*biases, two, *feeds]
    return pl.pallas_call(
        functools.partial(last_kernel, rows, [d.shape[0] for d in dqkv], quarter, count),
        grid=(rows.images,),
        in_specs=[block, block, whole(flags.shape), whole(vec.shape), whole(w.shape)]
        + [pl.BlockSpec((d.shape[0], rows.pad, width), lambda j: (0, j, 0)) for d in dqkv]
        + [whole(v.shape) for v in small],
        out_specs=[whole(out.shape) for out in outs],
        out_shape=outs,
        scratch_shapes=[pltpu.VMEM((3, width), F32)],
        compiler_params=params(),
        cost_estimate=cost(1500),
        name="last",
    )(base, low, flags, vec, w, *dqkv, *small)


def local(
    count,
    tokens,
    mask_flags,
    mask_token,
    norm1_gain,
    norm1_bias,
    qkv_weight,
    query_bias,
    value_bias,
    proj_weight,
    proj_bias,
    norm2_gain,
    norm2_bias,
    fc1_weight,
    fc1_bias,
    fc2_weight,
    fc2_bias,
    out_grad,
):
    images, patches = mask_flags.shape
    rows = Rows(images, patches)
    r, width = proj_weight.shape
    place = Place(count) if r % 16 == 0 and count == 4 * FAR else None
    quarter = fc1_weight.shape[1] // width

    half = quarter // 2
    vectors = (mask_token, norm1_gain, norm1_bias, query_bias, value_bias, proj_bias, norm2_gain, norm2_bias, fc2_bias)
    kinds = len(vectors) + quarter

    def whole_gather(stack):
        return Weight("whole", [lax.all_gather(stack, "fsdp", axis=1, tiled=True)])

    def whole_scatter(sums):
        share = lax.psum_scatter(sums if place else sums.astype(F32), "fsdp", scatter_dimension=1, tiled=True)
        return share if place else lax.psum(share, "rep")

    flow = Flow()
    pad_in = (tokens, out_grad)
    if place:
        z, x, c = place.own()
        first, second, ff_0, ff_1 = pack_call(count, vectors, fc1_bias, qkv_weight, proj_weight, fc1_weight, fc2_weight)
        flow.begin("wa", gather_fast(place, first))
        pad_in = flow.send(*pad_in)
    else:
        qkv_blocks = qkv_weight.reshape(r, 3, 3, GROUP).transpose(2, 0, 1, 3).reshape(3, r, 3 * GROUP)
        up_blocks = fc1_weight.reshape(r, count, quarter, r).transpose(2, 0, 1, 3).reshape(quarter, r, width)
        down_blocks = fc2_weight.reshape(quarter, r, width)
        ff = jnp.stack([up_blocks, down_blocks], axis=1).reshape(2 * quarter, r, width)
        w_a, w_b = whole_gather(qkv_blocks[:1]), whole_gather(jnp.concatenate([qkv_blocks[1:], proj_weight[None]]))
        w_f0, w_f1 = whole_gather(ff[: 2 * half]), whole_gather(ff[2 * half :])
        small = jnp.concatenate([v[None] for v in vectors] + [fc1_bias.reshape(quarter, r)])
        came = lax.all_gather(small, "fsdp", axis=1, tiled=True)
        came = jnp.pad(came, ((0, 16 - kinds), (0, 0)))
    base, grad = pad_call(rows, *pad_in)
    if place:
        (base,) = flow.meet(["wa"], base)
        flow.begin("wb", gather_wide(place, second))
        flow.begin("wf0", gather_even(place, ff_0))
        (base,) = flow.send(base)
        (base,) = flow.turn(["wa"], base)
        (base,) = flow.meet(["wa"], base)
        w_a = flow.done["wa"]
        came = jnp.stack([part[:, 0, r:, :r] for part in w_a.arrays]).reshape(2, 2, FAR, -1, r)
        came = jnp.where(c == 0, came, came[::-1])
        came = jnp.where(x == 0, came, came[:, ::-1])
        came = jnp.where(z % 2 == 0, came, came.reshape(2, 2, 2, 2, -1, r)[:, :, :, ::-1].reshape(came.shape))
        came = jnp.where(z < 2, came, came.reshape(2, 2, 2, 2, -1, r)[:, :, ::-1].reshape(came.shape))
        came = came.transpose(3, 2, 1, 0, 4)
    vec = came.reshape(16, width).astype(F32)

    base, norm = norm_one_call(rows, base, mask_flags, vec)
    if place:
        norm, ff_1 = flow.meet(["wb"], norm, ff_1)
        w_f1 = whole_gather(ff_1)
        (norm,) = flow.send(norm)
    attends = attend_call(place, rows, 0, 1, norm, vec, w_a)
    if place:
        norm, *attends = flow.turn(["wb", "wf0"], norm, *attends)
        norm, *attends = flow.meet(["wb"], norm, *attends)
        w_b = flow.done["wb"]
    q, k, v, att, probs, wqkv = attend_call(place, rows, 1, 2, norm, vec, w_b, attends)
    if place:
        (att,) = flow.turn(["wf0"], att)
    resid, norm_two, w_proj = project_call(place, rows, vec, base, att, w_b, 2)
    if place:
        (norm_two,) = flow.turn(["wf0"], norm_two)
        (norm_two,) = flow.meet(["wf0"], norm_two)
        w_f0 = flow.done["wf0"]

    form = "wide" if place else "whole"
    acc, gn, gb_0, f0 = feed_call(place, rows, 0, half, 0, norm_two, grad, vec, w_f0, "whole", r, ())
    f0 = whole_scatter(f0)
    acc, gn, gb_1, *f1 = feed_call(place, rows, half, half, 0, norm_two, grad, vec, w_f1, form, r, (acc, gn))
    if place:
        flow.begin("f1", scatter_wide(place, *f1))
        acc, gn = flow.send(acc, gn)

    block_out, lowered, da, sums_two = middle_call(rows, resid, acc, gn, grad, vec, w_proj)
    if place:
        (da,) = flow.turn(["f1"], da)
    dqkv, qs, *sums_c = attend_back_call(
        place, rows, 0, 3, norm, q, k, v, probs, da, r, form, project=[lowered, att]
    )
    if place:
        flow.begin("c", scatter_wide(place, *sums_c))
        dqkv, f0 = flow.meet(["f1"], dqkv, f0)
        flow.begin("f0", send_twin(place, f0))
        (dqkv,) = flow.send(dqkv)
    input_grad, late = last_call(
        rows,
        count,
        2 if place else 1,
        base,
        lowered,
        mask_flags,
        vec,
        wqkv,
        [dqkv],
        [qs],
        sums_two,
        [gb_0, gb_1],
    )
    if place:
        late, input_grad = flow.turn(["c", "f1", "f0"], late, input_grad)
        late = lax.all_to_all(late, ("rep", "fsdp"), 0, 0, tiled=True)
        (late,) = flow.meet(["c"], late)
        flow.begin("fy", send_twin(place, flow.done["f1"]))
        (late,) = flow.send(late)
        (late,) = flow.meet(["c", "fy"], late)
        flow.begin("cy", send_twin(place, flow.done["c"]))
        (late,) = flow.send(late)
        (late,) = flow.meet(["cy"], late)
        shares = late.sum(axis=0)
        sums = [side for name in ("f0", "fy", "cy") for pair in zip(*flow.done[name]) for side in pair]
        g_qkv, g_proj, g_up, g_down = unpack_call(count, quarter, sums)
    else:
        shares = lax.psum(lax.psum_scatter(late, "fsdp", scatter_dimension=0, tiled=True), "rep")[0]
        sums_c = whole_scatter(sums_c[0])
        g_proj = sums_c[0]
        g_qkv = sums_c[1:].reshape(3, r, 3, GROUP).transpose(1, 2, 0, 3).reshape(r, 3 * width)
        g_ff = jnp.concatenate([f0, whole_scatter(f1[0])]).reshape(quarter, 2, r, width)
        g_up = g_ff[:, 0].reshape(quarter, r, count, r).transpose(1, 2, 0, 3).reshape(r, quarter * width)
        g_down = g_ff[:, 1].reshape(quarter * r, width)
    token_s, gain1_s, shift1_s, qb_s, vb_s, pb_s, gain2_s, shift2_s, db_s = [shares[i] for i in range(9)]
    ub_s = shares[9:kinds].reshape(-1)
    return (
        block_out,
        input_grad,
        token_s,
        gain1_s,
        shift1_s,
        g_qkv,
        qb_s,
        vb_s,
        g_proj,
        pb_s,
        gain2_s,
        shift2_s,
        g_up,
        ub_s,
        g_down,
        db_s,
    )


def solution(mesh):
    both, one = P(("rep", "fsdp"), None), P("fsdp")
    flat = P("fsdp", None)
    in_specs = (both, both, one, one, one, flat, one, one, flat, one, one, one, flat, one, flat, one, both)
    out_specs = (both, both, one, one, one, flat, one, one, flat, one, one, one, flat, one, flat, one)
    return jax.shard_map(
        functools.partial(local, mesh.shape["fsdp"]),
        mesh=mesh,
        in_specs=in_specs,
        out_specs=out_specs,
        check_vma=False,
    )
```

```python
import functools
import math

import jax
import jax.numpy as jnp
from jax import lax
from jax.experimental import pallas as pl
from jax.experimental.pallas import tpu as pltpu
from jax.sharding import PartitionSpec as P

F32 = jnp.float32
BF16 = jnp.bfloat16
HEAD = 64
GROUP = 256
NEG = -1e30
VMEM = 56 * 2**20


def dot(a, b):
    return lax.dot_general(a, b, (((1,), (0,)), ((), ())), preferred_element_type=F32)


def dot_rows(a, b):
    return lax.dot_general(a, b, (((0,), (0,)), ((), ())), preferred_element_type=F32)


def dot_cols(a, b):
    return lax.dot_general(a, b, (((1,), (1,)), ((), ())), preferred_element_type=F32)


FAR = 4


class Place:
    def __init__(self, count):
        self.count = count

    def own(self):
        index = lax.axis_index("fsdp")
        return index // 4, (index // 2) % 2, index % 2

    def swap(self, bits):
        return [(i, i ^ bits) for i in range(self.count)]

    def core(self, v):
        return lax.ppermute(v, "fsdp", self.swap(1))

    def along_x(self, v):
        return lax.ppermute(v, "fsdp", self.swap(2))

    def along_z(self, d):
        return lambda v: lax.ppermute(v, "fsdp", self.swap(4 * d))

    def along_y(self, v):
        return lax.ppermute(v, "rep", [(0, 1), (1, 0)])

    def along_xy(self, v):
        n = self.count
        return lax.ppermute(
            v, ("rep", "fsdp"), [(y * n + i, (1 - y) * n + (i ^ 2)) for y in range(2) for i in range(n)]
        )


def shard_at(own, dc, dx, dz):
    z, x, c = own
    return (lax.bitwise_xor(z, dz) * 2 + lax.bitwise_xor(x, dx)) * 2 + lax.bitwise_xor(c, dc)


def add_low(*terms):
    total = terms[0].astype(F32)
    for term in terms[1:]:
        total = total + term.astype(F32)
    return total


def low(v):
    return v.astype(BF16)


def by_side(side, first, second, axis):
    return jnp.where(side == 0, jnp.concatenate([first, second], axis), jnp.concatenate([second, first], axis))


class Weight:
    def __init__(self, kind, arrays):
        self.kind = kind
        self.arrays = arrays


def gather_fast(place, stack):
    came = yield [(place.along_z(d), stack) for d in range(1, FAR)]
    own = jnp.stack([stack] + came)
    beside, own_core = yield [(place.along_x, own), (place.core, own)]
    (beside_core,) = yield [(place.core, beside)]
    return Weight("rows", [own, beside, own_core, beside_core])


def half_columns(stack):
    half = stack.shape[2] // 2
    return lax.dynamic_slice_in_dim(stack, lax.axis_index("rep") * half, half, axis=2)


def gather_wide(place, stack):
    mine = half_columns(stack)
    came = yield [(place.along_z(d), mine) for d in range(1, FAR)]
    own = jnp.stack([mine] + came)
    came = yield [(place.along_x, own), (place.along_y, own), (place.along_xy, own)]
    here = jnp.stack([own] + came)
    (across,) = yield [(place.core, here)]
    return Weight("halves", [here, across])


def gather_even(place, stack):
    mine = half_columns(stack)
    came = yield [(place.along_z(d), mine) for d in range(1, FAR)]
    own = jnp.stack([mine] + came)
    beside, twin = yield [(place.along_x, own), (place.along_y, own)]
    corner = yield [(place.along_y, beside[:2]), (place.along_x, twin[2:])]
    here = jnp.stack([own, beside, twin, jnp.concatenate(corner)])
    (across,) = yield [(place.core, here)]
    return Weight("halves", [here, across])


def gather_late_y(place, stack):
    mine = half_columns(stack)
    came = yield [(place.along_z(d), mine) for d in range(1, FAR)]
    own = jnp.stack([mine] + came)
    (beside,) = yield [(place.along_x, own)]
    side = jnp.stack([own, beside])
    (twin,) = yield [(place.along_y, side)]
    here = jnp.concatenate([side, twin])
    (across,) = yield [(place.core, here)]
    return Weight("halves", [here, across])


def scatter_early_y(place, keep, send):
    (came,) = yield [(place.core, send)]
    (came_y,) = yield [(place.along_y, low(add_low(keep[1], came[1])))]
    (came_x,) = yield [(place.along_x, low(add_low(keep[0, 1], came[0, 1], came_y[1])))]
    total = low(add_low(keep[0, 0], came[0, 0], came_y[0], came_x))
    came = yield [(place.along_z(d), total[d]) for d in range(1, FAR)]
    return low(add_low(total[0], *came))


def scatter_wide(place, keep, send):
    (came,) = yield [(place.core, send)]

    def pair(dy, dx):
        return low(add_low(keep[dy, dx], came[dy, dx]))

    came_xy = yield [(place.along_x, pair(0, 1)), (place.along_y, pair(1, 0)), (place.along_xy, pair(1, 1))]
    total = low(add_low(keep[0, 0], came[0, 0], *came_xy))
    came = yield [(place.along_z(d), total[d]) for d in range(1, FAR)]
    return low(add_low(total[0], *came))


def send_twin(place, *mine):
    twins = yield [(place.along_y, v) for v in mine]
    return list(mine), twins


class Flow:
    def __init__(self):
        self.live = {}
        self.done = {}

    def begin(self, name, steps):
        self.live[name] = (steps, next(steps), None)

    def send(self, *arrays, but=()):
        waiting = [name for name, (_, _, sent) in self.live.items() if sent is None and name not in but]
        flat = [v for name in waiting for _, v in self.live[name][1]]
        flat = list(lax.optimization_barrier(tuple(flat) + tuple(arrays)))
        for name in waiting:
            steps, pairs, _ = self.live[name]
            sent = [move(v) for (move, _), v in zip(pairs, flat)]
            flat = flat[len(pairs) :]
            self.live[name] = (steps, pairs, sent)
        return flat

    def meet(self, names, *arrays):
        names = [name for name in names if name in self.live]
        flat = [v for name in names for v in self.live[name][2]]
        flat = list(lax.optimization_barrier(tuple(flat) + tuple(arrays)))
        for name in names:
            steps, pairs, _ = self.live[name]
            mine, flat = flat[: len(pairs)], flat[len(pairs) :]
            try:
                self.live[name] = (steps, steps.send(mine), None)
            except StopIteration as stop:
                del self.live[name]
                self.done[name] = stop.value
        return flat

    def turn(self, names, *arrays):
        return self.send(*self.meet(names, *arrays))


def half_at(dy, width):
    at = lax.bitwise_xor(lax.axis_index("rep"), dy) * width
    return pl.ds(pl.multiple_of(at, 128), width)


def load_weight(place, kind, rows, refs, spot, lead=0):
    own = place.own()
    for dc in range(2):
        for dx in range(2):
            for d in range(FAR):
                at = pl.ds(pl.multiple_of(shard_at(own, dc, dx, d) * rows, 16), rows)
                if kind == "rows":
                    spot[at, :] = refs[2 * dc + dx][d, lead, :rows]
                else:
                    for dy in range(2):
                        spot[at, half_at(dy, refs[0].shape[-1])] = refs[dc][2 * dy + dx, d, lead]


def store_grad(place, spot, keep, send, lead=0):
    own = place.own()
    rows, width = keep.shape[-2:]
    for dc, ref in enumerate((keep, send)):
        for dx in range(2):
            for d in range(FAR):
                at = pl.ds(pl.multiple_of(shard_at(own, dc, dx, d) * rows, 16), rows)
                if len(keep.shape) == 5:
                    ref[dx, d, lead] = spot[at, :]
                else:
                    for dy in range(2):
                        ref[dy, dx, d, lead] = spot[at, half_at(dy, width)]


def norm_stats(v):
    mean = jnp.mean(v, axis=-1, keepdims=True)
    centred = v - mean
    spread = jnp.mean(centred * centred, axis=-1, keepdims=True)
    scale = lax.rsqrt(spread + 1e-06)
    return centred * scale, scale


def norm_back(up, xhat, scale, gain):
    e = up * gain
    return (e - jnp.mean(e, axis=-1, keepdims=True) - xhat * jnp.mean(e * xhat, axis=-1, keepdims=True)) * scale


ERF_P = 0.3275911 / math.sqrt(2.0)
ERF_A = (0.254829592, -0.284496736, 1.421413741, -1.453152027, 1.061405429)


def gelu_and_slope(z):
    t = 1.0 / (1.0 + ERF_P * jnp.abs(z))
    e = jnp.exp(-0.5 * (z * z))
    poly = 0.5 * ERF_A[4]
    for a in ERF_A[3::-1]:
        poly = poly * t + 0.5 * a
    q = poly * t * e
    phi = jnp.where(z > 0, 1.0 - q, q)
    return z * phi, phi + z * (e * (1.0 / math.sqrt(2.0 * math.pi)))


class Rows:
    def __init__(self, images, patches):
        self.images = images
        self.patches = patches
        self.pad = -(-patches // 16) * 16
        self.all = images * self.pad
        self.raw = images * patches

    def block(self, width, count=1):
        return pl.BlockSpec((self.pad * count, width), lambda j: (j, 0))


def flag_column(rows, flags):
    wide = flags[...].astype(F32)
    wide = jnp.concatenate([wide, jnp.zeros((8 - rows.images, rows.patches), F32)], axis=0)
    gap = -rows.patches % 128
    return jnp.concatenate([wide, jnp.zeros((8, gap), F32)], axis=1).T


def padded_image(rows, ref, i):
    lo = rows.patches * i
    first = lo // 16 * 16
    last = min(-(-(lo + rows.patches) // 16) * 16, rows.raw)
    part = ref[first:last, :].astype(F32)[lo - first : lo - first + rows.patches]
    return jnp.concatenate([part, jnp.zeros((rows.pad - rows.patches, ref.shape[1]), F32)], axis=0)


def pad_kernel(rows, tokens, grads, base_o, grad_o):
    j = pl.program_id(0)

    def image(i):
        base_o[...] = padded_image(rows, tokens, i).astype(BF16)
        grad_o[...] = padded_image(rows, grads, i).astype(BF16)

    for i in range(rows.images):
        pl.when(j == i)(functools.partial(image, i))


def norm_one_kernel(rows, tokens, flags, vec, base_o, norm_o):
    cols = flag_column(rows, flags)
    row = lax.broadcasted_iota(jnp.int32, (rows.pad, 1), 0)
    for i in range(rows.images):
        at = pl.ds(i * rows.pad, rows.pad)
        masked = jnp.logical_and(cols[: rows.pad, i : i + 1] > 0.5, row < rows.patches)
        base = jnp.where(masked, vec[0:1, :], tokens[at, :].astype(F32))
        base_o[at, :] = base.astype(BF16)
        xhat, _ = norm_stats(base)
        norm_o[at, :] = (xhat * vec[1:2, :] + vec[2:3, :]).astype(BF16)


def whole(shape):
    return pl.BlockSpec(shape, lambda *j: (0,) * len(shape))


def params():
    return pltpu.CompilerParams(vmem_limit_bytes=VMEM)


SCALE = 0.01


def cost(micros):
    return pl.CostEstimate(flops=int(micros * SCALE * 1.15e9), bytes_accessed=int(micros * SCALE * 3e6), transcendentals=0)


def pad_call(rows, tokens, grads):
    width = tokens.shape[1]
    out = jax.ShapeDtypeStruct((rows.all, width), BF16)
    return pl.pallas_call(
        functools.partial(pad_kernel, rows),
        grid=(rows.images,),
        in_specs=[whole(tokens.shape), whole(grads.shape)],
        out_specs=[rows.block(width)] * 2,
        out_shape=[out, out],
        compiler_params=params(),
        cost_estimate=cost(5),
        name="pad_rows",
    )(tokens, grads)


def norm_one_call(rows, tokens, flags, vec):
    out = jax.ShapeDtypeStruct(tokens.shape, BF16)
    return pl.pallas_call(
        functools.partial(norm_one_kernel, rows),
        out_shape=[out, out],
        compiler_params=params(),
        cost_estimate=cost(5),
        name="norm_one",
    )(tokens, flags, vec)


def pack_kernel(count, quarter, *refs):
    *vectors, wide, qkv, proj, up, down = refs[: -2 - quarter // 2]
    first_o, second_o, *ff_o = refs[-2 - quarter // 2 :]
    r, width = proj.shape

    def group(g):
        return [qkv[:, i * width + g * GROUP : i * width + (g + 1) * GROUP] for i in range(3)]

    for i, part in enumerate(group(0)):
        first_o[0, :r, i * GROUP : (i + 1) * GROUP] = part
    small = [v[...].astype(F32) for v in vectors]
    small += [wide[:, r * i : r * (i + 1)].astype(F32) for i in range(quarter)]
    small = jnp.concatenate(small + [jnp.zeros((16 - len(small), r), F32)], axis=0)
    first_o[0, r:, :] = jnp.concatenate([small, jnp.zeros((16, width - r), F32)], axis=1).astype(BF16)
    for g in (1, 2):
        for i, part in enumerate(group(g)):
            second_o[g - 1, :, i * GROUP : (i + 1) * GROUP] = part
    second_o[2] = proj[...]
    for t in range(quarter):
        out = ff_o[t // 2]
        cols = [up[:, (k * quarter + t) * r : (k * quarter + t + 1) * r] for k in range(count)]
        out[t % 2 * 2] = jnp.concatenate(cols, axis=1)
        out[t % 2 * 2 + 1] = down[t * r : (t + 1) * r, :]


def pack_call(count, vectors, wide, qkv, proj, up, down):
    r, width = proj.shape
    quarter = up.shape[1] // width
    shapes = [(1, r + 16, width), (3, r, width)] + [(4, r, width)] * (quarter // 2)
    return pl.pallas_call(
        functools.partial(pack_kernel, count, quarter),
        out_shape=[jax.ShapeDtypeStruct(shape, BF16) for shape in shapes],
        compiler_params=params(),
        cost_estimate=cost(2.5),
        name="pack",
    )(*[v[None] for v in vectors], wide[None], qkv, proj, up, down)


def unpack_kernel(count, quarter, *refs):
    sums, (qkv_o, proj_o, up_o, down_o) = refs[:6], refs[6:]
    r = proj_o.shape[0]
    width = proj_o.shape[1]

    def added(k):
        return [sums[2 * k][b].astype(F32) + sums[2 * k + 1][b].astype(F32) for b in range(sums[2 * k].shape[0])]

    def joined(k):
        out = []
        for b in range(sums[2 * k].shape[0]):
            mine, twin = sums[2 * k][b].astype(F32), sums[2 * k + 1][b].astype(F32)
            here = jnp.concatenate([mine, twin], axis=1)
            there = jnp.concatenate([twin, mine], axis=1)
            out.append(jnp.where(lax.axis_index("rep") == 0, here, there))
        return out

    ff = added(0) + joined(1)
    heads = joined(2)
    proj_o[...] = heads[0]
    for g in range(3):
        for i in range(3):
            qkv_o[:, i * width + g * GROUP : i * width + (g + 1) * GROUP] = heads[1 + g][:, i * GROUP : (i + 1) * GROUP]
    ups = [ff[2 * t] for t in range(quarter)]
    up_o[...] = jnp.concatenate([ups[t][:, k * r : (k + 1) * r] for k in range(count) for t in range(quarter)], axis=1)
    for t in range(quarter):
        down_o[t * r : (t + 1) * r, :] = ff[2 * t + 1]


def unpack_call(count, quarter, sums):
    r, width = sums[0].shape[1:]
    shapes = [(r, 3 * width), (r, width), (r, quarter * width), (quarter * r, width)]
    return pl.pallas_call(
        functools.partial(unpack_kernel, count, quarter),
        out_shape=[jax.ShapeDtypeStruct(shape, F32) for shape in shapes],
        compiler_params=params(),
        cost_estimate=cost(3),
        name="unpack",
    )(*sums)


def halves(x, first):
    zero = jnp.zeros_like(x)
    return jnp.concatenate([jnp.where(first, x, zero), jnp.where(first, zero, x)], axis=0)


def attend_kernel(place, kind, nw, before, rows, base_group, norm, vec, *refs):
    w_in, (q_o, k_o, v_o, att_o, p_o, w_o) = refs[:nw], refs[nw + before :]
    j = pl.program_id(0)
    w = w_o.at[0]
    if kind == "whole":
        w[...] = w_in[0][0]
    else:
        load_weight(place, kind, norm.shape[1] // place.count, w_in, w)
    x = norm[...]
    lanes = pl.ds(pl.multiple_of((base_group + j) * GROUP, GROUP), GROUP)
    q_o[0] = ((dot(x, w[:, 0:GROUP]) + vec[3:4, lanes]).astype(BF16) * 0.125).astype(BF16)
    k_o[0] = dot(x, w[:, GROUP : 2 * GROUP]).astype(BF16)
    v_o[0] = (dot(x, w[:, 2 * GROUP :]) + vec[4:5, lanes]).astype(BF16)
    s = rows.pad
    first = lax.broadcasted_iota(jnp.int32, (s, 128), 1) < HEAD
    live = lax.broadcasted_iota(jnp.int32, (s, 2 * s), 0) < rows.patches

    def image(i):
        at = pl.ds(pl.multiple_of(i * s, 16), s)
        for p in range(2):
            cols = pl.ds(128 * p, 128)
            q, k, v = q_o[0, at, cols], k_o[0, at, cols], v_o[0, at, cols]
            score = jnp.where(live, dot_cols(k, halves(q, first)), NEG)
            peak = jnp.max(score, axis=0, keepdims=True)
            e = jnp.exp(score - peak)
            probs = (e * (1.0 / jnp.sum(e, axis=0, keepdims=True))).astype(BF16)
            p_o[0, p, i] = probs
            o = dot_rows(probs, v)
            att_o[0, at, cols] = jnp.where(first, o[:s], o[s:]).astype(BF16)

    def step(i, carry):
        for u in range(3):
            image(i * 3 + u)
        return carry

    lax.fori_loop(0, rows.images // 3, step, 0)


def piece_specs(weight, blocks=1, first=0):
    if weight.kind == "whole":
        return [pl.BlockSpec((blocks, *weight.arrays[0].shape[1:]), lambda j: (first + j, 0, 0))]
    if weight.kind == "rows":
        z, _, r, w = weight.arrays[0].shape
        return [pl.BlockSpec((z, blocks, r, w), lambda j: (0, first + j, 0, 0))] * 4
    k, z, _, r, w = weight.arrays[0].shape
    return [pl.BlockSpec((k, z, blocks, r, w), lambda j: (0, 0, first + j, 0, 0))] * 2


def attend_call(place, rows, group, groups, norm, vec, weight, before=()):
    s = rows.pad
    width = norm.shape[1]
    row = pl.BlockSpec((1, rows.all, GROUP), lambda j: (group + j, 0, 0))
    out = jax.ShapeDtypeStruct((3, rows.all, GROUP), BF16)
    outs = [out] * 4 + [jax.ShapeDtypeStruct((3, 2, rows.images, s, 2 * s), BF16)]
    specs = [row] * 4 + [pl.BlockSpec((1, 2, rows.images, s, 2 * s), lambda j: (group + j, 0, 0, 0, 0))]
    outs.append(jax.ShapeDtypeStruct((3, width, 3 * GROUP), BF16))
    specs.append(pl.BlockSpec((1, width, 3 * GROUP), lambda j: (group + j, 0, 0)))
    args = [norm, vec, *weight.arrays, *before]
    first = len(args) - len(before)
    return pl.pallas_call(
        functools.partial(attend_kernel, place, weight.kind, len(weight.arrays), len(before), rows, group),
        grid=(groups,),
        in_specs=[whole(norm.shape), whole(vec.shape)]
        + piece_specs(weight)
        + [pl.BlockSpec(memory_space=pl.ANY)] * len(before),
        out_specs=specs,
        out_shape=outs,
        input_output_aliases={first + i: i for i in range(len(before))},
        compiler_params=params(),
        cost_estimate=cost(2 + 6 * groups),
        name="attend",
    )(*args)


def project_kernel(place, kind, nw, spot, vec, base, att, *refs):
    w_in, (resid_o, norm_o, w_o) = refs[:nw], refs[nw:]

    @pl.when(pl.program_id(0) == 0)
    def _():
        if kind == "whole":
            w_o[0] = w_in[0][0]
        else:
            load_weight(place, kind, base.shape[1] // place.count, w_in, w_o.at[0])

    both = jnp.concatenate([att[g] for g in range(att.shape[0])], axis=1)
    total = dot(both, w_o[0]) + base[...].astype(F32) + vec[5:6, :]
    resid_o[...] = total
    xhat, _ = norm_stats(total)
    norm_o[...] = (xhat * vec[6:7, :] + vec[7:8, :]).astype(BF16)


def project_call(place, rows, vec, base, att, weight, spot):
    width = base.shape[1]
    outs = [
        jax.ShapeDtypeStruct((rows.all, width), F32),
        jax.ShapeDtypeStruct((rows.all, width), BF16),
        jax.ShapeDtypeStruct((1, width, width), BF16),
    ]
    some = rows.images // 3
    pieces = [
        pl.BlockSpec(block.block_shape, lambda j, at=block.index_map(0): at)
        for block in piece_specs(weight, 1, spot)
    ]
    return pl.pallas_call(
        functools.partial(project_kernel, place, weight.kind, len(weight.arrays), spot),
        grid=(3,),
        in_specs=[whole(vec.shape), rows.block(width, some)]
        + [pl.BlockSpec((3, rows.pad * some, GROUP), lambda j: (0, j, 0))]
        + pieces,
        out_specs=[rows.block(width, some)] * 2 + [whole(outs[2].shape)],
        out_shape=outs,
        compiler_params=params(),
        cost_estimate=cost(7),
        name="project",
    )(vec, base, att, *weight.arrays)


def feed_kernel(place, kind, form, nw, rows, block, carried, norm, grad, vec, *refs):
    w_in, rest = refs[:nw], refs[nw:]
    if carried:
        (acc_in, gn_in), rest = rest[:2], rest[carried:]
    acc_o, gn_o, bias_o = rest[:3]
    j = pl.program_id(0)
    n = 1 if form == "whole" else 2
    grads_o, act_s, gp_s, rest = rest[3 : 3 + n], rest[3 + n], rest[4 + n], rest[5 + n :]
    if kind == "whole":
        w_up, w_down = w_in[0].at[0], w_in[0].at[1]
    else:
        w_up, w_down, rest = *rest[:2], rest[2:]
        r = norm.shape[1] // place.count
        load_weight(place, kind, r, w_in, w_up, 0)
        load_weight(place, kind, r, w_in, w_down, 1)

    @pl.when(j == 0)
    def _():
        if carried:
            acc_o[...] = acc_in[...]
            gn_o[...] = gn_in[...]
        else:
            acc_o[...] = jnp.zeros_like(acc_o)
            gn_o[...] = jnp.zeros_like(gn_o)

    bias = vec[pl.ds(9 + block + j, 1), :]
    step = rows.pad
    for b in range(rows.images):
        at = pl.ds(b * step, step)
        z = dot(norm[at, :], w_up[...]) + bias
        up = dot_cols(grad[at, :], w_down[...])
        act, slope = gelu_and_slope(z)
        act = act.astype(BF16)
        gp = (up * slope).astype(BF16)
        act_s[at, :] = act
        gp_s[at, :] = gp
        acc_o[at, :] += dot(act, w_down[...])
        gn_o[at, :] += dot_cols(gp, w_up[...])
    bias_o[0] = jnp.sum(gp_s[...].astype(F32), axis=0, keepdims=True)
    for i, (left, right) in enumerate(((norm, gp_s), (act_s, grad))):
        value = dot_rows(left[...], right[...]).astype(BF16)
        if form == "whole":
            grads_o[0][i] = value
        else:
            rest[0][...] = value
            store_grad(place, rest[0], *grads_o, i)


def grad_out(kind, blocks, width, r, per_step):
    if kind == "whole":
        return (
            [jax.ShapeDtypeStruct((blocks, width, width), BF16)],
            [pl.BlockSpec((per_step, width, width), lambda j: (j, 0, 0))],
        )
    if kind == "few":
        lead, w = (2, FAR), width
    else:
        lead, w = (2, 2, FAR), width // 2
    zero = (0,) * len(lead)
    return (
        [jax.ShapeDtypeStruct((*lead, blocks, r, w), BF16)] * 2,
        [pl.BlockSpec((*lead, per_step, r, w), lambda j: (*zero, j, 0, 0))] * 2,
    )


def feed_call(place, rows, block, blocks, spot, norm, grad, vec, weight, form, r, carried):
    width = norm.shape[1]
    acc = jax.ShapeDtypeStruct((rows.all, width), F32)
    outs, specs = grad_out(form, 2 * blocks, width, r, 2)
    scratch = [pltpu.VMEM((rows.all, width), BF16)] * 2
    scratch += [pltpu.VMEM((width, width), BF16)] * ((2 if weight.kind != "whole" else 0) + (form != "whole"))
    args = [norm, grad, vec, *weight.arrays, *carried]
    in_specs = [whole(norm.shape), whole(grad.shape), whole(vec.shape)] + piece_specs(weight, 2, spot)
    in_specs += [whole(acc.shape)] * len(carried)
    return pl.pallas_call(
        functools.partial(feed_kernel, place, weight.kind, form, len(weight.arrays), rows, block, len(carried)),
        grid=(blocks,),
        in_specs=in_specs,
        out_specs=[whole(acc.shape)] * 2 + [pl.BlockSpec((1, 1, width), lambda j: (j, 0, 0))] + specs,
        out_shape=[acc, acc, jax.ShapeDtypeStruct((blocks, 1, width), F32)] + outs,
        scratch_shapes=scratch,
        compiler_params=params(),
        cost_estimate=cost(15 * blocks),
        name="feed",
    )(*args)


PAIR = 2


def middle_kernel(rows, resid, acc, gn, grad, vec, w, out_o, low_o, da_o, sums_o):
    xhat, scale = norm_stats(resid[...])
    gain = vec[6:7, :]
    up = gn[...]
    g = grad[...].astype(F32)
    total = g + norm_back(up, xhat, scale, gain)
    lowered = total.astype(BF16)
    low_o[...] = lowered
    da_o[...] = dot_cols(lowered, w[0]).astype(BF16)
    sums = jnp.concatenate(
        [
            jnp.sum(total, axis=0, keepdims=True),
            jnp.sum(up * xhat, axis=0, keepdims=True),
            jnp.sum(up, axis=0, keepdims=True),
            jnp.sum(g, axis=0, keepdims=True),
        ],
        axis=0,
    )
    final = resid[...] + acc[...] + vec[8:9, :]
    j = pl.program_id(0)
    for i in range(rows.images // PAIR):

        @pl.when(j == i)
        def _():
            sums_o[...] = sums if i == 0 else sums_o[...] + sums
            for u in range(PAIR):
                lo = rows.patches * (PAIR * i + u)
                out_o[lo : lo + rows.patches, :] = final[rows.pad * u : rows.pad * u + rows.patches]


def middle_call(rows, resid, acc, gn, grad, vec, weight):
    width = resid.shape[1]
    block = rows.block(width, PAIR)
    outs = [
        jax.ShapeDtypeStruct((rows.raw, width), BF16),
        jax.ShapeDtypeStruct((rows.all, width), BF16),
        jax.ShapeDtypeStruct((rows.all, width), BF16),
        jax.ShapeDtypeStruct((4, width), F32),
    ]

    def kernel(resid, acc, gn, grad, vec, w, out_o, low_o, da_o, sums_o, out_s):
        middle_kernel(rows, resid, acc, gn, grad, vec, w, out_s, low_o, da_o, sums_o)

        @pl.when(pl.program_id(0) == rows.images // PAIR - 1)
        def _():
            out_o[...] = out_s[...].astype(BF16)

    return pl.pallas_call(
        kernel,
        grid=(rows.images // PAIR,),
        in_specs=[block] * 4 + [whole(vec.shape), whole(weight.shape)],
        out_specs=[whole(outs[0].shape), block, block, whole(outs[3].shape)],
        out_shape=outs,
        scratch_shapes=[pltpu.VMEM((rows.raw, width), F32)],
        compiler_params=params(),
        cost_estimate=cost(12),
        name="middle",
    )(resid, acc, gn, grad, vec, weight)


STEP = 2


def attend_back_kernel(place, kind, rows, projects, norm, da, *refs):
    g, j = pl.program_id(0), pl.program_id(1)
    q_i, k_i, v_i, p_i, refs = *refs[:4], refs[4:]
    if projects:
        (lowered, *atts), refs = refs[: 1 + projects], refs[1 + projects :]
    d_o, bias_o = refs[:2]
    if kind == "whole":
        (grads_o,) = refs[2:]
    else:
        keep, send, g_s = refs[2:]
    s = rows.pad
    some = rows.images // STEP
    first = lax.broadcasted_iota(jnp.int32, (s, 128), 1) < HEAD

    def emit(value, spot):
        if kind == "whole":
            grads_o[spot] = value.astype(BF16)
        else:
            g_s[...] = value.astype(BF16)
            store_grad(place, g_s, keep, send, spot)

    for i in range(some):
        at = pl.ds(i * s, s)
        to = pl.ds(pl.multiple_of((j * some + i) * s, 16), s)
        for p in range(2):
            cols = pl.ds(128 * p, 128)
            q, k, v = q_i[0, at, cols], k_i[0, at, cols], v_i[0, at, cols]
            q2, da2 = halves(q, first), halves(da[at, cols], first)
            low_probs = p_i[0, p, i]
            d_o[0, to, pl.ds(2 * GROUP + 128 * p, 128)] = dot(low_probs, da2).astype(BF16)
            up = dot_cols(v, da2)
            probs = low_probs.astype(F32)
            inner = jnp.sum(probs * up, axis=0, keepdims=True)
            ds = (probs * (up - inner)).astype(BF16)
            d_o[0, to, pl.ds(GROUP + 128 * p, 128)] = dot(ds, q2).astype(BF16)
            dq = dot_rows(ds, k)
            d_o[0, to, cols] = (jnp.where(first, dq[:s], dq[s:]) * 0.125).astype(BF16)

    @pl.when(j == STEP - 1)
    def _():
        if projects:

            @pl.when(g == 0)
            def _():
                both = jnp.concatenate([a[b] for a in atts for b in range(a.shape[0])], axis=1)
                emit(dot_rows(both, lowered[...]), 0)

        bias_o[0] = jnp.sum(d_o[0].astype(F32), axis=0, keepdims=True)
        emit(dot_rows(norm[...], d_o[0]), g + (1 if projects else 0))


def attend_back_call(place, rows, group, groups, norm, q, k, v, probs, da, r, shape="few", project=()):
    width = norm.shape[1]
    s = rows.pad
    some = rows.images // STEP
    row = pl.BlockSpec((1, s * some, GROUP), lambda g, j: (group + g, j, 0))
    in_specs = [whole(norm.shape), pl.BlockSpec((s * some, GROUP), lambda g, j: (j, group + g)), row, row, row]
    in_specs += [pl.BlockSpec((1, 2, some, s, 2 * s), lambda g, j: (group + g, 0, j, 0, 0))]
    in_specs += [whole(a.shape) for a in project]
    kind = shape
    outs, specs = grad_out(kind, groups + (1 if project else 0), width, r, 1)
    specs = [whole(out.shape) for out in outs]
    return pl.pallas_call(
        functools.partial(attend_back_kernel, place, kind, rows, max(len(project) - 1, 0)),
        grid=(groups, STEP),
        in_specs=in_specs,
        out_specs=[
            pl.BlockSpec((1, rows.all, width), lambda g, j: (g, 0, 0)),
            pl.BlockSpec((1, 1, width), lambda g, j: (g, 0, 0)),
        ]
        + specs,
        out_shape=[
            jax.ShapeDtypeStruct((groups, rows.all, width), BF16),
            jax.ShapeDtypeStruct((groups, 1, width), F32),
        ]
        + outs,
        scratch_shapes=[] if kind == "whole" else [pltpu.VMEM((width, width), BF16)],
        compiler_params=params(),
        cost_estimate=cost(11 * groups),
        name="attend_back",
    )(norm, da, q, k, v, probs, *project)


def last_kernel(rows, counts, quarter, count, base, low, flags, vec, w, *refs):
    n = len(counts)
    dqkv, biases, two, feeds, (out_o, late_o, sums_o) = refs[:n], refs[n : 2 * n], refs[2 * n], refs[2 * n + 1 : -3], refs[-3:]
    cols = flag_column(rows, flags)
    gain = vec[1:2, :]
    parts = [d[b] for d, count in zip(dqkv, counts) for b in range(count)]
    up = dot_cols(parts[0], w[0])
    for g in range(1, len(parts)):
        up = up + dot_cols(parts[g], w[g])
    xhat, scale = norm_stats(base[...].astype(F32))
    total = low[...].astype(F32) + norm_back(up, xhat, scale, gain)
    row = lax.broadcasted_iota(jnp.int32, (rows.pad, 1), 0)
    j = pl.program_id(0)
    for i in range(rows.images // PAIR):

        @pl.when(j == i)
        def _():
            flagged = [
                jnp.logical_and(cols[: rows.pad, PAIR * i + u : PAIR * i + u + 1] > 0.5, row < rows.patches)
                for u in range(PAIR)
            ]
            chosen = jnp.concatenate([jnp.where(f, 1.0, 0.0) for f in flagged], axis=0) > 0.5
            sums = jnp.concatenate(
                [
                    jnp.sum(jnp.where(chosen, total, 0.0), axis=0, keepdims=True),
                    jnp.sum(up * xhat, axis=0, keepdims=True),
                    jnp.sum(up, axis=0, keepdims=True),
                ],
                axis=0,
            )
            sums_o[...] = sums if i == 0 else sums_o[...] + sums
            kept = jnp.where(chosen, 0.0, total)
            for u in range(PAIR):
                lo = rows.patches * (PAIR * i + u)
                out_o[lo : lo + rows.patches, :] = kept[rows.pad * u : rows.pad * u + rows.patches]

    @pl.when(j == rows.images // PAIR - 1)
    def _():
        groups = [b[g] for b, group_count in zip(biases, counts) for g in range(group_count)]
        query = jnp.concatenate([g[:, :GROUP] for g in groups], axis=1)
        value = jnp.concatenate([g[:, 2 * GROUP :] for g in groups], axis=1)
        hidden = [f[b] for f in feeds for b in range(f.shape[0])]
        width = base.shape[1]
        every = jnp.concatenate(
            [sums_o[...], query, value, two[...], *hidden, jnp.zeros((9 - quarter - 2, width), F32)], axis=0
        )
        r = width // count
        for k in range(late_o.shape[0]):
            at = k % count
            late_o[k] = every[:, at * r : (at + 1) * r]


def last_call(rows, count, copies, base, low, flags, vec, w, dqkv, biases, two, feeds):
    width = base.shape[1]
    block = rows.block(width, PAIR)
    outs = [
        jax.ShapeDtypeStruct((rows.raw, width), F32),
        jax.ShapeDtypeStruct((copies * count, 16, width // count), F32),
    ]
    quarter = sum(f.shape[0] for f in feeds)
    small = [*biases, two, *feeds]
    return pl.pallas_call(
        functools.partial(last_kernel, rows, [d.shape[0] for d in dqkv], quarter, count),
        grid=(rows.images // PAIR,),
        in_specs=[block, block, whole(flags.shape), whole(vec.shape), whole(w.shape)]
        + [pl.BlockSpec((d.shape[0], PAIR * rows.pad, width), lambda j: (0, j, 0)) for d in dqkv]
        + [whole(v.shape) for v in small],
        out_specs=[whole(out.shape) for out in outs],
        out_shape=outs,
        scratch_shapes=[pltpu.VMEM((3, width), F32)],
        compiler_params=params(),
        cost_estimate=cost(1500),
        name="last",
    )(base, low, flags, vec, w, *dqkv, *small)


def local(
    count,
    tokens,
    mask_flags,
    mask_token,
    norm1_gain,
    norm1_bias,
    qkv_weight,
    query_bias,
    value_bias,
    proj_weight,
    proj_bias,
    norm2_gain,
    norm2_bias,
    fc1_weight,
    fc1_bias,
    fc2_weight,
    fc2_bias,
    out_grad,
):
    images, patches = mask_flags.shape
    rows = Rows(images, patches)
    r, width = proj_weight.shape
    place = Place(count) if r % 16 == 0 and count == 4 * FAR else None
    quarter = fc1_weight.shape[1] // width

    half = quarter // 2
    vectors = (mask_token, norm1_gain, norm1_bias, query_bias, value_bias, proj_bias, norm2_gain, norm2_bias, fc2_bias)
    kinds = len(vectors) + quarter

    def whole_gather(stack):
        return Weight("whole", [lax.all_gather(stack, "fsdp", axis=1, tiled=True)])

    def whole_scatter(sums):
        share = lax.psum_scatter(sums if place else sums.astype(F32), "fsdp", scatter_dimension=1, tiled=True)
        return share if place else lax.psum(share, "rep")

    flow = Flow()
    pad_in = (tokens, out_grad)
    if place:
        z, x, c = place.own()
        first, second, ff_0, ff_1 = pack_call(count, vectors, fc1_bias, qkv_weight, proj_weight, fc1_weight, fc2_weight)
        flow.begin("wa", gather_fast(place, first))
        pad_in = flow.send(*pad_in)
    else:
        qkv_blocks = qkv_weight.reshape(r, 3, 3, GROUP).transpose(2, 0, 1, 3).reshape(3, r, 3 * GROUP)
        up_blocks = fc1_weight.reshape(r, count, quarter, r).transpose(2, 0, 1, 3).reshape(quarter, r, width)
        down_blocks = fc2_weight.reshape(quarter, r, width)
        ff = jnp.stack([up_blocks, down_blocks], axis=1).reshape(2 * quarter, r, width)
        w_a, w_b = whole_gather(qkv_blocks[:1]), whole_gather(jnp.concatenate([qkv_blocks[1:], proj_weight[None]]))
        w_f0, w_f1 = whole_gather(ff[: 2 * half]), whole_gather(ff[2 * half :])
        small = jnp.concatenate([v[None] for v in vectors] + [fc1_bias.reshape(quarter, r)])
        came = lax.all_gather(small, "fsdp", axis=1, tiled=True)
        came = jnp.pad(came, ((0, 16 - kinds), (0, 0)))
    base, grad = pad_call(rows, *pad_in)
    if place:
        (base,) = flow.meet(["wa"], base)
        flow.begin("wb", gather_wide(place, second))
        flow.begin("wf0", gather_even(place, ff_0))
        (base,) = flow.send(base)
        (base,) = flow.turn(["wa"], base)
        (base,) = flow.meet(["wa"], base)
        w_a = flow.done["wa"]
        came = jnp.stack([part[:, 0, r:, :r] for part in w_a.arrays]).reshape(2, 2, FAR, -1, r)
        came = jnp.where(c == 0, came, came[::-1])
        came = jnp.where(x == 0, came, came[:, ::-1])
        came = jnp.where(z % 2 == 0, came, came.reshape(2, 2, 2, 2, -1, r)[:, :, :, ::-1].reshape(came.shape))
        came = jnp.where(z < 2, came, came.reshape(2, 2, 2, 2, -1, r)[:, :, ::-1].reshape(came.shape))
        came = came.transpose(3, 2, 1, 0, 4)
    vec = came.reshape(16, width).astype(F32)

    base, norm = norm_one_call(rows, base, mask_flags, vec)
    if place:
        norm, ff_1 = flow.meet(["wb"], norm, ff_1)
        w_f1 = whole_gather(ff_1)
        (norm,) = flow.send(norm)
    attends = attend_call(place, rows, 0, 1, norm, vec, w_a)
    if place:
        norm, *attends = flow.turn(["wb", "wf0"], norm, *attends)
        norm, *attends = flow.meet(["wb"], norm, *attends)
        w_b = flow.done["wb"]
    q, k, v, att, probs, wqkv = attend_call(place, rows, 1, 2, norm, vec, w_b, attends)
    if place:
        (att,) = flow.turn(["wf0"], att)
    resid, norm_two, w_proj = project_call(place, rows, vec, base, att, w_b, 2)
    if place:
        (norm_two,) = flow.turn(["wf0"], norm_two)
        (norm_two,) = flow.meet(["wf0"], norm_two)
        w_f0 = flow.done["wf0"]

    form = "wide" if place else "whole"
    acc, gn, gb_0, f0 = feed_call(place, rows, 0, half, 0, norm_two, grad, vec, w_f0, "whole", r, ())
    f0 = whole_scatter(f0)
    acc, gn, gb_1, *f1 = feed_call(place, rows, half, half, 0, norm_two, grad, vec, w_f1, form, r, (acc, gn))
    if place:
        flow.begin("f1", scatter_wide(place, *f1))
        acc, gn = flow.send(acc, gn)

    block_out, lowered, da, sums_two = middle_call(rows, resid, acc, gn, grad, vec, w_proj)
    if place:
        (da,) = flow.turn(["f1"], da)
    dqkv, qs, *sums_c = attend_back_call(
        place, rows, 0, 3, norm, q, k, v, probs, da, r, form, project=[lowered, att]
    )
    if place:
        flow.begin("c", scatter_wide(place, *sums_c))
        dqkv, f0 = flow.meet(["f1"], dqkv, f0)
        flow.begin("f0", send_twin(place, f0))
        (dqkv,) = flow.send(dqkv, but=("f1",))
    input_grad, late = last_call(
        rows,
        count,
        2 if place else 1,
        base,
        lowered,
        mask_flags,
        vec,
        wqkv,
        [dqkv],
        [qs],
        sums_two,
        [gb_0, gb_1],
    )
    if place:
        late, input_grad = flow.turn(["c", "f0"], late, input_grad)
        late = lax.all_to_all(late, ("rep", "fsdp"), 0, 0, tiled=True)
        (late,) = flow.meet(["c", "f1"], late)
        flow.begin("fy", send_twin(place, flow.done["f1"]))
        (late,) = flow.send(late)
        (late,) = flow.meet(["c", "fy"], late)
        flow.begin("cy", send_twin(place, flow.done["c"]))
        (late,) = flow.send(late)
        (late,) = flow.meet(["cy"], late)
        shares = late.sum(axis=0)
        sums = [side for name in ("f0", "fy", "cy") for pair in zip(*flow.done[name]) for side in pair]
        g_qkv, g_proj, g_up, g_down = unpack_call(count, quarter, sums)
    else:
        shares = lax.psum(lax.psum_scatter(late, "fsdp", scatter_dimension=0, tiled=True), "rep")[0]
        sums_c = whole_scatter(sums_c[0])
        g_proj = sums_c[0]
        g_qkv = sums_c[1:].reshape(3, r, 3, GROUP).transpose(1, 2, 0, 3).reshape(r, 3 * width)
        g_ff = jnp.concatenate([f0, whole_scatter(f1[0])]).reshape(quarter, 2, r, width)
        g_up = g_ff[:, 0].reshape(quarter, r, count, r).transpose(1, 2, 0, 3).reshape(r, quarter * width)
        g_down = g_ff[:, 1].reshape(quarter * r, width)
    token_s, gain1_s, shift1_s, qb_s, vb_s, pb_s, gain2_s, shift2_s, db_s = [shares[i] for i in range(9)]
    ub_s = shares[9:kinds].reshape(-1)
    return (
        block_out,
        input_grad,
        token_s,
        gain1_s,
        shift1_s,
        g_qkv,
        qb_s,
        vb_s,
        g_proj,
        pb_s,
        gain2_s,
        shift2_s,
        g_up,
        ub_s,
        g_down,
        db_s,
    )


def solution(mesh):
    both, one = P(("rep", "fsdp"), None), P("fsdp")
    flat = P("fsdp", None)
    in_specs = (both, both, one, one, one, flat, one, one, flat, one, one, one, flat, one, flat, one, both)
    out_specs = (both, both, one, one, one, flat, one, one, flat, one, one, one, flat, one, flat, one)
    return jax.shard_map(
        functools.partial(local, mesh.shape["fsdp"]),
        mesh=mesh,
        in_specs=in_specs,
        out_specs=out_specs,
        check_vma=False,
    )
```

```python
import functools
import math

import jax
import jax.numpy as jnp
from jax import lax
from jax.experimental import pallas as pl
from jax.experimental.pallas import tpu as pltpu
from jax.sharding import PartitionSpec as P

F32 = jnp.float32
BF16 = jnp.bfloat16
HEAD = 64
GROUP = 256
NEG = -1e30
VMEM = 56 * 2**20


def dot(a, b):
    return lax.dot_general(a, b, (((1,), (0,)), ((), ())), preferred_element_type=F32)


def dot_rows(a, b):
    return lax.dot_general(a, b, (((0,), (0,)), ((), ())), preferred_element_type=F32)


def dot_cols(a, b):
    return lax.dot_general(a, b, (((1,), (1,)), ((), ())), preferred_element_type=F32)


FAR = 4


class Place:
    def __init__(self, count):
        self.count = count

    def own(self):
        index = lax.axis_index("fsdp")
        return index // 4, (index // 2) % 2, index % 2

    def swap(self, bits):
        return [(i, i ^ bits) for i in range(self.count)]

    def core(self, v):
        return lax.ppermute(v, "fsdp", self.swap(1))

    def along_x(self, v):
        return lax.ppermute(v, "fsdp", self.swap(2))

    def along_z(self, d):
        return lambda v: lax.ppermute(v, "fsdp", self.swap(4 * d))

    def along_y(self, v):
        return lax.ppermute(v, "rep", [(0, 1), (1, 0)])

    def along_xy(self, v):
        n = self.count
        return lax.ppermute(
            v, ("rep", "fsdp"), [(y * n + i, (1 - y) * n + (i ^ 2)) for y in range(2) for i in range(n)]
        )


def shard_at(own, dc, dx, dz):
    z, x, c = own
    return (lax.bitwise_xor(z, dz) * 2 + lax.bitwise_xor(x, dx)) * 2 + lax.bitwise_xor(c, dc)


def add_low(*terms):
    total = terms[0].astype(F32)
    for term in terms[1:]:
        total = total + term.astype(F32)
    return total


def low(v):
    return v.astype(BF16)


def by_side(side, first, second, axis):
    return jnp.where(side == 0, jnp.concatenate([first, second], axis), jnp.concatenate([second, first], axis))


class Weight:
    def __init__(self, kind, arrays):
        self.kind = kind
        self.arrays = arrays


def gather_fast(place, stack):
    came = yield [(place.along_z(d), stack) for d in range(1, FAR)]
    own = jnp.stack([stack] + came)
    beside, own_core = yield [(place.along_x, own), (place.core, own)]
    (beside_core,) = yield [(place.core, beside)]
    return Weight("rows", [own, beside, own_core, beside_core])


def half_columns(stack):
    half = stack.shape[2] // 2
    return lax.dynamic_slice_in_dim(stack, lax.axis_index("rep") * half, half, axis=2)


def gather_wide(place, stack):
    mine = half_columns(stack)
    came = yield [(place.along_z(d), mine) for d in range(1, FAR)]
    own = jnp.stack([mine] + came)
    came = yield [(place.along_x, own), (place.along_y, own), (place.along_xy, own)]
    here = jnp.stack([own] + came)
    (across,) = yield [(place.core, here)]
    return Weight("halves", [here, across])


def gather_even(place, stack):
    mine = half_columns(stack)
    came = yield [(place.along_z(d), mine) for d in range(1, FAR)]
    own = jnp.stack([mine] + came)
    beside, twin = yield [(place.along_x, own), (place.along_y, own)]
    corner = yield [(place.along_y, beside[:2]), (place.along_x, twin[2:])]
    here = jnp.stack([own, beside, twin, jnp.concatenate(corner)])
    (across,) = yield [(place.core, here)]
    return Weight("halves", [here, across])


def gather_late_y(place, stack):
    mine = half_columns(stack)
    came = yield [(place.along_z(d), mine) for d in range(1, FAR)]
    own = jnp.stack([mine] + came)
    (beside,) = yield [(place.along_x, own)]
    side = jnp.stack([own, beside])
    (twin,) = yield [(place.along_y, side)]
    here = jnp.concatenate([side, twin])
    (across,) = yield [(place.core, here)]
    return Weight("halves", [here, across])


def scatter_early_y(place, keep, send):
    (came,) = yield [(place.core, send)]
    (came_y,) = yield [(place.along_y, low(add_low(keep[1], came[1])))]
    (came_x,) = yield [(place.along_x, low(add_low(keep[0, 1], came[0, 1], came_y[1])))]
    total = low(add_low(keep[0, 0], came[0, 0], came_y[0], came_x))
    came = yield [(place.along_z(d), total[d]) for d in range(1, FAR)]
    return low(add_low(total[0], *came))


def scatter_wide(place, keep, send):
    (came,) = yield [(place.core, send)]

    def pair(dy, dx):
        return low(add_low(keep[dy, dx], came[dy, dx]))

    came_xy = yield [(place.along_x, pair(0, 1)), (place.along_y, pair(1, 0)), (place.along_xy, pair(1, 1))]
    total = low(add_low(keep[0, 0], came[0, 0], *came_xy))
    came = yield [(place.along_z(d), total[d]) for d in range(1, FAR)]
    return low(add_low(total[0], *came))


def send_twin(place, *mine):
    twins = yield [(place.along_y, v) for v in mine]
    return list(mine), twins


class Flow:
    def __init__(self):
        self.live = {}
        self.done = {}

    def begin(self, name, steps):
        self.live[name] = (steps, next(steps), None)

    def send(self, *arrays, but=()):
        waiting = [name for name, (_, _, sent) in self.live.items() if sent is None and name not in but]
        flat = [v for name in waiting for _, v in self.live[name][1]]
        flat = list(lax.optimization_barrier(tuple(flat) + tuple(arrays)))
        for name in waiting:
            steps, pairs, _ = self.live[name]
            sent = [move(v) for (move, _), v in zip(pairs, flat)]
            flat = flat[len(pairs) :]
            self.live[name] = (steps, pairs, sent)
        return flat

    def meet(self, names, *arrays):
        names = [name for name in names if name in self.live]
        flat = [v for name in names for v in self.live[name][2]]
        flat = list(lax.optimization_barrier(tuple(flat) + tuple(arrays)))
        for name in names:
            steps, pairs, _ = self.live[name]
            mine, flat = flat[: len(pairs)], flat[len(pairs) :]
            try:
                self.live[name] = (steps, steps.send(mine), None)
            except StopIteration as stop:
                del self.live[name]
                self.done[name] = stop.value
        return flat

    def turn(self, names, *arrays):
        return self.send(*self.meet(names, *arrays))


def half_at(dy, width):
    at = lax.bitwise_xor(lax.axis_index("rep"), dy) * width
    return pl.ds(pl.multiple_of(at, 128), width)


def load_weight(place, kind, rows, refs, spot, lead=0):
    own = place.own()
    for dc in range(2):
        for dx in range(2):
            for d in range(FAR):
                at = pl.ds(pl.multiple_of(shard_at(own, dc, dx, d) * rows, 16), rows)
                if kind == "rows":
                    spot[at, :] = refs[2 * dc + dx][d, lead, :rows]
                else:
                    for dy in range(2):
                        spot[at, half_at(dy, refs[0].shape[-1])] = refs[dc][2 * dy + dx, d, lead]


def store_grad(place, spot, keep, send, lead=0):
    own = place.own()
    rows, width = keep.shape[-2:]
    for dc, ref in enumerate((keep, send)):
        for dx in range(2):
            for d in range(FAR):
                at = pl.ds(pl.multiple_of(shard_at(own, dc, dx, d) * rows, 16), rows)
                if len(keep.shape) == 5:
                    ref[dx, d, lead] = spot[at, :]
                else:
                    for dy in range(2):
                        ref[dy, dx, d, lead] = spot[at, half_at(dy, width)]


def norm_stats(v):
    mean = jnp.mean(v, axis=-1, keepdims=True)
    centred = v - mean
    spread = jnp.mean(centred * centred, axis=-1, keepdims=True)
    scale = lax.rsqrt(spread + 1e-06)
    return centred * scale, scale


def norm_back(up, xhat, scale, gain):
    e = up * gain
    return (e - jnp.mean(e, axis=-1, keepdims=True) - xhat * jnp.mean(e * xhat, axis=-1, keepdims=True)) * scale


ERF_P = 0.3275911 / math.sqrt(2.0)
ERF_A = (0.254829592, -0.284496736, 1.421413741, -1.453152027, 1.061405429)


def gelu_and_slope(z):
    t = 1.0 / (1.0 + ERF_P * jnp.abs(z))
    e = jnp.exp(-0.5 * (z * z))
    poly = 0.5 * ERF_A[4]
    for a in ERF_A[3::-1]:
        poly = poly * t + 0.5 * a
    q = poly * t * e
    phi = jnp.where(z > 0, 1.0 - q, q)
    return z * phi, phi + z * (e * (1.0 / math.sqrt(2.0 * math.pi)))


class Rows:
    def __init__(self, images, patches):
        self.images = images
        self.patches = patches
        self.pad = -(-patches // 16) * 16
        self.all = images * self.pad
        self.raw = images * patches

    def block(self, width, count=1):
        return pl.BlockSpec((self.pad * count, width), lambda j: (j, 0))


def flag_column(rows, flags):
    wide = flags[...].astype(F32)
    wide = jnp.concatenate([wide, jnp.zeros((8 - rows.images, rows.patches), F32)], axis=0)
    gap = -rows.patches % 128
    return jnp.concatenate([wide, jnp.zeros((8, gap), F32)], axis=1).T


def padded_image(rows, ref, i):
    lo = rows.patches * i
    first = lo // 16 * 16
    last = min(-(-(lo + rows.patches) // 16) * 16, rows.raw)
    part = ref[first:last, :].astype(F32)[lo - first : lo - first + rows.patches]
    return jnp.concatenate([part, jnp.zeros((rows.pad - rows.patches, ref.shape[1]), F32)], axis=0)


def pad_kernel(rows, tokens, grads, base_o, grad_o):
    j = pl.program_id(0)

    def image(i):
        base_o[...] = padded_image(rows, tokens, i).astype(BF16)
        grad_o[...] = padded_image(rows, grads, i).astype(BF16)

    for i in range(rows.images):
        pl.when(j == i)(functools.partial(image, i))


def norm_one_kernel(rows, tokens, flags, vec, base_o, norm_o):
    cols = flag_column(rows, flags)
    row = lax.broadcasted_iota(jnp.int32, (rows.pad, 1), 0)
    for i in range(rows.images):
        at = pl.ds(i * rows.pad, rows.pad)
        masked = jnp.logical_and(cols[: rows.pad, i : i + 1] > 0.5, row < rows.patches)
        base = jnp.where(masked, vec[0:1, :], tokens[at, :].astype(F32))
        base_o[at, :] = base.astype(BF16)
        xhat, _ = norm_stats(base)
        norm_o[at, :] = (xhat * vec[1:2, :] + vec[2:3, :]).astype(BF16)


def whole(shape):
    return pl.BlockSpec(shape, lambda *j: (0,) * len(shape))


def params():
    return pltpu.CompilerParams(vmem_limit_bytes=VMEM)


SCALE = 0.01


def cost(micros):
    return pl.CostEstimate(flops=int(micros * SCALE * 1.15e9), bytes_accessed=int(micros * SCALE * 3e6), transcendentals=0)


def pad_call(rows, tokens, grads):
    width = tokens.shape[1]
    out = jax.ShapeDtypeStruct((rows.all, width), BF16)
    return pl.pallas_call(
        functools.partial(pad_kernel, rows),
        grid=(rows.images,),
        in_specs=[whole(tokens.shape), whole(grads.shape)],
        out_specs=[rows.block(width)] * 2,
        out_shape=[out, out],
        compiler_params=params(),
        cost_estimate=cost(5),
        name="pad_rows",
    )(tokens, grads)


def norm_one_call(rows, tokens, flags, vec):
    out = jax.ShapeDtypeStruct(tokens.shape, BF16)
    return pl.pallas_call(
        functools.partial(norm_one_kernel, rows),
        out_shape=[out, out],
        compiler_params=params(),
        cost_estimate=cost(5),
        name="norm_one",
    )(tokens, flags, vec)


def pack_kernel(count, quarter, *refs):
    *vectors, wide, qkv, proj, up, down = refs[: -2 - quarter // 2]
    first_o, second_o, *ff_o = refs[-2 - quarter // 2 :]
    r, width = proj.shape

    def group(g):
        return [qkv[:, i * width + g * GROUP : i * width + (g + 1) * GROUP] for i in range(3)]

    for i, part in enumerate(group(0)):
        first_o[0, :r, i * GROUP : (i + 1) * GROUP] = part
    small = [v[...].astype(F32) for v in vectors]
    small += [wide[:, r * i : r * (i + 1)].astype(F32) for i in range(quarter)]
    small = jnp.concatenate(small + [jnp.zeros((16 - len(small), r), F32)], axis=0)
    first_o[0, r:, :] = jnp.concatenate([small, jnp.zeros((16, width - r), F32)], axis=1).astype(BF16)
    for g in (1, 2):
        for i, part in enumerate(group(g)):
            second_o[g - 1, :, i * GROUP : (i + 1) * GROUP] = part
    second_o[2] = proj[...]
    for t in range(quarter):
        out = ff_o[t // 2]
        cols = [up[:, (k * quarter + t) * r : (k * quarter + t + 1) * r] for k in range(count)]
        out[t % 2 * 2] = jnp.concatenate(cols, axis=1)
        out[t % 2 * 2 + 1] = down[t * r : (t + 1) * r, :]


def pack_call(count, vectors, wide, qkv, proj, up, down):
    r, width = proj.shape
    quarter = up.shape[1] // width
    shapes = [(1, r + 16, width), (3, r, width)] + [(4, r, width)] * (quarter // 2)
    return pl.pallas_call(
        functools.partial(pack_kernel, count, quarter),
        out_shape=[jax.ShapeDtypeStruct(shape, BF16) for shape in shapes],
        compiler_params=params(),
        cost_estimate=cost(2.5),
        name="pack",
    )(*[v[None] for v in vectors], wide[None], qkv, proj, up, down)


def unpack_kernel(count, quarter, *refs):
    sums, (qkv_o, proj_o, up_o, down_o) = refs[:6], refs[6:]
    r = proj_o.shape[0]
    width = proj_o.shape[1]

    def added(k):
        return [sums[2 * k][b].astype(F32) + sums[2 * k + 1][b].astype(F32) for b in range(sums[2 * k].shape[0])]

    def joined(k):
        out = []
        for b in range(sums[2 * k].shape[0]):
            mine, twin = sums[2 * k][b].astype(F32), sums[2 * k + 1][b].astype(F32)
            here = jnp.concatenate([mine, twin], axis=1)
            there = jnp.concatenate([twin, mine], axis=1)
            out.append(jnp.where(lax.axis_index("rep") == 0, here, there))
        return out

    ff = added(0) + joined(1)
    heads = joined(2)
    proj_o[...] = heads[0]
    for g in range(3):
        for i in range(3):
            qkv_o[:, i * width + g * GROUP : i * width + (g + 1) * GROUP] = heads[1 + g][:, i * GROUP : (i + 1) * GROUP]
    ups = [ff[2 * t] for t in range(quarter)]
    up_o[...] = jnp.concatenate([ups[t][:, k * r : (k + 1) * r] for k in range(count) for t in range(quarter)], axis=1)
    for t in range(quarter):
        down_o[t * r : (t + 1) * r, :] = ff[2 * t + 1]


def unpack_call(count, quarter, sums):
    r, width = sums[0].shape[1:]
    shapes = [(r, 3 * width), (r, width), (r, quarter * width), (quarter * r, width)]
    return pl.pallas_call(
        functools.partial(unpack_kernel, count, quarter),
        out_shape=[jax.ShapeDtypeStruct(shape, F32) for shape in shapes],
        compiler_params=params(),
        cost_estimate=cost(3),
        name="unpack",
    )(*sums)


def halves(x, first):
    zero = jnp.zeros_like(x)
    return jnp.concatenate([jnp.where(first, x, zero), jnp.where(first, zero, x)], axis=0)


def attend_kernel(place, kind, nw, before, rows, base_group, norm, vec, *refs):
    w_in, (q_o, k_o, v_o, att_o, p_o, w_o) = refs[:nw], refs[nw + before :]
    j = pl.program_id(0)
    w = w_o.at[0]
    if kind == "whole":
        w[...] = w_in[0][0]
    else:
        load_weight(place, kind, norm.shape[1] // place.count, w_in, w)
    x = norm[...]
    lanes = pl.ds(pl.multiple_of((base_group + j) * GROUP, GROUP), GROUP)
    q_o[0] = ((dot(x, w[:, 0:GROUP]) + vec[3:4, lanes]).astype(BF16) * 0.125).astype(BF16)
    k_o[0] = dot(x, w[:, GROUP : 2 * GROUP]).astype(BF16)
    v_o[0] = (dot(x, w[:, 2 * GROUP :]) + vec[4:5, lanes]).astype(BF16)
    s = rows.pad
    first = lax.broadcasted_iota(jnp.int32, (s, 128), 1) < HEAD
    live = lax.broadcasted_iota(jnp.int32, (s, 2 * s), 0) < rows.patches

    def image(i):
        at = pl.ds(pl.multiple_of(i * s, 16), s)
        for p in range(2):
            cols = pl.ds(128 * p, 128)
            q, k, v = q_o[0, at, cols], k_o[0, at, cols], v_o[0, at, cols]
            score = jnp.where(live, dot_cols(k, halves(q, first)), NEG)
            peak = jnp.max(score, axis=0, keepdims=True)
            e = jnp.exp(score - peak)
            probs = (e * (1.0 / jnp.sum(e, axis=0, keepdims=True))).astype(BF16)
            p_o[0, p, i] = probs
            o = dot_rows(probs, v)
            att_o[0, at, cols] = jnp.where(first, o[:s], o[s:]).astype(BF16)

    def step(i, carry):
        for u in range(3):
            image(i * 3 + u)
        return carry

    lax.fori_loop(0, rows.images // 3, step, 0)


def piece_specs(weight, blocks=1, first=0):
    if weight.kind == "whole":
        return [pl.BlockSpec((blocks, *weight.arrays[0].shape[1:]), lambda j: (first + j, 0, 0))]
    if weight.kind == "rows":
        z, _, r, w = weight.arrays[0].shape
        return [pl.BlockSpec((z, blocks, r, w), lambda j: (0, first + j, 0, 0))] * 4
    k, z, _, r, w = weight.arrays[0].shape
    return [pl.BlockSpec((k, z, blocks, r, w), lambda j: (0, 0, first + j, 0, 0))] * 2


def attend_call(place, rows, group, groups, norm, vec, weight, before=()):
    s = rows.pad
    width = norm.shape[1]
    row = pl.BlockSpec((1, rows.all, GROUP), lambda j: (group + j, 0, 0))
    out = jax.ShapeDtypeStruct((3, rows.all, GROUP), BF16)
    outs = [out] * 4 + [jax.ShapeDtypeStruct((3, 2, rows.images, s, 2 * s), BF16)]
    specs = [row] * 4 + [pl.BlockSpec((1, 2, rows.images, s, 2 * s), lambda j: (group + j, 0, 0, 0, 0))]
    outs.append(jax.ShapeDtypeStruct((3, width, 3 * GROUP), BF16))
    specs.append(pl.BlockSpec((1, width, 3 * GROUP), lambda j: (group + j, 0, 0)))
    args = [norm, vec, *weight.arrays, *before]
    first = len(args) - len(before)
    return pl.pallas_call(
        functools.partial(attend_kernel, place, weight.kind, len(weight.arrays), len(before), rows, group),
        grid=(groups,),
        in_specs=[whole(norm.shape), whole(vec.shape)]
        + piece_specs(weight)
        + [pl.BlockSpec(memory_space=pl.ANY)] * len(before),
        out_specs=specs,
        out_shape=outs,
        input_output_aliases={first + i: i for i in range(len(before))},
        compiler_params=params(),
        cost_estimate=cost(2 + 6 * groups),
        name="attend",
    )(*args)


def project_kernel(place, kind, nw, spot, vec, base, att, *refs):
    w_in, (resid_o, norm_o, w_o) = refs[:nw], refs[nw:]

    @pl.when(pl.program_id(0) == 0)
    def _():
        if kind == "whole":
            w_o[0] = w_in[0][0]
        else:
            load_weight(place, kind, base.shape[1] // place.count, w_in, w_o.at[0])

    both = jnp.concatenate([att[g] for g in range(att.shape[0])], axis=1)
    total = dot(both, w_o[0]) + base[...].astype(F32) + vec[5:6, :]
    resid_o[...] = total
    xhat, _ = norm_stats(total)
    norm_o[...] = (xhat * vec[6:7, :] + vec[7:8, :]).astype(BF16)


def project_call(place, rows, vec, base, att, weight, spot):
    width = base.shape[1]
    outs = [
        jax.ShapeDtypeStruct((rows.all, width), F32),
        jax.ShapeDtypeStruct((rows.all, width), BF16),
        jax.ShapeDtypeStruct((1, width, width), BF16),
    ]
    some = rows.images // 3
    pieces = [
        pl.BlockSpec(block.block_shape, lambda j, at=block.index_map(0): at)
        for block in piece_specs(weight, 1, spot)
    ]
    return pl.pallas_call(
        functools.partial(project_kernel, place, weight.kind, len(weight.arrays), spot),
        grid=(3,),
        in_specs=[whole(vec.shape), rows.block(width, some)]
        + [pl.BlockSpec((3, rows.pad * some, GROUP), lambda j: (0, j, 0))]
        + pieces,
        out_specs=[rows.block(width, some)] * 2 + [whole(outs[2].shape)],
        out_shape=outs,
        compiler_params=params(),
        cost_estimate=cost(7),
        name="project",
    )(vec, base, att, *weight.arrays)


def feed_kernel(place, kind, form, nw, rows, block, carried, norm, grad, vec, *refs):
    w_in, rest = refs[:nw], refs[nw:]
    if carried:
        (acc_in, gn_in), rest = rest[:2], rest[carried:]
    acc_o, gn_o, bias_o = rest[:3]
    j = pl.program_id(0)
    n = 1 if form == "whole" else 2
    grads_o, act_s, gp_s, rest = rest[3 : 3 + n], rest[3 + n], rest[4 + n], rest[5 + n :]
    if kind == "whole":
        w_up, w_down = w_in[0].at[0], w_in[0].at[1]
    else:
        w_up, w_down, rest = *rest[:2], rest[2:]
        r = norm.shape[1] // place.count
        load_weight(place, kind, r, w_in, w_up, 0)
        load_weight(place, kind, r, w_in, w_down, 1)

    @pl.when(j == 0)
    def _():
        if carried:
            acc_o[...] = acc_in[...]
            gn_o[...] = gn_in[...]
        else:
            acc_o[...] = jnp.zeros_like(acc_o)
            gn_o[...] = jnp.zeros_like(gn_o)

    bias = vec[pl.ds(9 + block + j, 1), :]
    step = 3 * rows.pad
    for b in range(rows.images // 3):
        at = pl.ds(b * step, step)
        z = dot(norm[at, :], w_up[...]) + bias
        up = dot_cols(grad[at, :], w_down[...])
        act, slope = gelu_and_slope(z)
        act = act.astype(BF16)
        gp = (up * slope).astype(BF16)
        act_s[at, :] = act
        gp_s[at, :] = gp
        acc_o[at, :] += dot(act, w_down[...])
        gn_o[at, :] += dot_cols(gp, w_up[...])
    bias_o[0] = jnp.sum(gp_s[...].astype(F32), axis=0, keepdims=True)
    for i, (left, right) in enumerate(((norm, gp_s), (act_s, grad))):
        value = dot_rows(left[...], right[...]).astype(BF16)
        if form == "whole":
            grads_o[0][i] = value
        else:
            rest[0][...] = value
            store_grad(place, rest[0], *grads_o, i)


def grad_out(kind, blocks, width, r, per_step):
    if kind == "whole":
        return (
            [jax.ShapeDtypeStruct((blocks, width, width), BF16)],
            [pl.BlockSpec((per_step, width, width), lambda j: (j, 0, 0))],
        )
    if kind == "few":
        lead, w = (2, FAR), width
    else:
        lead, w = (2, 2, FAR), width // 2
    zero = (0,) * len(lead)
    return (
        [jax.ShapeDtypeStruct((*lead, blocks, r, w), BF16)] * 2,
        [pl.BlockSpec((*lead, per_step, r, w), lambda j: (*zero, j, 0, 0))] * 2,
    )


def feed_call(place, rows, block, blocks, spot, norm, grad, vec, weight, form, r, carried):
    width = norm.shape[1]
    acc = jax.ShapeDtypeStruct((rows.all, width), F32)
    outs, specs = grad_out(form, 2 * blocks, width, r, 2)
    scratch = [pltpu.VMEM((rows.all, width), BF16)] * 2
    scratch += [pltpu.VMEM((width, width), BF16)] * ((2 if weight.kind != "whole" else 0) + (form != "whole"))
    args = [norm, grad, vec, *weight.arrays, *carried]
    in_specs = [whole(norm.shape), whole(grad.shape), whole(vec.shape)] + piece_specs(weight, 2, spot)
    in_specs += [whole(acc.shape)] * len(carried)
    return pl.pallas_call(
        functools.partial(feed_kernel, place, weight.kind, form, len(weight.arrays), rows, block, len(carried)),
        grid=(blocks,),
        in_specs=in_specs,
        out_specs=[whole(acc.shape)] * 2 + [pl.BlockSpec((1, 1, width), lambda j: (j, 0, 0))] + specs,
        out_shape=[acc, acc, jax.ShapeDtypeStruct((blocks, 1, width), F32)] + outs,
        scratch_shapes=scratch,
        compiler_params=params(),
        cost_estimate=cost(15 * blocks),
        name="feed",
    )(*args)


PAIR = 2


def middle_kernel(rows, resid, acc, gn, grad, vec, w, out_o, low_o, da_o, sums_o):
    xhat, scale = norm_stats(resid[...])
    gain = vec[6:7, :]
    up = gn[...]
    g = grad[...].astype(F32)
    total = g + norm_back(up, xhat, scale, gain)
    lowered = total.astype(BF16)
    low_o[...] = lowered
    da_o[...] = dot_cols(lowered, w[0]).astype(BF16)
    sums = jnp.concatenate(
        [
            jnp.sum(total, axis=0, keepdims=True),
            jnp.sum(up * xhat, axis=0, keepdims=True),
            jnp.sum(up, axis=0, keepdims=True),
            jnp.sum(g, axis=0, keepdims=True),
        ],
        axis=0,
    )
    final = resid[...] + acc[...] + vec[8:9, :]
    j = pl.program_id(0)
    for i in range(rows.images // PAIR):

        @pl.when(j == i)
        def _():
            sums_o[...] = sums if i == 0 else sums_o[...] + sums
            for u in range(PAIR):
                lo = rows.patches * (PAIR * i + u)
                out_o[lo : lo + rows.patches, :] = final[rows.pad * u : rows.pad * u + rows.patches]


def middle_call(rows, resid, acc, gn, grad, vec, weight):
    width = resid.shape[1]
    block = rows.block(width, PAIR)
    outs = [
        jax.ShapeDtypeStruct((rows.raw, width), BF16),
        jax.ShapeDtypeStruct((rows.all, width), BF16),
        jax.ShapeDtypeStruct((rows.all, width), BF16),
        jax.ShapeDtypeStruct((4, width), F32),
    ]

    def kernel(resid, acc, gn, grad, vec, w, out_o, low_o, da_o, sums_o, out_s):
        middle_kernel(rows, resid, acc, gn, grad, vec, w, out_s, low_o, da_o, sums_o)

        @pl.when(pl.program_id(0) == rows.images // PAIR - 1)
        def _():
            out_o[...] = out_s[...].astype(BF16)

    return pl.pallas_call(
        kernel,
        grid=(rows.images // PAIR,),
        in_specs=[block] * 4 + [whole(vec.shape), whole(weight.shape)],
        out_specs=[whole(outs[0].shape), block, block, whole(outs[3].shape)],
        out_shape=outs,
        scratch_shapes=[pltpu.VMEM((rows.raw, width), F32)],
        compiler_params=params(),
        cost_estimate=cost(12),
        name="middle",
    )(resid, acc, gn, grad, vec, weight)


STEP = 2


def attend_back_kernel(place, kind, rows, projects, norm, da, *refs):
    g, j = pl.program_id(0), pl.program_id(1)
    q_i, k_i, v_i, p_i, refs = *refs[:4], refs[4:]
    if projects:
        (lowered, *atts), refs = refs[: 1 + projects], refs[1 + projects :]
    d_o, bias_o = refs[:2]
    if kind == "whole":
        (grads_o,) = refs[2:]
    else:
        keep, send, g_s = refs[2:]
    s = rows.pad
    some = rows.images // STEP
    first = lax.broadcasted_iota(jnp.int32, (s, 128), 1) < HEAD

    def emit(value, spot):
        if kind == "whole":
            grads_o[spot] = value.astype(BF16)
        else:
            g_s[...] = value.astype(BF16)
            store_grad(place, g_s, keep, send, spot)

    for i in range(some):
        at = pl.ds(i * s, s)
        to = pl.ds(pl.multiple_of((j * some + i) * s, 16), s)
        for p in range(2):
            cols = pl.ds(128 * p, 128)
            q, k, v = q_i[0, at, cols], k_i[0, at, cols], v_i[0, at, cols]
            q2, da2 = halves(q, first), halves(da[at, cols], first)
            low_probs = p_i[0, p, i]
            d_o[0, to, pl.ds(2 * GROUP + 128 * p, 128)] = dot(low_probs, da2).astype(BF16)
            up = dot_cols(v, da2)
            probs = low_probs.astype(F32)
            inner = jnp.sum(probs * up, axis=0, keepdims=True)
            ds = (probs * (up - inner)).astype(BF16)
            d_o[0, to, pl.ds(GROUP + 128 * p, 128)] = dot(ds, q2).astype(BF16)
            dq = dot_rows(ds, k)
            d_o[0, to, cols] = (jnp.where(first, dq[:s], dq[s:]) * 0.125).astype(BF16)

    @pl.when(j == STEP - 1)
    def _():
        if projects:

            @pl.when(g == 0)
            def _():
                both = jnp.concatenate([a[b] for a in atts for b in range(a.shape[0])], axis=1)
                emit(dot_rows(both, lowered[...]), 0)

        bias_o[0] = jnp.sum(d_o[0].astype(F32), axis=0, keepdims=True)
        emit(dot_rows(norm[...], d_o[0]), g + (1 if projects else 0))


def attend_back_call(place, rows, group, groups, norm, q, k, v, probs, da, r, shape="few", project=()):
    width = norm.shape[1]
    s = rows.pad
    some = rows.images // STEP
    row = pl.BlockSpec((1, s * some, GROUP), lambda g, j: (group + g, j, 0))
    in_specs = [whole(norm.shape), pl.BlockSpec((s * some, GROUP), lambda g, j: (j, group + g)), row, row, row]
    in_specs += [pl.BlockSpec((1, 2, some, s, 2 * s), lambda g, j: (group + g, 0, j, 0, 0))]
    in_specs += [whole(a.shape) for a in project]
    kind = shape
    outs, specs = grad_out(kind, groups + (1 if project else 0), width, r, 1)
    specs = [whole(out.shape) for out in outs]
    return pl.pallas_call(
        functools.partial(attend_back_kernel, place, kind, rows, max(len(project) - 1, 0)),
        grid=(groups, STEP),
        in_specs=in_specs,
        out_specs=[
            pl.BlockSpec((1, rows.all, width), lambda g, j: (g, 0, 0)),
            pl.BlockSpec((1, 1, width), lambda g, j: (g, 0, 0)),
        ]
        + specs,
        out_shape=[
            jax.ShapeDtypeStruct((groups, rows.all, width), BF16),
            jax.ShapeDtypeStruct((groups, 1, width), F32),
        ]
        + outs,
        scratch_shapes=[] if kind == "whole" else [pltpu.VMEM((width, width), BF16)],
        compiler_params=params(),
        cost_estimate=cost(11 * groups),
        name="attend_back",
    )(norm, da, q, k, v, probs, *project)


def last_kernel(rows, counts, quarter, count, base, low, flags, vec, w, *refs):
    n = len(counts)
    dqkv, biases, two, feeds, (out_o, late_o, sums_o) = refs[:n], refs[n : 2 * n], refs[2 * n], refs[2 * n + 1 : -3], refs[-3:]
    cols = flag_column(rows, flags)
    gain = vec[1:2, :]
    parts = [d[b] for d, count in zip(dqkv, counts) for b in range(count)]
    up = dot_cols(parts[0], w[0])
    for g in range(1, len(parts)):
        up = up + dot_cols(parts[g], w[g])
    xhat, scale = norm_stats(base[...].astype(F32))
    total = low[...].astype(F32) + norm_back(up, xhat, scale, gain)
    row = lax.broadcasted_iota(jnp.int32, (rows.pad, 1), 0)
    j = pl.program_id(0)
    for i in range(rows.images // PAIR):

        @pl.when(j == i)
        def _():
            flagged = [
                jnp.logical_and(cols[: rows.pad, PAIR * i + u : PAIR * i + u + 1] > 0.5, row < rows.patches)
                for u in range(PAIR)
            ]
            chosen = jnp.concatenate([jnp.where(f, 1.0, 0.0) for f in flagged], axis=0) > 0.5
            sums = jnp.concatenate(
                [
                    jnp.sum(jnp.where(chosen, total, 0.0), axis=0, keepdims=True),
                    jnp.sum(up * xhat, axis=0, keepdims=True),
                    jnp.sum(up, axis=0, keepdims=True),
                ],
                axis=0,
            )
            sums_o[...] = sums if i == 0 else sums_o[...] + sums
            kept = jnp.where(chosen, 0.0, total)
            for u in range(PAIR):
                lo = rows.patches * (PAIR * i + u)
                out_o[lo : lo + rows.patches, :] = kept[rows.pad * u : rows.pad * u + rows.patches]

    @pl.when(j == rows.images // PAIR - 1)
    def _():
        groups = [b[g] for b, group_count in zip(biases, counts) for g in range(group_count)]
        query = jnp.concatenate([g[:, :GROUP] for g in groups], axis=1)
        value = jnp.concatenate([g[:, 2 * GROUP :] for g in groups], axis=1)
        hidden = [f[b] for f in feeds for b in range(f.shape[0])]
        width = base.shape[1]
        every = jnp.concatenate(
            [sums_o[...], query, value, two[...], *hidden, jnp.zeros((9 - quarter - 2, width), F32)], axis=0
        )
        r = width // count
        for k in range(late_o.shape[0]):
            at = k % count
            late_o[k] = every[:, at * r : (at + 1) * r]


def last_call(rows, count, copies, base, low, flags, vec, w, dqkv, biases, two, feeds):
    width = base.shape[1]
    block = rows.block(width, PAIR)
    outs = [
        jax.ShapeDtypeStruct((rows.raw, width), F32),
        jax.ShapeDtypeStruct((copies * count, 16, width // count), F32),
    ]
    quarter = sum(f.shape[0] for f in feeds)
    small = [*biases, two, *feeds]
    return pl.pallas_call(
        functools.partial(last_kernel, rows, [d.shape[0] for d in dqkv], quarter, count),
        grid=(rows.images // PAIR,),
        in_specs=[block, block, whole(flags.shape), whole(vec.shape), whole(w.shape)]
        + [pl.BlockSpec((d.shape[0], PAIR * rows.pad, width), lambda j: (0, j, 0)) for d in dqkv]
        + [whole(v.shape) for v in small],
        out_specs=[whole(out.shape) for out in outs],
        out_shape=outs,
        scratch_shapes=[pltpu.VMEM((3, width), F32)],
        compiler_params=params(),
        cost_estimate=cost(1500),
        name="last",
    )(base, low, flags, vec, w, *dqkv, *small)


def local(
    count,
    tokens,
    mask_flags,
    mask_token,
    norm1_gain,
    norm1_bias,
    qkv_weight,
    query_bias,
    value_bias,
    proj_weight,
    proj_bias,
    norm2_gain,
    norm2_bias,
    fc1_weight,
    fc1_bias,
    fc2_weight,
    fc2_bias,
    out_grad,
):
    images, patches = mask_flags.shape
    rows = Rows(images, patches)
    r, width = proj_weight.shape
    place = Place(count) if r % 16 == 0 and count == 4 * FAR else None
    quarter = fc1_weight.shape[1] // width

    half = quarter // 2
    vectors = (mask_token, norm1_gain, norm1_bias, query_bias, value_bias, proj_bias, norm2_gain, norm2_bias, fc2_bias)
    kinds = len(vectors) + quarter

    def whole_gather(stack):
        return Weight("whole", [lax.all_gather(stack, "fsdp", axis=1, tiled=True)])

    def whole_scatter(sums):
        share = lax.psum_scatter(sums if place else sums.astype(F32), "fsdp", scatter_dimension=1, tiled=True)
        return share if place else lax.psum(share, "rep")

    flow = Flow()
    pad_in = (tokens, out_grad)
    if place:
        z, x, c = place.own()
        first, second, ff_0, ff_1 = pack_call(count, vectors, fc1_bias, qkv_weight, proj_weight, fc1_weight, fc2_weight)
        flow.begin("wa", gather_fast(place, first))
        pad_in = flow.send(*pad_in)
    else:
        qkv_blocks = qkv_weight.reshape(r, 3, 3, GROUP).transpose(2, 0, 1, 3).reshape(3, r, 3 * GROUP)
        up_blocks = fc1_weight.reshape(r, count, quarter, r).transpose(2, 0, 1, 3).reshape(quarter, r, width)
        down_blocks = fc2_weight.reshape(quarter, r, width)
        ff = jnp.stack([up_blocks, down_blocks], axis=1).reshape(2 * quarter, r, width)
        w_a, w_b = whole_gather(qkv_blocks[:1]), whole_gather(jnp.concatenate([qkv_blocks[1:], proj_weight[None]]))
        w_f0, w_f1 = whole_gather(ff[: 2 * half]), whole_gather(ff[2 * half :])
        small = jnp.concatenate([v[None] for v in vectors] + [fc1_bias.reshape(quarter, r)])
        came = lax.all_gather(small, "fsdp", axis=1, tiled=True)
        came = jnp.pad(came, ((0, 16 - kinds), (0, 0)))
    base, grad = pad_call(rows, *pad_in)
    if place:
        (base,) = flow.meet(["wa"], base)
        flow.begin("wb", gather_wide(place, second))
        flow.begin("wf0", gather_even(place, ff_0))
        (base,) = flow.send(base)
        (base,) = flow.turn(["wa"], base)
        (base,) = flow.meet(["wa"], base)
        w_a = flow.done["wa"]
        came = jnp.stack([part[:, 0, r:, :r] for part in w_a.arrays]).reshape(2, 2, FAR, -1, r)
        came = jnp.where(c == 0, came, came[::-1])
        came = jnp.where(x == 0, came, came[:, ::-1])
        came = jnp.where(z % 2 == 0, came, came.reshape(2, 2, 2, 2, -1, r)[:, :, :, ::-1].reshape(came.shape))
        came = jnp.where(z < 2, came, came.reshape(2, 2, 2, 2, -1, r)[:, :, ::-1].reshape(came.shape))
        came = came.transpose(3, 2, 1, 0, 4)
    vec = came.reshape(16, width).astype(F32)

    base, norm = norm_one_call(rows, base, mask_flags, vec)
    if place:
        norm, ff_1 = flow.meet(["wb"], norm, ff_1)
        w_f1 = whole_gather(ff_1)
        (norm,) = flow.send(norm)
    attends = attend_call(place, rows, 0, 1, norm, vec, w_a)
    if place:
        norm, *attends = flow.turn(["wb", "wf0"], norm, *attends)
        norm, *attends = flow.meet(["wb"], norm, *attends)
        w_b = flow.done["wb"]
    q, k, v, att, probs, wqkv = attend_call(place, rows, 1, 2, norm, vec, w_b, attends)
    if place:
        (att,) = flow.turn(["wf0"], att)
    resid, norm_two, w_proj = project_call(place, rows, vec, base, att, w_b, 2)
    if place:
        (norm_two,) = flow.turn(["wf0"], norm_two)
        (norm_two,) = flow.meet(["wf0"], norm_two)
        w_f0 = flow.done["wf0"]

    form = "wide" if place else "whole"
    acc, gn, gb_0, f0 = feed_call(place, rows, 0, half, 0, norm_two, grad, vec, w_f0, "whole", r, ())
    f0 = whole_scatter(f0)
    acc, gn, gb_1, *f1 = feed_call(place, rows, half, half, 0, norm_two, grad, vec, w_f1, form, r, (acc, gn))
    if place:
        flow.begin("f1", scatter_wide(place, *f1))
        acc, gn = flow.send(acc, gn)

    block_out, lowered, da, sums_two = middle_call(rows, resid, acc, gn, grad, vec, w_proj)
    if place:
        (da,) = flow.turn(["f1"], da)
    dqkv, qs, *sums_c = attend_back_call(
        place, rows, 0, 3, norm, q, k, v, probs, da, r, form, project=[lowered, att]
    )
    if place:
        flow.begin("c", scatter_wide(place, *sums_c))
        dqkv, f0 = flow.meet(["f1"], dqkv, f0)
        flow.begin("f0", send_twin(place, f0))
        (dqkv,) = flow.send(dqkv, but=("f1",))
    input_grad, late = last_call(
        rows,
        count,
        2 if place else 1,
        base,
        lowered,
        mask_flags,
        vec,
        wqkv,
        [dqkv],
        [qs],
        sums_two,
        [gb_0, gb_1],
    )
    if place:
        late, input_grad = flow.turn(["c", "f0"], late, input_grad)
        late = lax.all_to_all(late, ("rep", "fsdp"), 0, 0, tiled=True)
        (late,) = flow.meet(["c", "f1"], late)
        flow.begin("fy", send_twin(place, flow.done["f1"]))
        (late,) = flow.send(late)
        (late,) = flow.meet(["c", "fy"], late)
        flow.begin("cy", send_twin(place, flow.done["c"]))
        (late,) = flow.send(late)
        (late,) = flow.meet(["cy"], late)
        shares = late.sum(axis=0)
        sums = [side for name in ("f0", "fy", "cy") for pair in zip(*flow.done[name]) for side in pair]
        g_qkv, g_proj, g_up, g_down = unpack_call(count, quarter, sums)
    else:
        shares = lax.psum(lax.psum_scatter(late, "fsdp", scatter_dimension=0, tiled=True), "rep")[0]
        sums_c = whole_scatter(sums_c[0])
        g_proj = sums_c[0]
        g_qkv = sums_c[1:].reshape(3, r, 3, GROUP).transpose(1, 2, 0, 3).reshape(r, 3 * width)
        g_ff = jnp.concatenate([f0, whole_scatter(f1[0])]).reshape(quarter, 2, r, width)
        g_up = g_ff[:, 0].reshape(quarter, r, count, r).transpose(1, 2, 0, 3).reshape(r, quarter * width)
        g_down = g_ff[:, 1].reshape(quarter * r, width)
    token_s, gain1_s, shift1_s, qb_s, vb_s, pb_s, gain2_s, shift2_s, db_s = [shares[i] for i in range(9)]
    ub_s = shares[9:kinds].reshape(-1)
    return (
        block_out,
        input_grad,
        token_s,
        gain1_s,
        shift1_s,
        g_qkv,
        qb_s,
        vb_s,
        g_proj,
        pb_s,
        gain2_s,
        shift2_s,
        g_up,
        ub_s,
        g_down,
        db_s,
    )


def solution(mesh):
    both, one = P(("rep", "fsdp"), None), P("fsdp")
    flat = P("fsdp", None)
    in_specs = (both, both, one, one, one, flat, one, one, flat, one, one, one, flat, one, flat, one, both)
    out_specs = (both, both, one, one, one, flat, one, one, flat, one, one, one, flat, one, flat, one)
    return jax.shard_map(
        functools.partial(local, mesh.shape["fsdp"]),
        mesh=mesh,
        in_specs=in_specs,
        out_specs=out_specs,
        check_vma=False,
    )
```

```python
import functools
import math

import jax
import jax.numpy as jnp
from jax import lax
from jax.experimental import pallas as pl
from jax.experimental.pallas import tpu as pltpu
from jax.sharding import PartitionSpec as P

F32 = jnp.float32
BF16 = jnp.bfloat16
HEAD = 64
GROUP = 256
NEG = -1e30
VMEM = 56 * 2**20


def dot(a, b):
    return lax.dot_general(a, b, (((1,), (0,)), ((), ())), preferred_element_type=F32)


def dot_rows(a, b):
    return lax.dot_general(a, b, (((0,), (0,)), ((), ())), preferred_element_type=F32)


def dot_cols(a, b):
    return lax.dot_general(a, b, (((1,), (1,)), ((), ())), preferred_element_type=F32)


FAR = 4


class Place:
    def __init__(self, count):
        self.count = count

    def own(self):
        index = lax.axis_index("fsdp")
        return index // 4, (index // 2) % 2, index % 2

    def swap(self, bits):
        return [(i, i ^ bits) for i in range(self.count)]

    def core(self, v):
        return lax.ppermute(v, "fsdp", self.swap(1))

    def along_x(self, v):
        return lax.ppermute(v, "fsdp", self.swap(2))

    def along_z(self, d):
        return lambda v: lax.ppermute(v, "fsdp", self.swap(4 * d))

    def along_y(self, v):
        return lax.ppermute(v, "rep", [(0, 1), (1, 0)])

    def along_xy(self, v):
        n = self.count
        return lax.ppermute(
            v, ("rep", "fsdp"), [(y * n + i, (1 - y) * n + (i ^ 2)) for y in range(2) for i in range(n)]
        )


def shard_at(own, dc, dx, dz):
    z, x, c = own
    return (lax.bitwise_xor(z, dz) * 2 + lax.bitwise_xor(x, dx)) * 2 + lax.bitwise_xor(c, dc)


def add_low(*terms):
    total = terms[0].astype(F32)
    for term in terms[1:]:
        total = total + term.astype(F32)
    return total


def low(v):
    return v.astype(BF16)


def by_side(side, first, second, axis):
    return jnp.where(side == 0, jnp.concatenate([first, second], axis), jnp.concatenate([second, first], axis))


class Weight:
    def __init__(self, kind, arrays):
        self.kind = kind
        self.arrays = arrays


def gather_fast(place, stack):
    came = yield [(place.along_z(d), stack) for d in range(1, FAR)]
    own = jnp.stack([stack] + came)
    beside, own_core = yield [(place.along_x, own), (place.core, own)]
    (beside_core,) = yield [(place.core, beside)]
    return Weight("rows", [own, beside, own_core, beside_core])


def half_columns(stack):
    half = stack.shape[2] // 2
    return lax.dynamic_slice_in_dim(stack, lax.axis_index("rep") * half, half, axis=2)


def gather_wide(place, stack):
    mine = half_columns(stack)
    came = yield [(place.along_z(d), mine) for d in range(1, FAR)]
    own = jnp.stack([mine] + came)
    came = yield [(place.along_x, own), (place.along_y, own), (place.along_xy, own)]
    here = jnp.stack([own] + came)
    (across,) = yield [(place.core, here)]
    return Weight("halves", [here, across])


def gather_even(place, stack):
    mine = half_columns(stack)
    came = yield [(place.along_z(d), mine) for d in range(1, FAR)]
    own = jnp.stack([mine] + came)
    beside, twin = yield [(place.along_x, own), (place.along_y, own)]
    corner = yield [(place.along_y, beside[:2]), (place.along_x, twin[2:])]
    here = jnp.stack([own, beside, twin, jnp.concatenate(corner)])
    (across,) = yield [(place.core, here)]
    return Weight("halves", [here, across])


def gather_late_y(place, stack):
    mine = half_columns(stack)
    came = yield [(place.along_z(d), mine) for d in range(1, FAR)]
    own = jnp.stack([mine] + came)
    (beside,) = yield [(place.along_x, own)]
    side = jnp.stack([own, beside])
    (twin,) = yield [(place.along_y, side)]
    here = jnp.concatenate([side, twin])
    (across,) = yield [(place.core, here)]
    return Weight("halves", [here, across])


def scatter_early_y(place, keep, send):
    (came,) = yield [(place.core, send)]
    (came_y,) = yield [(place.along_y, low(add_low(keep[1], came[1])))]
    (came_x,) = yield [(place.along_x, low(add_low(keep[0, 1], came[0, 1], came_y[1])))]
    total = low(add_low(keep[0, 0], came[0, 0], came_y[0], came_x))
    came = yield [(place.along_z(d), total[d]) for d in range(1, FAR)]
    return low(add_low(total[0], *came))


def scatter_wide(place, keep, send):
    (came,) = yield [(place.core, send)]

    def pair(dy, dx):
        return low(add_low(keep[dy, dx], came[dy, dx]))

    came_xy = yield [(place.along_x, pair(0, 1)), (place.along_y, pair(1, 0)), (place.along_xy, pair(1, 1))]
    total = low(add_low(keep[0, 0], came[0, 0], *came_xy))
    came = yield [(place.along_z(d), total[d]) for d in range(1, FAR)]
    return low(add_low(total[0], *came))


def send_twin(place, *mine):
    twins = yield [(place.along_y, v) for v in mine]
    return list(mine), twins


class Flow:
    def __init__(self):
        self.live = {}
        self.done = {}

    def begin(self, name, steps):
        self.live[name] = (steps, next(steps), None)

    def send(self, *arrays, but=()):
        waiting = [name for name, (_, _, sent) in self.live.items() if sent is None and name not in but]
        flat = [v for name in waiting for _, v in self.live[name][1]]
        flat = list(lax.optimization_barrier(tuple(flat) + tuple(arrays)))
        for name in waiting:
            steps, pairs, _ = self.live[name]
            sent = [move(v) for (move, _), v in zip(pairs, flat)]
            flat = flat[len(pairs) :]
            self.live[name] = (steps, pairs, sent)
        return flat

    def meet(self, names, *arrays):
        names = [name for name in names if name in self.live]
        flat = [v for name in names for v in self.live[name][2]]
        flat = list(lax.optimization_barrier(tuple(flat) + tuple(arrays)))
        for name in names:
            steps, pairs, _ = self.live[name]
            mine, flat = flat[: len(pairs)], flat[len(pairs) :]
            try:
                self.live[name] = (steps, steps.send(mine), None)
            except StopIteration as stop:
                del self.live[name]
                self.done[name] = stop.value
        return flat

    def turn(self, names, *arrays):
        return self.send(*self.meet(names, *arrays))


def half_at(dy, width):
    at = lax.bitwise_xor(lax.axis_index("rep"), dy) * width
    return pl.ds(pl.multiple_of(at, 128), width)


def load_weight(place, kind, rows, refs, spot, lead=0):
    own = place.own()
    for dc in range(2):
        for dx in range(2):
            for d in range(FAR):
                at = pl.ds(pl.multiple_of(shard_at(own, dc, dx, d) * rows, 16), rows)
                if kind == "rows":
                    spot[at, :] = refs[2 * dc + dx][d, lead, :rows]
                else:
                    for dy in range(2):
                        spot[at, half_at(dy, refs[0].shape[-1])] = refs[dc][2 * dy + dx, d, lead]


def store_grad(place, spot, keep, send, lead=0):
    own = place.own()
    rows, width = keep.shape[-2:]
    for dc, ref in enumerate((keep, send)):
        for dx in range(2):
            for d in range(FAR):
                at = pl.ds(pl.multiple_of(shard_at(own, dc, dx, d) * rows, 16), rows)
                if len(keep.shape) == 5:
                    ref[dx, d, lead] = spot[at, :]
                else:
                    for dy in range(2):
                        ref[dy, dx, d, lead] = spot[at, half_at(dy, width)]


def norm_stats(v):
    mean = jnp.mean(v, axis=-1, keepdims=True)
    centred = v - mean
    spread = jnp.mean(centred * centred, axis=-1, keepdims=True)
    scale = lax.rsqrt(spread + 1e-06)
    return centred * scale, scale


def norm_back(up, xhat, scale, gain):
    e = up * gain
    return (e - jnp.mean(e, axis=-1, keepdims=True) - xhat * jnp.mean(e * xhat, axis=-1, keepdims=True)) * scale


ERF_P = 0.3275911 / math.sqrt(2.0)
ERF_A = (0.254829592, -0.284496736, 1.421413741, -1.453152027, 1.061405429)


def gelu_and_slope(z):
    t = 1.0 / (1.0 + ERF_P * jnp.abs(z))
    e = jnp.exp(-0.5 * (z * z))
    poly = 0.5 * ERF_A[4]
    for a in ERF_A[3::-1]:
        poly = poly * t + 0.5 * a
    q = poly * t * e
    phi = jnp.where(z > 0, 1.0 - q, q)
    return z * phi, phi + z * (e * (1.0 / math.sqrt(2.0 * math.pi)))


class Rows:
    def __init__(self, images, patches):
        self.images = images
        self.patches = patches
        self.pad = -(-patches // 16) * 16
        self.all = images * self.pad
        self.raw = images * patches

    def block(self, width, count=1):
        return pl.BlockSpec((self.pad * count, width), lambda j: (j, 0))


def flag_column(rows, flags):
    wide = flags[...].astype(F32)
    wide = jnp.concatenate([wide, jnp.zeros((8 - rows.images, rows.patches), F32)], axis=0)
    gap = -rows.patches % 128
    return jnp.concatenate([wide, jnp.zeros((8, gap), F32)], axis=1).T


def padded_image(rows, ref, i):
    lo = rows.patches * i
    first = lo // 16 * 16
    last = min(-(-(lo + rows.patches) // 16) * 16, rows.raw)
    part = ref[first:last, :].astype(F32)[lo - first : lo - first + rows.patches]
    return jnp.concatenate([part, jnp.zeros((rows.pad - rows.patches, ref.shape[1]), F32)], axis=0)


def pad_kernel(rows, tokens, grads, base_o, grad_o):
    j = pl.program_id(0)

    def image(i):
        base_o[...] = padded_image(rows, tokens, i).astype(BF16)
        grad_o[...] = padded_image(rows, grads, i).astype(BF16)

    for i in range(rows.images):
        pl.when(j == i)(functools.partial(image, i))


def norm_one_kernel(rows, tokens, flags, vec, base_o, norm_o):
    cols = flag_column(rows, flags)
    row = lax.broadcasted_iota(jnp.int32, (rows.pad, 1), 0)
    for i in range(rows.images):
        at = pl.ds(i * rows.pad, rows.pad)
        masked = jnp.logical_and(cols[: rows.pad, i : i + 1] > 0.5, row < rows.patches)
        base = jnp.where(masked, vec[0:1, :], tokens[at, :].astype(F32))
        base_o[at, :] = base.astype(BF16)
        xhat, _ = norm_stats(base)
        norm_o[at, :] = (xhat * vec[1:2, :] + vec[2:3, :]).astype(BF16)


def whole(shape):
    return pl.BlockSpec(shape, lambda *j: (0,) * len(shape))


def params():
    return pltpu.CompilerParams(vmem_limit_bytes=VMEM)


SCALE = 0.01


def cost(micros):
    return pl.CostEstimate(flops=int(micros * SCALE * 1.15e9), bytes_accessed=int(micros * SCALE * 3e6), transcendentals=0)


def pad_call(rows, tokens, grads):
    width = tokens.shape[1]
    out = jax.ShapeDtypeStruct((rows.all, width), BF16)
    return pl.pallas_call(
        functools.partial(pad_kernel, rows),
        grid=(rows.images,),
        in_specs=[whole(tokens.shape), whole(grads.shape)],
        out_specs=[rows.block(width)] * 2,
        out_shape=[out, out],
        compiler_params=params(),
        cost_estimate=cost(5),
        name="pad_rows",
    )(tokens, grads)


def norm_one_call(rows, tokens, flags, vec):
    out = jax.ShapeDtypeStruct(tokens.shape, BF16)
    return pl.pallas_call(
        functools.partial(norm_one_kernel, rows),
        out_shape=[out, out],
        compiler_params=params(),
        cost_estimate=cost(5),
        name="norm_one",
    )(tokens, flags, vec)


def pack_kernel(count, quarter, *refs):
    *vectors, wide, qkv, proj, up, down = refs[: -2 - quarter // 2]
    first_o, second_o, *ff_o = refs[-2 - quarter // 2 :]
    r, width = proj.shape

    def group(g):
        return [qkv[:, i * width + g * GROUP : i * width + (g + 1) * GROUP] for i in range(3)]

    for i, part in enumerate(group(0)):
        first_o[0, :r, i * GROUP : (i + 1) * GROUP] = part
    small = [v[...].astype(F32) for v in vectors]
    small += [wide[:, r * i : r * (i + 1)].astype(F32) for i in range(quarter)]
    small = jnp.concatenate(small + [jnp.zeros((16 - len(small), r), F32)], axis=0)
    first_o[0, r:, :] = jnp.concatenate([small, jnp.zeros((16, width - r), F32)], axis=1).astype(BF16)
    for g in (1, 2):
        for i, part in enumerate(group(g)):
            second_o[g - 1, :, i * GROUP : (i + 1) * GROUP] = part
    second_o[2] = proj[...]
    for t in range(quarter):
        out = ff_o[t // 2]
        cols = [up[:, (k * quarter + t) * r : (k * quarter + t + 1) * r] for k in range(count)]
        out[t % 2 * 2] = jnp.concatenate(cols, axis=1)
        out[t % 2 * 2 + 1] = down[t * r : (t + 1) * r, :]


def pack_call(count, vectors, wide, qkv, proj, up, down):
    r, width = proj.shape
    quarter = up.shape[1] // width
    shapes = [(1, r + 16, width), (3, r, width)] + [(4, r, width)] * (quarter // 2)
    return pl.pallas_call(
        functools.partial(pack_kernel, count, quarter),
        out_shape=[jax.ShapeDtypeStruct(shape, BF16) for shape in shapes],
        compiler_params=params(),
        cost_estimate=cost(2.5),
        name="pack",
    )(*[v[None] for v in vectors], wide[None], qkv, proj, up, down)


def unpack_kernel(count, quarter, *refs):
    sums, (qkv_o, proj_o, up_o, down_o) = refs[:6], refs[6:]
    r = proj_o.shape[0]
    width = proj_o.shape[1]

    def added(k):
        return [sums[2 * k][b].astype(F32) + sums[2 * k + 1][b].astype(F32) for b in range(sums[2 * k].shape[0])]

    def joined(k):
        out = []
        for b in range(sums[2 * k].shape[0]):
            mine, twin = sums[2 * k][b].astype(F32), sums[2 * k + 1][b].astype(F32)
            here = jnp.concatenate([mine, twin], axis=1)
            there = jnp.concatenate([twin, mine], axis=1)
            out.append(jnp.where(lax.axis_index("rep") == 0, here, there))
        return out

    ff = added(0) + joined(1)
    heads = joined(2)
    proj_o[...] = heads[0]
    for g in range(3):
        for i in range(3):
            qkv_o[:, i * width + g * GROUP : i * width + (g + 1) * GROUP] = heads[1 + g][:, i * GROUP : (i + 1) * GROUP]
    ups = [ff[2 * t] for t in range(quarter)]
    up_o[...] = jnp.concatenate([ups[t][:, k * r : (k + 1) * r] for k in range(count) for t in range(quarter)], axis=1)
    for t in range(quarter):
        down_o[t * r : (t + 1) * r, :] = ff[2 * t + 1]


def unpack_call(count, quarter, sums):
    r, width = sums[0].shape[1:]
    shapes = [(r, 3 * width), (r, width), (r, quarter * width), (quarter * r, width)]
    return pl.pallas_call(
        functools.partial(unpack_kernel, count, quarter),
        out_shape=[jax.ShapeDtypeStruct(shape, F32) for shape in shapes],
        compiler_params=params(),
        cost_estimate=cost(3),
        name="unpack",
    )(*sums)


def halves(x, first):
    zero = jnp.zeros_like(x)
    return jnp.concatenate([jnp.where(first, x, zero), jnp.where(first, zero, x)], axis=0)


def attend_kernel(place, kind, nw, before, rows, base_group, norm, vec, *refs):
    w_in, (q_o, k_o, v_o, att_o, p_o, w_o) = refs[:nw], refs[nw + before :]
    j = pl.program_id(0)
    w = w_o.at[0]
    if kind == "whole":
        w[...] = w_in[0][0]
    else:
        load_weight(place, kind, norm.shape[1] // place.count, w_in, w)
    x = norm[...]
    lanes = pl.ds(pl.multiple_of((base_group + j) * GROUP, GROUP), GROUP)
    q_o[0] = ((dot(x, w[:, 0:GROUP]) + vec[3:4, lanes]).astype(BF16) * 0.125).astype(BF16)
    k_o[0] = dot(x, w[:, GROUP : 2 * GROUP]).astype(BF16)
    v_o[0] = (dot(x, w[:, 2 * GROUP :]) + vec[4:5, lanes]).astype(BF16)
    s = rows.pad
    first = lax.broadcasted_iota(jnp.int32, (s, 128), 1) < HEAD
    live = lax.broadcasted_iota(jnp.int32, (s, 2 * s), 0) < rows.patches

    def image(i):
        at = pl.ds(pl.multiple_of(i * s, 16), s)
        for p in range(2):
            cols = pl.ds(128 * p, 128)
            q, k, v = q_o[0, at, cols], k_o[0, at, cols], v_o[0, at, cols]
            score = jnp.where(live, dot_cols(k, halves(q, first)), NEG)
            peak = jnp.max(score, axis=0, keepdims=True)
            e = jnp.exp(score - peak)
            probs = (e * (1.0 / jnp.sum(e, axis=0, keepdims=True))).astype(BF16)
            p_o[0, p, i] = probs
            o = dot_rows(probs, v)
            att_o[0, at, cols] = jnp.where(first, o[:s], o[s:]).astype(BF16)

    def step(i, carry):
        for u in range(3):
            image(i * 3 + u)
        return carry

    lax.fori_loop(0, rows.images // 3, step, 0)


def piece_specs(weight, blocks=1, first=0):
    if weight.kind == "whole":
        return [pl.BlockSpec((blocks, *weight.arrays[0].shape[1:]), lambda j: (first + j, 0, 0))]
    if weight.kind == "rows":
        z, _, r, w = weight.arrays[0].shape
        return [pl.BlockSpec((z, blocks, r, w), lambda j: (0, first + j, 0, 0))] * 4
    k, z, _, r, w = weight.arrays[0].shape
    return [pl.BlockSpec((k, z, blocks, r, w), lambda j: (0, 0, first + j, 0, 0))] * 2


def attend_call(place, rows, group, groups, norm, vec, weight, before=()):
    s = rows.pad
    width = norm.shape[1]
    row = pl.BlockSpec((1, rows.all, GROUP), lambda j: (group + j, 0, 0))
    out = jax.ShapeDtypeStruct((3, rows.all, GROUP), BF16)
    outs = [out] * 4 + [jax.ShapeDtypeStruct((3, 2, rows.images, s, 2 * s), BF16)]
    specs = [row] * 4 + [pl.BlockSpec((1, 2, rows.images, s, 2 * s), lambda j: (group + j, 0, 0, 0, 0))]
    outs.append(jax.ShapeDtypeStruct((3, width, 3 * GROUP), BF16))
    specs.append(pl.BlockSpec((1, width, 3 * GROUP), lambda j: (group + j, 0, 0)))
    args = [norm, vec, *weight.arrays, *before]
    first = len(args) - len(before)
    return pl.pallas_call(
        functools.partial(attend_kernel, place, weight.kind, len(weight.arrays), len(before), rows, group),
        grid=(groups,),
        in_specs=[whole(norm.shape), whole(vec.shape)]
        + piece_specs(weight)
        + [pl.BlockSpec(memory_space=pl.ANY)] * len(before),
        out_specs=specs,
        out_shape=outs,
        input_output_aliases={first + i: i for i in range(len(before))},
        compiler_params=params(),
        cost_estimate=cost(2 + 6 * groups),
        name="attend",
    )(*args)


def project_kernel(place, kind, nw, spot, vec, base, att, *refs):
    w_in, (resid_o, norm_o, w_o) = refs[:nw], refs[nw:]

    @pl.when(pl.program_id(0) == 0)
    def _():
        if kind == "whole":
            w_o[0] = w_in[0][0]
        else:
            load_weight(place, kind, base.shape[1] // place.count, w_in, w_o.at[0])

    both = jnp.concatenate([att[g] for g in range(att.shape[0])], axis=1)
    total = dot(both, w_o[0]) + base[...].astype(F32) + vec[5:6, :]
    resid_o[...] = total
    xhat, _ = norm_stats(total)
    norm_o[...] = (xhat * vec[6:7, :] + vec[7:8, :]).astype(BF16)


def project_call(place, rows, vec, base, att, weight, spot):
    width = base.shape[1]
    outs = [
        jax.ShapeDtypeStruct((rows.all, width), F32),
        jax.ShapeDtypeStruct((rows.all, width), BF16),
        jax.ShapeDtypeStruct((1, width, width), BF16),
    ]
    some = rows.images // 3
    pieces = [
        pl.BlockSpec(block.block_shape, lambda j, at=block.index_map(0): at)
        for block in piece_specs(weight, 1, spot)
    ]
    return pl.pallas_call(
        functools.partial(project_kernel, place, weight.kind, len(weight.arrays), spot),
        grid=(3,),
        in_specs=[whole(vec.shape), rows.block(width, some)]
        + [pl.BlockSpec((3, rows.pad * some, GROUP), lambda j: (0, j, 0))]
        + pieces,
        out_specs=[rows.block(width, some)] * 2 + [whole(outs[2].shape)],
        out_shape=outs,
        compiler_params=params(),
        cost_estimate=cost(7),
        name="project",
    )(vec, base, att, *weight.arrays)


def feed_kernel(place, kind, form, nw, rows, block, carried, norm, grad, vec, *refs):
    w_in, rest = refs[:nw], refs[nw:]
    if carried:
        (acc_in, gn_in), rest = rest[:2], rest[carried:]
    acc_o, gn_o, bias_o = rest[:3]
    j = pl.program_id(0)
    n = 1 if form == "whole" else 2
    grads_o, act_s, gp_s, rest = rest[3 : 3 + n], rest[3 + n], rest[4 + n], rest[5 + n :]
    if kind == "whole":
        w_up, w_down = w_in[0].at[0], w_in[0].at[1]
    else:
        w_up, w_down, rest = *rest[:2], rest[2:]
        r = norm.shape[1] // place.count
        load_weight(place, kind, r, w_in, w_up, 0)
        load_weight(place, kind, r, w_in, w_down, 1)

    @pl.when(j == 0)
    def _():
        if carried:
            acc_o[...] = acc_in[...]
            gn_o[...] = gn_in[...]
        else:
            acc_o[...] = jnp.zeros_like(acc_o)
            gn_o[...] = jnp.zeros_like(gn_o)

    bias = vec[pl.ds(9 + block + j, 1), :]
    step = 3 * rows.pad
    for b in range(rows.images // 3):
        at = pl.ds(b * step, step)
        z = dot(norm[at, :], w_up[...]) + bias
        up = dot_cols(grad[at, :], w_down[...])
        act, slope = gelu_and_slope(z)
        act = act.astype(BF16)
        gp = (up * slope).astype(BF16)
        act_s[at, :] = act
        gp_s[at, :] = gp
        acc_o[at, :] += dot(act, w_down[...])
        gn_o[at, :] += dot_cols(gp, w_up[...])
    bias_o[0] = jnp.sum(gp_s[...].astype(F32), axis=0, keepdims=True)
    for i, (left, right) in enumerate(((norm, gp_s), (act_s, grad))):
        value = dot_rows(left[...], right[...]).astype(BF16)
        if form == "whole":
            grads_o[0][i] = value
        else:
            rest[0][...] = value
            store_grad(place, rest[0], *grads_o, i)


def grad_out(kind, blocks, width, r, per_step):
    if kind == "whole":
        return (
            [jax.ShapeDtypeStruct((blocks, width, width), BF16)],
            [pl.BlockSpec((per_step, width, width), lambda j: (j, 0, 0))],
        )
    if kind == "few":
        lead, w = (2, FAR), width
    else:
        lead, w = (2, 2, FAR), width // 2
    zero = (0,) * len(lead)
    return (
        [jax.ShapeDtypeStruct((*lead, blocks, r, w), BF16)] * 2,
        [pl.BlockSpec((*lead, per_step, r, w), lambda j: (*zero, j, 0, 0))] * 2,
    )


def feed_call(place, rows, block, blocks, spot, norm, grad, vec, weight, form, r, carried):
    width = norm.shape[1]
    acc = jax.ShapeDtypeStruct((rows.all, width), F32)
    outs, specs = grad_out(form, 2 * blocks, width, r, 2)
    scratch = [pltpu.VMEM((rows.all, width), BF16)] * 2
    scratch += [pltpu.VMEM((width, width), BF16)] * ((2 if weight.kind != "whole" else 0) + (form != "whole"))
    args = [norm, grad, vec, *weight.arrays, *carried]
    in_specs = [whole(norm.shape), whole(grad.shape), whole(vec.shape)] + piece_specs(weight, 2, spot)
    in_specs += [whole(acc.shape)] * len(carried)
    return pl.pallas_call(
        functools.partial(feed_kernel, place, weight.kind, form, len(weight.arrays), rows, block, len(carried)),
        grid=(blocks,),
        in_specs=in_specs,
        out_specs=[whole(acc.shape)] * 2 + [pl.BlockSpec((1, 1, width), lambda j: (j, 0, 0))] + specs,
        out_shape=[acc, acc, jax.ShapeDtypeStruct((blocks, 1, width), F32)] + outs,
        scratch_shapes=scratch,
        compiler_params=params(),
        cost_estimate=cost(15 * blocks),
        name="feed",
    )(*args)


PAIR = 3


def middle_kernel(rows, resid, acc, gn, grad, vec, w, out_o, low_o, da_o, sums_o):
    xhat, scale = norm_stats(resid[...])
    gain = vec[6:7, :]
    up = gn[...]
    g = grad[...].astype(F32)
    total = g + norm_back(up, xhat, scale, gain)
    lowered = total.astype(BF16)
    low_o[...] = lowered
    da_o[...] = dot_cols(lowered, w[0]).astype(BF16)
    sums = jnp.concatenate(
        [
            jnp.sum(total, axis=0, keepdims=True),
            jnp.sum(up * xhat, axis=0, keepdims=True),
            jnp.sum(up, axis=0, keepdims=True),
            jnp.sum(g, axis=0, keepdims=True),
        ],
        axis=0,
    )
    final = resid[...] + acc[...] + vec[8:9, :]
    j = pl.program_id(0)
    for i in range(rows.images // PAIR):

        @pl.when(j == i)
        def _():
            sums_o[...] = sums if i == 0 else sums_o[...] + sums
            for u in range(PAIR):
                lo = rows.patches * (PAIR * i + u)
                out_o[lo : lo + rows.patches, :] = final[rows.pad * u : rows.pad * u + rows.patches]


def middle_call(rows, resid, acc, gn, grad, vec, weight):
    width = resid.shape[1]
    block = rows.block(width, PAIR)
    outs = [
        jax.ShapeDtypeStruct((rows.raw, width), BF16),
        jax.ShapeDtypeStruct((rows.all, width), BF16),
        jax.ShapeDtypeStruct((rows.all, width), BF16),
        jax.ShapeDtypeStruct((4, width), F32),
    ]

    def kernel(resid, acc, gn, grad, vec, w, out_o, low_o, da_o, sums_o, out_s):
        middle_kernel(rows, resid, acc, gn, grad, vec, w, out_s, low_o, da_o, sums_o)

        @pl.when(pl.program_id(0) == rows.images // PAIR - 1)
        def _():
            out_o[...] = out_s[...].astype(BF16)

    return pl.pallas_call(
        kernel,
        grid=(rows.images // PAIR,),
        in_specs=[block] * 4 + [whole(vec.shape), whole(weight.shape)],
        out_specs=[whole(outs[0].shape), block, block, whole(outs[3].shape)],
        out_shape=outs,
        scratch_shapes=[pltpu.VMEM((rows.raw, width), F32)],
        compiler_params=params(),
        cost_estimate=cost(12),
        name="middle",
    )(resid, acc, gn, grad, vec, weight)


STEP = 2


def attend_back_kernel(place, kind, rows, projects, norm, da, *refs):
    g, j = pl.program_id(0), pl.program_id(1)
    q_i, k_i, v_i, p_i, refs = *refs[:4], refs[4:]
    if projects:
        (lowered, *atts), refs = refs[: 1 + projects], refs[1 + projects :]
    d_o, bias_o = refs[:2]
    if kind == "whole":
        (grads_o,) = refs[2:]
    else:
        keep, send, g_s = refs[2:]
    s = rows.pad
    some = rows.images // STEP
    first = lax.broadcasted_iota(jnp.int32, (s, 128), 1) < HEAD

    def emit(value, spot):
        if kind == "whole":
            grads_o[spot] = value.astype(BF16)
        else:
            g_s[...] = value.astype(BF16)
            store_grad(place, g_s, keep, send, spot)

    for i in range(some):
        at = pl.ds(i * s, s)
        to = pl.ds(pl.multiple_of((j * some + i) * s, 16), s)
        for p in range(2):
            cols = pl.ds(128 * p, 128)
            q, k, v = q_i[0, at, cols], k_i[0, at, cols], v_i[0, at, cols]
            q2, da2 = halves(q, first), halves(da[at, cols], first)
            low_probs = p_i[0, p, i]
            d_o[0, to, pl.ds(2 * GROUP + 128 * p, 128)] = dot(low_probs, da2).astype(BF16)
            up = dot_cols(v, da2)
            probs = low_probs.astype(F32)
            inner = jnp.sum(probs * up, axis=0, keepdims=True)
            ds = (probs * (up - inner)).astype(BF16)
            d_o[0, to, pl.ds(GROUP + 128 * p, 128)] = dot(ds, q2).astype(BF16)
            dq = dot_rows(ds, k)
            d_o[0, to, cols] = (jnp.where(first, dq[:s], dq[s:]) * 0.125).astype(BF16)

    @pl.when(j == STEP - 1)
    def _():
        if projects:

            @pl.when(g == 0)
            def _():
                both = jnp.concatenate([a[b] for a in atts for b in range(a.shape[0])], axis=1)
                emit(dot_rows(both, lowered[...]), 0)

        bias_o[0] = jnp.sum(d_o[0].astype(F32), axis=0, keepdims=True)
        emit(dot_rows(norm[...], d_o[0]), g + (1 if projects else 0))


def attend_back_call(place, rows, group, groups, norm, q, k, v, probs, da, r, shape="few", project=()):
    width = norm.shape[1]
    s = rows.pad
    some = rows.images // STEP
    row = pl.BlockSpec((1, s * some, GROUP), lambda g, j: (group + g, j, 0))
    in_specs = [whole(norm.shape), pl.BlockSpec((s * some, GROUP), lambda g, j: (j, group + g)), row, row, row]
    in_specs += [pl.BlockSpec((1, 2, some, s, 2 * s), lambda g, j: (group + g, 0, j, 0, 0))]
    in_specs += [whole(a.shape) for a in project]
    kind = shape
    outs, specs = grad_out(kind, groups + (1 if project else 0), width, r, 1)
    specs = [whole(out.shape) for out in outs]
    return pl.pallas_call(
        functools.partial(attend_back_kernel, place, kind, rows, max(len(project) - 1, 0)),
        grid=(groups, STEP),
        in_specs=in_specs,
        out_specs=[
            pl.BlockSpec((1, rows.all, width), lambda g, j: (g, 0, 0)),
            pl.BlockSpec((1, 1, width), lambda g, j: (g, 0, 0)),
        ]
        + specs,
        out_shape=[
            jax.ShapeDtypeStruct((groups, rows.all, width), BF16),
            jax.ShapeDtypeStruct((groups, 1, width), F32),
        ]
        + outs,
        scratch_shapes=[] if kind == "whole" else [pltpu.VMEM((width, width), BF16)],
        compiler_params=params(),
        cost_estimate=cost(11 * groups),
        name="attend_back",
    )(norm, da, q, k, v, probs, *project)


def last_kernel(rows, counts, quarter, count, base, low, flags, vec, w, *refs):
    n = len(counts)
    dqkv, biases, two, feeds, (out_o, late_o, sums_o) = refs[:n], refs[n : 2 * n], refs[2 * n], refs[2 * n + 1 : -3], refs[-3:]
    cols = flag_column(rows, flags)
    gain = vec[1:2, :]
    parts = [d[b] for d, count in zip(dqkv, counts) for b in range(count)]
    up = dot_cols(parts[0], w[0])
    for g in range(1, len(parts)):
        up = up + dot_cols(parts[g], w[g])
    xhat, scale = norm_stats(base[...].astype(F32))
    total = low[...].astype(F32) + norm_back(up, xhat, scale, gain)
    row = lax.broadcasted_iota(jnp.int32, (rows.pad, 1), 0)
    j = pl.program_id(0)
    for i in range(rows.images // PAIR):

        @pl.when(j == i)
        def _():
            flagged = [
                jnp.logical_and(cols[: rows.pad, PAIR * i + u : PAIR * i + u + 1] > 0.5, row < rows.patches)
                for u in range(PAIR)
            ]
            chosen = jnp.concatenate([jnp.where(f, 1.0, 0.0) for f in flagged], axis=0) > 0.5
            sums = jnp.concatenate(
                [
                    jnp.sum(jnp.where(chosen, total, 0.0), axis=0, keepdims=True),
                    jnp.sum(up * xhat, axis=0, keepdims=True),
                    jnp.sum(up, axis=0, keepdims=True),
                ],
                axis=0,
            )
            sums_o[...] = sums if i == 0 else sums_o[...] + sums
            kept = jnp.where(chosen, 0.0, total)
            for u in range(PAIR):
                lo = rows.patches * (PAIR * i + u)
                out_o[lo : lo + rows.patches, :] = kept[rows.pad * u : rows.pad * u + rows.patches]

    @pl.when(j == rows.images // PAIR - 1)
    def _():
        groups = [b[g] for b, group_count in zip(biases, counts) for g in range(group_count)]
        query = jnp.concatenate([g[:, :GROUP] for g in groups], axis=1)
        value = jnp.concatenate([g[:, 2 * GROUP :] for g in groups], axis=1)
        hidden = [f[b] for f in feeds for b in range(f.shape[0])]
        width = base.shape[1]
        every = jnp.concatenate(
            [sums_o[...], query, value, two[...], *hidden, jnp.zeros((9 - quarter - 2, width), F32)], axis=0
        )
        r = width // count
        for k in range(late_o.shape[0]):
            at = k % count
            late_o[k] = every[:, at * r : (at + 1) * r]


def last_call(rows, count, copies, base, low, flags, vec, w, dqkv, biases, two, feeds):
    width = base.shape[1]
    block = rows.block(width, PAIR)
    outs = [
        jax.ShapeDtypeStruct((rows.raw, width), F32),
        jax.ShapeDtypeStruct((copies * count, 16, width // count), F32),
    ]
    quarter = sum(f.shape[0] for f in feeds)
    small = [*biases, two, *feeds]
    return pl.pallas_call(
        functools.partial(last_kernel, rows, [d.shape[0] for d in dqkv], quarter, count),
        grid=(rows.images // PAIR,),
        in_specs=[block, block, whole(flags.shape), whole(vec.shape), whole(w.shape)]
        + [pl.BlockSpec((d.shape[0], PAIR * rows.pad, width), lambda j: (0, j, 0)) for d in dqkv]
        + [whole(v.shape) for v in small],
        out_specs=[whole(out.shape) for out in outs],
        out_shape=outs,
        scratch_shapes=[pltpu.VMEM((3, width), F32)],
        compiler_params=params(),
        cost_estimate=cost(1500),
        name="last",
    )(base, low, flags, vec, w, *dqkv, *small)


def local(
    count,
    tokens,
    mask_flags,
    mask_token,
    norm1_gain,
    norm1_bias,
    qkv_weight,
    query_bias,
    value_bias,
    proj_weight,
    proj_bias,
    norm2_gain,
    norm2_bias,
    fc1_weight,
    fc1_bias,
    fc2_weight,
    fc2_bias,
    out_grad,
):
    images, patches = mask_flags.shape
    rows = Rows(images, patches)
    r, width = proj_weight.shape
    place = Place(count) if r % 16 == 0 and count == 4 * FAR else None
    quarter = fc1_weight.shape[1] // width

    half = quarter // 2
    vectors = (mask_token, norm1_gain, norm1_bias, query_bias, value_bias, proj_bias, norm2_gain, norm2_bias, fc2_bias)
    kinds = len(vectors) + quarter

    def whole_gather(stack):
        return Weight("whole", [lax.all_gather(stack, "fsdp", axis=1, tiled=True)])

    def whole_scatter(sums):
        share = lax.psum_scatter(sums if place else sums.astype(F32), "fsdp", scatter_dimension=1, tiled=True)
        return share if place else lax.psum(share, "rep")

    flow = Flow()
    pad_in = (tokens, out_grad)
    if place:
        z, x, c = place.own()
        first, second, ff_0, ff_1 = pack_call(count, vectors, fc1_bias, qkv_weight, proj_weight, fc1_weight, fc2_weight)
        flow.begin("wa", gather_fast(place, first))
        pad_in = flow.send(*pad_in)
    else:
        qkv_blocks = qkv_weight.reshape(r, 3, 3, GROUP).transpose(2, 0, 1, 3).reshape(3, r, 3 * GROUP)
        up_blocks = fc1_weight.reshape(r, count, quarter, r).transpose(2, 0, 1, 3).reshape(quarter, r, width)
        down_blocks = fc2_weight.reshape(quarter, r, width)
        ff = jnp.stack([up_blocks, down_blocks], axis=1).reshape(2 * quarter, r, width)
        w_a, w_b = whole_gather(qkv_blocks[:1]), whole_gather(jnp.concatenate([qkv_blocks[1:], proj_weight[None]]))
        w_f0, w_f1 = whole_gather(ff[: 2 * half]), whole_gather(ff[2 * half :])
        small = jnp.concatenate([v[None] for v in vectors] + [fc1_bias.reshape(quarter, r)])
        came = lax.all_gather(small, "fsdp", axis=1, tiled=True)
        came = jnp.pad(came, ((0, 16 - kinds), (0, 0)))
    base, grad = pad_call(rows, *pad_in)
    if place:
        (base,) = flow.meet(["wa"], base)
        flow.begin("wb", gather_wide(place, second))
        flow.begin("wf0", gather_even(place, ff_0))
        (base,) = flow.send(base)
        (base,) = flow.turn(["wa"], base)
        (base,) = flow.meet(["wa"], base)
        w_a = flow.done["wa"]
        came = jnp.stack([part[:, 0, r:, :r] for part in w_a.arrays]).reshape(2, 2, FAR, -1, r)
        came = jnp.where(c == 0, came, came[::-1])
        came = jnp.where(x == 0, came, came[:, ::-1])
        came = jnp.where(z % 2 == 0, came, came.reshape(2, 2, 2, 2, -1, r)[:, :, :, ::-1].reshape(came.shape))
        came = jnp.where(z < 2, came, came.reshape(2, 2, 2, 2, -1, r)[:, :, ::-1].reshape(came.shape))
        came = came.transpose(3, 2, 1, 0, 4)
    vec = came.reshape(16, width).astype(F32)

    base, norm = norm_one_call(rows, base, mask_flags, vec)
    if place:
        norm, ff_1 = flow.meet(["wb"], norm, ff_1)
        w_f1 = whole_gather(ff_1)
        (norm,) = flow.send(norm)
    attends = attend_call(place, rows, 0, 1, norm, vec, w_a)
    if place:
        norm, *attends = flow.turn(["wb", "wf0"], norm, *attends)
        norm, *attends = flow.meet(["wb"], norm, *attends)
        w_b = flow.done["wb"]
    q, k, v, att, probs, wqkv = attend_call(place, rows, 1, 2, norm, vec, w_b, attends)
    if place:
        (att,) = flow.turn(["wf0"], att)
    resid, norm_two, w_proj = project_call(place, rows, vec, base, att, w_b, 2)
    if place:
        (norm_two,) = flow.turn(["wf0"], norm_two)
        (norm_two,) = flow.meet(["wf0"], norm_two)
        w_f0 = flow.done["wf0"]

    form = "wide" if place else "whole"
    acc, gn, gb_0, f0 = feed_call(place, rows, 0, half, 0, norm_two, grad, vec, w_f0, "whole", r, ())
    f0 = whole_scatter(f0)
    acc, gn, gb_1, *f1 = feed_call(place, rows, half, half, 0, norm_two, grad, vec, w_f1, form, r, (acc, gn))
    if place:
        flow.begin("f1", scatter_wide(place, *f1))
        acc, gn = flow.send(acc, gn)

    block_out, lowered, da, sums_two = middle_call(rows, resid, acc, gn, grad, vec, w_proj)
    if place:
        (da,) = flow.turn(["f1"], da)
    dqkv, qs, *sums_c = attend_back_call(
        place, rows, 0, 3, norm, q, k, v, probs, da, r, form, project=[lowered, att]
    )
    if place:
        flow.begin("c", scatter_wide(place, *sums_c))
        dqkv, f0 = flow.meet(["f1"], dqkv, f0)
        flow.begin("f0", send_twin(place, f0))
        (dqkv,) = flow.send(dqkv, but=("f1",))
    input_grad, late = last_call(
        rows,
        count,
        2 if place else 1,
        base,
        lowered,
        mask_flags,
        vec,
        wqkv,
        [dqkv],
        [qs],
        sums_two,
        [gb_0, gb_1],
    )
    if place:
        late, input_grad = flow.turn(["c", "f0"], late, input_grad)
        late = lax.all_to_all(late, ("rep", "fsdp"), 0, 0, tiled=True)
        (late,) = flow.meet(["c", "f1"], late)
        flow.begin("fy", send_twin(place, flow.done["f1"]))
        (late,) = flow.send(late)
        (late,) = flow.meet(["c", "fy"], late)
        flow.begin("cy", send_twin(place, flow.done["c"]))
        (late,) = flow.send(late)
        (late,) = flow.meet(["cy"], late)
        shares = late.sum(axis=0)
        sums = [side for name in ("f0", "fy", "cy") for pair in zip(*flow.done[name]) for side in pair]
        g_qkv, g_proj, g_up, g_down = unpack_call(count, quarter, sums)
    else:
        shares = lax.psum(lax.psum_scatter(late, "fsdp", scatter_dimension=0, tiled=True), "rep")[0]
        sums_c = whole_scatter(sums_c[0])
        g_proj = sums_c[0]
        g_qkv = sums_c[1:].reshape(3, r, 3, GROUP).transpose(1, 2, 0, 3).reshape(r, 3 * width)
        g_ff = jnp.concatenate([f0, whole_scatter(f1[0])]).reshape(quarter, 2, r, width)
        g_up = g_ff[:, 0].reshape(quarter, r, count, r).transpose(1, 2, 0, 3).reshape(r, quarter * width)
        g_down = g_ff[:, 1].reshape(quarter * r, width)
    token_s, gain1_s, shift1_s, qb_s, vb_s, pb_s, gain2_s, shift2_s, db_s = [shares[i] for i in range(9)]
    ub_s = shares[9:kinds].reshape(-1)
    return (
        block_out,
        input_grad,
        token_s,
        gain1_s,
        shift1_s,
        g_qkv,
        qb_s,
        vb_s,
        g_proj,
        pb_s,
        gain2_s,
        shift2_s,
        g_up,
        ub_s,
        g_down,
        db_s,
    )


def solution(mesh):
    both, one = P(("rep", "fsdp"), None), P("fsdp")
    flat = P("fsdp", None)
    in_specs = (both, both, one, one, one, flat, one, one, flat, one, one, one, flat, one, flat, one, both)
    out_specs = (both, both, one, one, one, flat, one, one, flat, one, one, one, flat, one, flat, one)
    return jax.shard_map(
        functools.partial(local, mesh.shape["fsdp"]),
        mesh=mesh,
        in_specs=in_specs,
        out_specs=out_specs,
        check_vma=False,
    )
```
